32 devices in a mesh: member: 2 (over y), frow: 4 (over x, core), fcol: 4 (over z).
Axes of the slice: x: 2, y: 2, z: 4, core: 2. Of those that a mesh axis runs over, the one named last changes fastest.
Arguments:
- latlon_cot: float32 [3, 16, 65536], P(None, None, ('member', 'frow', 'fcol')), parts along dimension 2, may hold values from -6 to 6
- dest_tile: int32 [32768, 1], P(('frow', 'fcol')), may hold values from 0 to 15; in each aligned block of 2048 rows (0 to 2047, 2048 to 4095, ...) at most 256 rows name the same one
- base_cell: int32 [32768], P(('frow', 'fcol')), may hold values from 0 to 888
- corner_frac: float32 [2, 32768], P(None, ('frow', 'fcol')), may hold values from 0 to 1
- saved_states: float32 [2, 2, 3, 16, 64, 512], P(None, None, None, None, ('member', 'frow'), 'fcol'), parts along dimension 4, may hold values from -1.2 to 1.7, as said below
- gravity: float32 [16], replicated, may hold values from 0.5 to 4
Outputs:
- sensitivity: float32 [3, 16, 64, 512], P(None, None, ('member', 'frow'), 'fcol'), parts along dimension 2
The draws below stay inside these ranges and needn't reach their ends.
There are 2 independent parts, one for each index of `member`. The reference program is written for one: setup_inputs(seed, part) draws one part's arguments, and reference() takes and returns one part's arrays. A program takes and returns all parts, laid end to end along the dimension named above; an argument that names none is the same for every part. Nothing has to cross between parts.
Inputs may be any that keep to these rules, and one draw needn't show every extreme that they name: `dest_tile`: the tile index is frow index times 4 plus fcol index; of the points of one tile's block at most 256 name one tile, and in every draw some tile is named that often. `base_cell`: the cell r * 127 + c for tile row r and tile column c; the other three corners are one row and one column further, inside the same tile. saved_states[n, k] is the state entering section k of step n; the height field lies in 0.3 to 1.7 and the winds in -1.2 to 1.2.
All inputs are finite; a program needn't handle non-finite values.
Results may differ from the reference program's by a relative error of at most 0.0003.
Values sent between devices are 32-bit elements; how exact they have to be, the bound alone decides.
No kernel may reach another device: no remote copies, remote signals or barrier semaphores. Data moves between devices by JAX's collectives and lax.ppermute only.
A program may use at most 64 MiB of HBM per device.

```python
import math
import jax
import jax.numpy as jnp
import numpy as np
from jax import lax

LEVELS = 16
ROWS_DEV = 8
COLS_DEV = 128
LL_DEV = 2048
TILES = 16
CAP = 256
NR = 32
NC = 512
LL_TOT = 32768
N_FCOL = 4


def draw_saved_states(key, part):
    key = jax.random.fold_in(key, 7)
    key_height, key_winds = jax.random.split(key)
    shape_height = (2, 2, 1, LEVELS, NR, NC)
    shape_winds = (2, 2, 2, LEVELS, NR, NC)
    height = jax.random.uniform(key_height, shape_height, jnp.float32, 0.5, 1.5)
    winds = 0.4 * jax.random.truncated_normal(key_winds, -3.0, 3.0, shape_winds, jnp.float32)
    return jnp.concatenate([height, winds], axis=2)


def plant(result, rng, smallest, largest):
    extent = result.shape
    index_at = [jax.random.randint(jax.random.fold_in(rng, axis), (), 0, extent[axis]) for axis in range(len(extent))]
    result = result.at[tuple(index_at)].set(smallest)
    longest = extent.index(max(extent))
    index_at[longest] = (index_at[longest] + 1) % extent[longest]
    return result.at[tuple(index_at)].set(largest)


def level_of(own_key, extent, cuts, smallest, high):
    def one(dim, blocks):
        draws = jax.random.uniform(jax.random.fold_in(jax.random.fold_in(own_key, 6), dim), (blocks,), jnp.float32, smallest / len(cuts), high / len(cuts))
        return jnp.repeat(jnp.exp(draws), extent[dim] // blocks).reshape((-1,) + (1,) * (len(extent) - dim - 1))

    gain = one(*cuts[0])
    for cut in cuts[1:]:
        gain = gain * one(*cut)
    return gain


def deal_out(own_key, own, number, rows, count, top, most, slope):
    sequence = jax.random.permutation(own_key, count)
    packed, common = load_shares(count, rows * top, most, slope, True), load_shares(count, rows * top, most, slope, False)
    places = jnp.arange(count)

    def named(sizes, offset_by):
        used = int((sizes > 0).sum())
        fixed = max(1, used // 4)
        shifted = fixed + (places - fixed + offset_by * (used - fixed)) % max(1, count - fixed)
        return jnp.zeros((count,), jnp.int32).at[sequence[jnp.where(places < fixed, places, shifted)]].set(jnp.asarray(sizes, jnp.int32))

    sizes = jnp.where(number % 4 == 0, named(packed, number // 4), named(common, number - number // 4 - 1))
    mixed = jax.random.permutation(jax.random.fold_in(own, 3), count)
    giver, receiver = mixed[0:count // 2 * 2:2], mixed[1:count // 2 * 2:2]
    room = jnp.minimum(sizes[giver] - 1, most - sizes[receiver]) // 2
    room = jnp.where((giver == sequence[0]) | (receiver == sequence[0]) | (sizes[receiver] == 0), 0, jnp.maximum(room, 0))
    shifted = jax.random.randint(jax.random.fold_in(own, 4), (count // 2,), 0, 1 << 20) % (room + 1)
    sizes = sizes.at[giver].add(-shifted).at[receiver].add(shifted)
    items = jnp.searchsorted(jnp.cumsum(sizes), jnp.arange(rows * top), side="right").astype(jnp.int32)
    grid = items.reshape(top, rows).T
    grid = grid[jax.random.permutation(jax.random.fold_in(own, 1), rows)]
    offset_by = jax.random.randint(jax.random.fold_in(own, 2), (rows, 1), 0, top)
    return jnp.take_along_axis(grid, (jnp.arange(top)[None, :] + offset_by) % top, axis=1)


def load_shares(amount, total, most, skew, full):
    weights = [(1 << 20) // math.isqrt(rank ** skew) + 1 for rank in range(1, amount + 1)]
    largest = most if full else min(most, max(-(-total // amount), total * weights[0] // sum(weights)))
    least = 1 if total - largest >= amount - 1 else 0
    counts, rest = [largest] + [least] * (amount - 1), total - largest - least * (amount - 1)
    while rest > 0:
        movable = [i for i in range(1, amount) if counts[i] < largest] or [i for i in range(1, amount) if counts[i] < most]
        mass, budget = sum([weights[i] for i in movable]), rest
        for i in movable:
            addition = min(most - counts[i], max(1, budget * weights[i] // mass), rest)
            counts[i] = counts[i] + addition
            rest = rest - addition
    return np.array(counts)


def noise(rng, shape, width, bound, cuts=(), kind=jnp.bfloat16):
    drawn = width * jax.random.normal(rng, shape, jnp.float32)
    if cuts:
        drawn = drawn * level_of(rng, shape, cuts, -0.22, 0.18)
    return jnp.clip(drawn, -bound, bound).astype(kind)


def setup_inputs(seed: int = 0, part: int = 0) -> dict:
    streams_of = jax.random.split(jax.random.key(seed), 7)
    own_keys = jax.random.split(jax.random.fold_in(streams_of[6], part), 7)
    latlon_cot = noise(own_keys[0], (3, LEVELS, LL_TOT), 1.0, 6.0, ((2, 16),), jnp.float32)
    dest_tile_keys = jax.random.split(jax.random.fold_in(streams_of[1], 1), LL_TOT // LL_DEV)
    dest_tile_turns = jax.random.permutation(jax.random.fold_in(streams_of[1], 3), LL_TOT // LL_DEV)
    dest_tile = jax.vmap(lambda own, number: deal_out(jax.random.fold_in(streams_of[1], 2), own, number, LL_DEV, TILES, 1, CAP, 2))(dest_tile_keys, dest_tile_turns).reshape((LL_TOT, 1))
    base_cell = plant(jax.random.randint(streams_of[2], (LL_TOT,), 0, (ROWS_DEV - 1) * (COLS_DEV - 1)), jax.random.fold_in(streams_of[2], 1), 0, ((ROWS_DEV - 1) * (COLS_DEV - 1)) - 1).astype(jnp.int32)
    corner_frac = jnp.clip(1.0 * jax.random.uniform(streams_of[3], (2, LL_TOT), jnp.float32) ** level_of(streams_of[3], (2, LL_TOT), ((1, 16),), -0.2, 0.2), 0.0, 1.0)
    saved_states = draw_saved_states(jax.random.fold_in(jax.random.fold_in(streams_of[6], part), 71), part)
    gravity = jnp.clip(jnp.exp(jax.random.uniform(streams_of[5], (LEVELS,), jnp.float32, math.log(0.5), math.log(4.0))), 0.5, 4.0)
    return dict(latlon_cot=latlon_cot, dest_tile=dest_tile, base_cell=base_cell, corner_frac=corner_frac, saved_states=saved_states, gravity=gravity)


time_step = 0.25
coriolis_peak = 0.8

def coriolis(grid_rows, total_rows):
    return coriolis_peak * (2.0 * (grid_rows + 0.5) / total_rows - 1.0)

def tendency(current, gravity, rotation):
    height, east_wind, north_wind = (current[0], current[1], current[2])
    gravity_col = gravity[:, None, None]

    def along_x(values):
        return 0.5 * (values[:, 1:-1, 2:] - values[:, 1:-1, :-2])

    def along_y(values):
        return 0.5 * (values[:, 2:, 1:-1] - values[:, :-2, 1:-1])

    def centre(values):
        return values[:, 1:-1, 1:-1]
    east_mid = centre(east_wind)
    north_mid = centre(north_wind)
    height_rate = -(along_x(height * east_wind) + along_y(height * north_wind))
    east_rate = -gravity_col * along_x(height) - east_mid * along_x(east_wind) - north_mid * along_y(east_wind) + rotation * north_mid
    north_rate = -gravity_col * along_y(height) - east_mid * along_x(north_wind) - north_mid * along_y(north_wind) - rotation * east_mid
    return jnp.stack([height_rate, east_rate, north_rate])

def corner_weights(along_rows, along_cols):
    return ((0, 0, (1.0 - along_rows) * (1.0 - along_cols)), (0, 1, (1.0 - along_rows) * along_cols), (1, 0, along_rows * (1.0 - along_cols)), (1, 1, along_rows * along_cols))

def extend(current):
    padded = jnp.pad(current, ((0, 0), (0, 0), (1, 1), (0, 0)))
    return jnp.concatenate([padded[..., -1:], padded, padded[..., :1]], axis=-1)

def reference(latlon_cot, dest_tile, base_cell, corner_frac, saved_states, gravity):
    target = dest_tile[:, 0]
    tile_row = target // N_FCOL
    tile_col = target % N_FCOL
    row_of = base_cell // (COLS_DEV - 1)
    col_of = base_cell % (COLS_DEV - 1)
    anchor = ((tile_row * ROWS_DEV + row_of) * NC + tile_col * COLS_DEV + col_of).astype(jnp.int32)

    def one_field(field_values):
        canvas = jnp.zeros((LEVELS, NR * NC), field_values.dtype)
        for row_step, col_step, weight in corner_weights(corner_frac[0], corner_frac[1]):
            canvas = canvas.at[:, anchor + row_step * NC + col_step].add(field_values * weight[None, :])
        return canvas
    adjoint = lax.map(one_field, latlon_cot).reshape(3, LEVELS, NR, NC)
    rotation = coriolis(jnp.arange(NR).astype(jnp.float32), NR)[:, None]

    def pull_back(current, cotangent):
        _, pullback = jax.vjp(lambda state_now: tendency(extend(state_now), gravity, rotation), current)
        return pullback(cotangent)[0]
    for which_step in (1, 0):
        middle = 0.5 * adjoint + 0.5 * time_step * pull_back(saved_states[which_step, 1], adjoint)
        adjoint = 0.5 * adjoint + middle + time_step * pull_back(saved_states[which_step, 0], middle)
    return adjoint
```

```python
import functools

import jax
import jax.numpy as jnp
from jax import lax
from jax.experimental import pallas as pl
from jax.experimental.pallas import tpu as pltpu
from jax.sharding import PartitionSpec as P

time_step = 0.25
coriolis_peak = 0.8

HALO = 4
GROUP = 256
LANES = 128
F32 = jnp.float32
BF16 = jnp.bfloat16
PARAMS = pltpu.CompilerParams(vmem_limit_bytes=40 * 1024 * 1024)


def split(values):
    high = values.astype(BF16)
    return high, (values - high.astype(F32)).astype(BF16)


def dot_nt(a, b):
    return lax.dot_general(a, b, (((1,), (1,)), ((), ())), preferred_element_type=F32)


def pack_kernel(capacity, tile_count, tile_rows, columns, cot, dest, base, frac, out, ranks, onehot, high, low):
    channels, points = cot.shape
    groups = out.shape[0]
    target = dest[...]
    corner = base[...]
    row = jnp.zeros_like(corner)
    for k in range(1, tile_rows - 1):
        row = row + (corner >= k * (columns - 1)).astype(jnp.int32)
    col = corner - row * (columns - 1)

    before = (
        lax.broadcasted_iota(jnp.int32, (GROUP, GROUP), 0)
        < lax.broadcasted_iota(jnp.int32, (GROUP, GROUP), 1)
    ).astype(F32).astype(BF16)
    tiles = lax.broadcasted_iota(jnp.int32, (tile_count, GROUP), 0)
    first = (tiles * capacity).astype(F32)
    count = jnp.zeros((tile_count, 1), F32)
    for b in range(points // GROUP):
        part = slice(b * GROUP, (b + 1) * GROUP)
        named = (tiles == target[:, part]).astype(F32)
        ahead = jnp.dot(named.astype(BF16), before, preferred_element_type=F32)
        place = jnp.sum(named * (ahead + count + first), axis=0, keepdims=True)
        count = count + jnp.sum(named, axis=1, keepdims=True)
        ranks[:, part] = place.astype(jnp.int32)
    place = ranks[...]
    group = place // GROUP
    lane = place - group * GROUP
    slots = lax.broadcasted_iota(jnp.int32, (GROUP, points), 0)
    onehot[...] = (slots == lane).astype(F32).astype(BF16)

    coords = jnp.concatenate([row.astype(F32), col.astype(F32), frac[...]], axis=0)
    data = jnp.concatenate([cot[...], coords, coords], axis=0)
    data_high, data_low = split(data)
    rows = data.shape[0]
    for g in range(groups):
        mine = (group == g).astype(F32).astype(BF16)
        high[g * rows : (g + 1) * rows, :] = data_high * mine
        low[g * rows : (g + 1) * rows, :] = data_low * mine
    upper = lax.broadcasted_iota(jnp.int32, (8, LANES), 0) < 4
    packed = dot_nt(high[...], onehot[...]) + dot_nt(low[...], onehot[...])
    for g in range(groups):
        block = packed[g * rows : (g + 1) * rows, :]
        out[g, :channels, :] = block[:channels, :LANES]
        out[g, channels : 2 * channels, :] = block[:channels, LANES:]
        out[g, 2 * channels :, :] = jnp.where(upper, block[channels:, :LANES], block[channels:, LANES:])


def pack(cot, dest, base, frac, capacity, tile_count, tile_rows, columns):
    channels, points = cot.shape
    groups = tile_count * capacity // GROUP
    rows = channels + 8
    return pl.pallas_call(
        functools.partial(pack_kernel, capacity, tile_count, tile_rows, columns),
        out_shape=jax.ShapeDtypeStruct((groups, 2 * channels + 8, LANES), F32),
        scratch_shapes=[
            pltpu.VMEM((1, points), jnp.int32),
            pltpu.VMEM((GROUP, points), BF16),
            pltpu.VMEM((groups * rows, points), BF16),
            pltpu.VMEM((groups * rows, points), BF16),
        ],
        compiler_params=PARAMS,
        name="pack_points",
    )(cot, dest, base, frac)


def scatter_kernel(got, canvas, north, south, high, low, weight):
    groups = got.shape[0]
    tile_rows, channels, columns = canvas.shape
    cells = lax.broadcasted_iota(jnp.int32, (columns, LANES), 0).astype(F32)
    lines = lax.broadcasted_iota(jnp.int32, (tile_rows, LANES), 0).astype(F32)

    def hat(index, corner, fraction):
        away = index - corner
        return jnp.where(away == 0.0, 1.0 - fraction, jnp.where(away == 1.0, fraction, 0.0))

    for g in range(groups):
        for half in range(2):
            part = slice((2 * g + half) * LANES, (2 * g + half + 1) * LANES)
            coords = got[g, 2 * channels + 4 * half : 2 * channels + 4 * half + 4, :]
            row, col, along_rows, along_cols = (coords[k : k + 1, :] for k in range(4))
            weight_high, weight_low = split(hat(cells, col, along_cols))
            weight[:columns, part] = weight_high
            weight[columns:, part] = weight_low
            values = got[g, half * channels : (half + 1) * channels, :]
            row_weight = hat(lines, row, along_rows)
            for r in range(tile_rows):
                product_high, product_low = split(values * row_weight[r : r + 1, :])
                high[r * channels : (r + 1) * channels, part] = product_high
                low[r * channels : (r + 1) * channels, part] = product_low
    both = dot_nt(high[...], weight[...])
    total = both[:, :columns] + both[:, columns:] + dot_nt(low[...], weight[:columns, :])
    for r in range(tile_rows):
        line = total[r * channels : (r + 1) * channels, :]
        canvas[r] = line
        if r < HALO:
            north[r] = line
        if r >= tile_rows - HALO:
            south[r - tile_rows + HALO] = line


def scatter(got, channels, tile_rows, columns):
    slots = got.shape[0] * GROUP
    return pl.pallas_call(
        scatter_kernel,
        out_shape=(
            jax.ShapeDtypeStruct((tile_rows, channels, columns), F32),
            jax.ShapeDtypeStruct((HALO, channels, columns), F32),
            jax.ShapeDtypeStruct((HALO, channels, columns), F32),
        ),
        scratch_shapes=[
            pltpu.VMEM((tile_rows * channels, slots), BF16),
            pltpu.VMEM((tile_rows * channels, slots), BF16),
            pltpu.VMEM((2 * columns, slots), BF16),
        ],
        compiler_params=PARAMS,
        name="scatter_points",
    )(got)


def edge_columns(lines):
    lane = lax.broadcasted_iota(jnp.int32, lines[0][1].shape, 1)
    owner = ((lane + 4) // 8) % 16
    result = jnp.zeros_like(lines[0][1])
    for k, line in lines:
        result = jnp.where(owner == k, pltpu.roll(line, (8 * k) % LANES, 1), result)
    return result


def beside(from_left, from_right):
    lane = lax.broadcasted_iota(jnp.int32, from_left.shape, 1)
    return jnp.where(lane % 8 < 4, from_right, from_left)


def row_mask(n_row):
    at = lax.axis_index("frow")
    return jnp.where(at > 0, 1.0, 0.0).astype(F32), jnp.where(at < n_row - 1, 1.0, 0.0).astype(F32)


def adjoint_edges_kernel(n_row, canvas, above, below, edges):
    tile_rows = canvas.shape[0]
    keep_above, keep_below = row_mask(n_row)
    lines = [(k, above[k] * keep_above) for k in range(HALO)]
    lines += [(HALO + k, canvas[k]) for k in range(tile_rows)]
    lines += [(HALO + tile_rows + k, below[k] * keep_below) for k in range(HALO)]
    edges[...] = edge_columns(lines)


def adjoint_edges(canvas, above, below, n_row):
    return pl.pallas_call(
        functools.partial(adjoint_edges_kernel, n_row),
        out_shape=jax.ShapeDtypeStruct(canvas.shape[1:], F32),
        compiler_params=PARAMS,
        name="adjoint_edges",
    )(canvas, above, below)


def first_row(which):
    return sum(HALO - k for k in range(which))


def turn_states_kernel(order, states, turned, north, south):
    tile_rows = turned.shape[1]
    channels = turned.shape[2]
    for which, source in enumerate(order):
        width = HALO - which
        for r in range(tile_rows):
            line = states[source, pl.ds(r, channels, stride=tile_rows), :]
            turned[which, r] = line
            if r < width:
                north[first_row(which) + r] = line
            if r >= tile_rows - width:
                south[first_row(which) + r - tile_rows + width] = line


def turn_states(states, order, channels, tile_rows, columns):
    stages = len(order)
    rim = first_row(stages)
    return pl.pallas_call(
        functools.partial(turn_states_kernel, order),
        out_shape=(
            jax.ShapeDtypeStruct((stages, tile_rows, channels, columns), F32),
            jax.ShapeDtypeStruct((rim, channels, columns), F32),
            jax.ShapeDtypeStruct((rim, channels, columns), F32),
        ),
        compiler_params=PARAMS,
        name="turn_states",
    )(states)


def state_lines(which, turned, above, below, keep_above, keep_below):
    tile_rows = turned.shape[1]
    width = HALO - which
    at = first_row(which)
    lines = [(HALO - width + k, above[at + k] * keep_above) for k in range(width)]
    lines += [(HALO + k, turned[which, k]) for k in range(tile_rows)]
    lines += [(HALO + tile_rows + k, below[at + k] * keep_below) for k in range(width)]
    return lines


def state_edges_kernel(n_row, turned, above, below, edges):
    keep_above, keep_below = row_mask(n_row)
    for which in range(turned.shape[0]):
        edges[which] = edge_columns(state_lines(which, turned, above, below, keep_above, keep_below))


def state_edges(turned, above, below, n_row):
    stages, _, channels, columns = turned.shape
    return pl.pallas_call(
        functools.partial(state_edges_kernel, n_row),
        out_shape=jax.ShapeDtypeStruct((stages, channels, columns), F32),
        compiler_params=PARAMS,
        name="state_edges",
    )(turned, above, below)


def widen_states_kernel(n_row, turned, above, below, from_left, from_right, wide):
    columns = turned.shape[3]
    keep_above, keep_below = row_mask(n_row)
    for which in range(turned.shape[0]):
        rim = beside(from_left[which], from_right[which])
        for k, line in state_lines(which, turned, above, below, keep_above, keep_below):
            wide[which, k, :, :columns] = line
            wide[which, k, :, columns:] = pltpu.roll(rim, (-8 * k) % LANES, 1)


def widen_states(turned, above, below, from_left, from_right, n_row):
    stages, tile_rows, channels, columns = turned.shape
    return pl.pallas_call(
        functools.partial(widen_states_kernel, n_row),
        out_shape=jax.ShapeDtypeStruct((stages, tile_rows + 2 * HALO, channels, 2 * columns), F32),
        compiler_params=PARAMS,
        name="widen_states",
    )(turned, above, below, from_left, from_right)


def steps_kernel(n_row, canvas, above, below, from_left, from_right, wide, gravity, out, start, middle, after, last):
    tile_rows, channels, columns = canvas.shape
    levels = channels // 3
    total_rows = tile_rows * n_row
    base_row = lax.axis_index("frow") * tile_rows
    keep_above, keep_below = row_mask(n_row)
    rim = beside(from_left[...], from_right[...])
    lines = [(k, above[k] * keep_above) for k in range(HALO)]
    lines += [(HALO + k, canvas[k]) for k in range(tile_rows)]
    lines += [(HALO + tile_rows + k, below[k] * keep_below) for k in range(HALO)]
    for k, line in lines:
        start[k, :, :columns] = line
        start[k, :, columns:] = pltpu.roll(rim, (-8 * k) % LANES, 1)
    pull = jnp.broadcast_to(gravity[...], (levels, 2 * columns))

    def along_x(values):
        return 0.5 * (pltpu.roll(values, 2 * columns - 1, 1) - pltpu.roll(values, 1, 1))

    def field(ref, k, which):
        return ref[k, which * levels : (which + 1) * levels, :]

    def pull_back(stage, adjoint, k):
        a, b, c = (field(adjoint, k, w) for w in range(3))
        a_up, b_up, c_up = (field(adjoint, k - 1, w) for w in range(3))
        a_down, b_down, c_down = (field(adjoint, k + 1, w) for w in range(3))
        state = wide.at[stage]
        h, u, v = (field(state, k, w) for w in range(3))
        u_up, v_up = (field(state, k - 1, w) for w in (1, 2))
        u_down, v_down = (field(state, k + 1, w) for w in (1, 2))
        rotation = coriolis_peak * (2.0 * ((base_row + k - HALO).astype(F32) + 0.5) / total_rows - 1.0)
        a_x = along_x(a)
        a_y = 0.5 * (a_down - a_up)
        height = u * a_x + v * a_y + pull * (along_x(b) + 0.5 * (c_down - c_up))
        east = (
            h * a_x
            + along_x(u * b)
            + 0.5 * (v_down * b_down - v_up * b_up)
            - b * along_x(u)
            - c * along_x(v)
            - rotation * c
        )
        north = (
            h * a_y
            + along_x(u * c)
            + 0.5 * (v_down * c_down - v_up * c_up)
            - b * (0.5 * (u_down - u_up))
            - c * (0.5 * (v_down - v_up))
            + rotation * b
        )
        return (a, b, c), (height, east, north)

    def keep(k):
        row = base_row + k - HALO
        return jnp.where((row >= 0) & (row < total_rows), 1.0, 0.0).astype(F32)

    def half_step(stage, adjoint, result):
        def body(k, _):
            old, change = pull_back(stage, adjoint, k)
            for w in range(3):
                result[k, w * levels : (w + 1) * levels, :] = keep(k) * (
                    0.5 * old[w] + (0.5 * time_step) * change[w]
                )
            return 0

        width = HALO - 1 - stage
        lax.fori_loop(HALO - width, HALO + tile_rows + width, body, 0, unroll=2)

    def full_step(stage, adjoint, mid, store):
        def body(k, _):
            mids, change = pull_back(stage, mid, k)
            for w in range(3):
                store(k, w, 0.5 * field(adjoint, k, w) + mids[w] + time_step * change[w])
            return 0

        width = HALO - 1 - stage
        lax.fori_loop(HALO - width, HALO + tile_rows + width, body, 0, unroll=2)

    def to_after(k, w, value):
        after[k, w * levels : (w + 1) * levels, :] = keep(k) * value

    def to_out(k, w, value):
        out[pl.ds(w * levels * tile_rows + k - HALO, levels, stride=tile_rows), :] = value[:, :columns]

    half_step(0, start, middle)
    full_step(1, start, middle, to_after)
    half_step(2, after, last)
    full_step(3, after, last, to_out)


def steps(canvas, above, below, from_left, from_right, wide, gravity, n_row):
    tile_rows, channels, columns = canvas.shape
    extended = pltpu.VMEM((tile_rows + 2 * HALO, channels, 2 * columns), F32)
    return pl.pallas_call(
        functools.partial(steps_kernel, n_row),
        out_shape=jax.ShapeDtypeStruct((channels * tile_rows, columns), F32),
        scratch_shapes=[extended] * 4,
        compiler_params=PARAMS,
        name="adjoint_steps",
    )(canvas, above, below, from_left, from_right, wide, gravity)


def shifted(values, axis, by):
    count = lax.axis_size(axis)
    return lax.ppermute(values, axis, [(i, (i + by) % count) for i in range(count)])


def to_partners(packed, channels, capacity, tile_count):
    if capacity == GROUP:
        return lax.all_to_all(packed, ("frow", "fcol"), split_axis=0, concat_axis=0, tiled=True)
    groups = packed.shape[0]
    rows = channels + 4
    halves = [
        jnp.concatenate(
            [
                packed[:, h * channels : (h + 1) * channels],
                packed[:, 2 * channels + 4 * h : 2 * channels + 4 * h + 4],
            ],
            axis=1,
        )
        for h in range(2)
    ]
    slots = jnp.stack(halves, axis=2).transpose(1, 0, 2, 3).reshape(rows, tile_count, capacity)
    slots = lax.all_to_all(slots, ("frow", "fcol"), split_axis=1, concat_axis=1, tiled=True)
    slots = slots.reshape(rows, groups, 2, LANES).transpose(1, 2, 0, 3)
    return jnp.concatenate(
        [slots[:, 0, :channels], slots[:, 1, :channels], slots[:, 0, channels:], slots[:, 1, channels:]], axis=1
    )


def per_device(latlon_cot, dest_tile, base_cell, corner_frac, saved_states, gravity):
    n_row = lax.axis_size("frow")
    tile_count = n_row * lax.axis_size("fcol")
    levels = gravity.shape[0]
    tile_rows = saved_states.shape[4]
    columns = saved_states.shape[5]
    channels = 3 * levels
    points = base_cell.shape[0]
    capacity = 2 * points // tile_count

    packed = pack(
        latlon_cot.reshape(channels, points),
        dest_tile.reshape(1, points),
        base_cell.reshape(1, points),
        corner_frac,
        capacity,
        tile_count,
        tile_rows,
        columns,
    )
    got = to_partners(packed, channels, capacity, tile_count)

    turned, north, south = turn_states(
        saved_states.reshape(4, channels * tile_rows, columns), (3, 2, 1, 0), channels, tile_rows, columns
    )
    state_above = shifted(south, "frow", 1)
    state_below = shifted(north, "frow", -1)
    edges = state_edges(turned, state_above, state_below, n_row)
    wide = widen_states(
        turned, state_above, state_below, shifted(edges, "fcol", 1), shifted(edges, "fcol", -1), n_row
    )

    canvas, north, south = scatter(got, channels, tile_rows, columns)
    above = shifted(south, "frow", 1)
    below = shifted(north, "frow", -1)
    edges = adjoint_edges(canvas, above, below, n_row)
    result = steps(
        canvas,
        above,
        below,
        shifted(edges, "fcol", 1),
        shifted(edges, "fcol", -1),
        wide,
        gravity.reshape(levels, 1),
        n_row,
    )
    return result.reshape(3, levels, tile_rows, columns)


def solution(mesh):
    placed = (
        P(None, None, ("member", "frow", "fcol")),
        P(("frow", "fcol"), None),
        P(("frow", "fcol")),
        P(None, ("frow", "fcol")),
        P(None, None, None, None, ("member", "frow"), "fcol"),
        P(),
    )
    return jax.shard_map(
        per_device,
        mesh=mesh,
        in_specs=placed,
        out_specs=P(None, None, ("member", "frow"), "fcol"),
        check_vma=False,
    )
```

```python
import functools

import jax
import jax.numpy as jnp
from jax import lax
from jax.experimental import pallas as pl
from jax.experimental.pallas import tpu as pltpu
from jax.sharding import PartitionSpec as P

time_step = 0.25
coriolis_peak = 0.8

HALO = 4
GROUP = 256
LANES = 128
F32 = jnp.float32
BF16 = jnp.bfloat16
PARAMS = pltpu.CompilerParams(vmem_limit_bytes=40 * 1024 * 1024)


def split(values):
    high = values.astype(BF16)
    return high, (values - high.astype(F32)).astype(BF16)


def dot_nt(a, b):
    return lax.dot_general(a, b, (((1,), (1,)), ((), ())), preferred_element_type=F32)


def slot_blocks(cot, where, group, lane, groups, tile_rows, columns, onehot, high, low):
    channels, points = cot.shape
    corner = where[1:2, :]
    row = jnp.zeros_like(corner)
    for k in range(1, tile_rows - 1):
        row = row + (corner >= float(k * (columns - 1))).astype(F32)
    col = corner - row * float(columns - 1)
    coords = jnp.concatenate([row, col, where[2:, :]], axis=0)
    data = jnp.concatenate([cot[...], coords, coords], axis=0)
    data_high, data_low = split(data)
    slots = lax.broadcasted_iota(jnp.int32, (GROUP, points), 0)
    onehot[...] = (slots == lane).astype(F32).astype(BF16)
    rows = channels + 8
    for g in range(groups):
        mine = (group == g).astype(F32).astype(BF16)
        high[g * rows : (g + 1) * rows, :] = data_high * mine
        low[g * rows : (g + 1) * rows, :] = data_low * mine
    packed = dot_nt(high[...], onehot[...]) + dot_nt(low[...], onehot[...])
    upper = lax.broadcasted_iota(jnp.int32, (8, LANES), 0) < 4
    for g in range(groups):
        block = packed[g * rows : (g + 1) * rows, :]
        yield (
            block[:channels, :LANES],
            block[:channels, LANES:],
            jnp.where(upper, block[channels:, :LANES], block[channels:, LANES:]),
        )


def count_ahead(target, tiles, base, place):
    before = (
        lax.broadcasted_iota(jnp.int32, (GROUP, GROUP), 0)
        < lax.broadcasted_iota(jnp.int32, (GROUP, GROUP), 1)
    ).astype(F32).astype(BF16)
    count = jnp.zeros((tiles.shape[0], 1), F32)
    for b in range(target.shape[1] // GROUP):
        part = slice(b * GROUP, (b + 1) * GROUP)
        named = (tiles == target[:, part]).astype(F32)
        ahead = jnp.dot(named.astype(BF16), before, preferred_element_type=F32)
        found = jnp.sum(named * (ahead + count + base + 1.0), axis=0, keepdims=True)
        count = count + jnp.sum(named, axis=1, keepdims=True)
        place[:, part] = found.astype(jnp.int32) - 1


def store_block(out, at, pieces):
    channels = pieces[0].shape[0]
    out[at : at + channels, :] = pieces[0]
    out[at + channels : at + 2 * channels, :] = pieces[1]
    out[at + 2 * channels : at + 2 * channels + 8, :] = pieces[2]


def pack_scratch(channels, points, groups):
    return [
        pltpu.VMEM((1, points), jnp.int32),
        pltpu.VMEM((GROUP, points), BF16),
        pltpu.VMEM((groups * (channels + 8), points), BF16),
        pltpu.VMEM((groups * (channels + 8), points), BF16),
    ]


def pack_all_kernel(capacity, tile_count, tile_rows, columns, cot, where, out, place, onehot, high, low):
    tiles = lax.broadcasted_iota(jnp.int32, (tile_count, GROUP), 0)
    count_ahead(where[0:1, :].astype(jnp.int32), tiles, (tiles * capacity).astype(F32), place)
    slot = place[...]
    group = slot // GROUP
    blocks = slot_blocks(
        cot, where, group, slot - group * GROUP, out.shape[0], tile_rows, columns, onehot, high, low
    )
    for g, pieces in enumerate(blocks):
        store_block(out.at[g], 0, pieces)


def pack_all(cot, where, capacity, tile_count, tile_rows, columns):
    channels, points = cot.shape
    groups = tile_count * capacity // GROUP
    return pl.pallas_call(
        functools.partial(pack_all_kernel, capacity, tile_count, tile_rows, columns),
        out_shape=jax.ShapeDtypeStruct((groups, 2 * channels + 8, LANES), F32),
        scratch_shapes=pack_scratch(channels, points, groups),
        compiler_params=PARAMS,
        name="pack_points",
    )(cot, where)


def chip_offsets(n_row, n_col):
    offsets = [(0, 0)]
    for step in sorted(range(n_col), key=lambda z: -(z & -z) if z else 1):
        offsets += [(other, step) for other in range(0, n_row, 2) if (other, step) != (0, 0)]
    return offsets


def pack_chips_kernel(offsets, n_col, tile_rows, columns, cot, where, *refs):
    outs, (place, onehot, high, low) = refs[:-4], refs[-4:]
    own = None
    if len(outs) > 1:
        own, outs = outs[0], outs[1:]
    groups = len(offsets)
    at_row, at_col = lax.axis_index("frow"), lax.axis_index("fcol")
    index = lax.broadcasted_iota(jnp.int32, (groups, GROUP), 0)
    tiles = jnp.zeros((groups, GROUP), jnp.int32)
    for g, (df, dz) in enumerate(offsets):
        tiles = jnp.where(index == g, (at_row ^ df) * n_col + (at_col ^ dz), tiles)
    count_ahead(where[0:1, :].astype(jnp.int32), tiles, (index * GROUP).astype(F32), place)
    slot = place[...]
    group = jnp.where(slot < 0, groups, slot // GROUP)
    blocks = slot_blocks(
        cot, where, group, slot - group * GROUP, groups, tile_rows, columns, onehot, high, low
    )
    for g, pieces in enumerate(blocks):
        if own is None:
            store_block(outs[0].at[g], 0, pieces)
        else:
            size = own.shape[1]
            outs[g][:size, :] = own[g]
            store_block(outs[g], size, pieces)


def pack_chips(cot, where, own, offsets, n_col, tile_rows, columns):
    channels, points = cot.shape
    rows, groups = 2 * channels + 8, len(offsets)
    if own is None:
        shapes = jax.ShapeDtypeStruct((groups, rows, LANES), F32)
    else:
        shapes = [jax.ShapeDtypeStruct((2 * rows, LANES), F32)] * groups
    return pl.pallas_call(
        functools.partial(pack_chips_kernel, offsets, n_col, tile_rows, columns),
        out_shape=shapes,
        scratch_shapes=pack_scratch(channels, points, groups),
        compiler_params=PARAMS,
        name="pack_own" if own is None else "pack_partner",
    )(cot, where, *([] if own is None else [own]))


def scatter_kernel(count, first, last, *refs):
    blocks, refs = refs[:count], refs[count:]
    if not first:
        total, refs = refs[0], refs[1:]
    outs, (high, low, weight) = refs[:-3], refs[-3:]
    tile_rows, channels, columns = outs[0].shape
    rows = 2 * channels + 8
    cells = lax.broadcasted_iota(jnp.int32, (columns, LANES), 0).astype(F32)
    lines = lax.broadcasted_iota(jnp.int32, (tile_rows, LANES), 0).astype(F32)

    def hat(index, corner, fraction):
        away = index - corner
        return jnp.where(away == 0.0, 1.0 - fraction, jnp.where(away == 1.0, fraction, 0.0))

    at = 0
    for block in blocks:
        for source in range(block.shape[0] // rows):
            for half in range(2):
                part = slice(at, at + LANES)
                at += LANES
                begin = source * rows + 2 * channels + 4 * half
                coords = block[begin : begin + 4, :]
                row, col, along_rows, along_cols = (coords[k : k + 1, :] for k in range(4))
                weight_high, weight_low = split(hat(cells, col, along_cols))
                weight[:columns, part] = weight_high
                weight[columns:, part] = weight_low
                begin = source * rows + half * channels
                values = block[begin : begin + channels, :]
                row_weight = hat(lines, row, along_rows)
                for r in range(tile_rows):
                    product_high, product_low = split(values * row_weight[r : r + 1, :])
                    high[r * channels : (r + 1) * channels, part] = product_high
                    low[r * channels : (r + 1) * channels, part] = product_low
    both = dot_nt(high[...], weight[...])
    sums = both[:, :columns] + both[:, columns:] + dot_nt(low[...], weight[:columns, :])
    for r in range(tile_rows):
        line = sums[r * channels : (r + 1) * channels, :]
        if not first:
            line = line + total[r]
        outs[0][r] = line
        if last and r < HALO:
            outs[1][r] = line
        if last and r >= tile_rows - HALO:
            outs[2][r - tile_rows + HALO] = line


def scatter(blocks, total, last, channels, tile_rows, columns):
    slots = sum(block.shape[0] for block in blocks) // (2 * channels + 8) * GROUP
    shapes = [jax.ShapeDtypeStruct((tile_rows, channels, columns), F32)]
    if last:
        shapes += [jax.ShapeDtypeStruct((HALO, channels, columns), F32)] * 2
    return pl.pallas_call(
        functools.partial(scatter_kernel, len(blocks), total is None, last),
        out_shape=shapes,
        scratch_shapes=[
            pltpu.VMEM((tile_rows * channels, slots), BF16),
            pltpu.VMEM((tile_rows * channels, slots), BF16),
            pltpu.VMEM((2 * columns, slots), BF16),
        ],
        compiler_params=PARAMS,
        name="scatter_points",
    )(*blocks, *([] if total is None else [total]))


def edge_columns(lines):
    lane = lax.broadcasted_iota(jnp.int32, lines[0][1].shape, 1)
    owner = ((lane + 4) // 8) % 16
    result = jnp.zeros_like(lines[0][1])
    for k, line in lines:
        result = jnp.where(owner == k, pltpu.roll(line, (8 * k) % LANES, 1), result)
    return result


def beside(from_left, from_right):
    lane = lax.broadcasted_iota(jnp.int32, from_left.shape, 1)
    return jnp.where(lane % 8 < 4, from_right, from_left)


def row_mask(n_row):
    at = lax.axis_index("frow")
    return jnp.where(at > 0, 1.0, 0.0).astype(F32), jnp.where(at < n_row - 1, 1.0, 0.0).astype(F32)


def adjoint_edges_kernel(n_row, canvas, above, below, edges):
    tile_rows = canvas.shape[0]
    keep_above, keep_below = row_mask(n_row)
    lines = [(k, above[k] * keep_above) for k in range(HALO)]
    lines += [(HALO + k, canvas[k]) for k in range(tile_rows)]
    lines += [(HALO + tile_rows + k, below[k] * keep_below) for k in range(HALO)]
    edges[...] = edge_columns(lines)


def adjoint_edges(canvas, above, below, n_row):
    return pl.pallas_call(
        functools.partial(adjoint_edges_kernel, n_row),
        out_shape=jax.ShapeDtypeStruct(canvas.shape[1:], F32),
        compiler_params=PARAMS,
        name="adjoint_edges",
    )(canvas, above, below)


def first_row(which):
    return sum(HALO - k for k in range(which))


def turn_states_kernel(order, states, turned, north, south):
    tile_rows = turned.shape[1]
    channels = turned.shape[2]
    for which, source in enumerate(order):
        width = HALO - which
        for r in range(tile_rows):
            line = states[source, pl.ds(r, channels, stride=tile_rows), :]
            turned[which, r] = line
            if r < width:
                north[first_row(which) + r] = line
            if r >= tile_rows - width:
                south[first_row(which) + r - tile_rows + width] = line


def turn_states(states, order, channels, tile_rows, columns):
    stages = len(order)
    rim = first_row(stages)
    return pl.pallas_call(
        functools.partial(turn_states_kernel, order),
        out_shape=(
            jax.ShapeDtypeStruct((stages, tile_rows, channels, columns), F32),
            jax.ShapeDtypeStruct((rim, channels, columns), F32),
            jax.ShapeDtypeStruct((rim, channels, columns), F32),
        ),
        compiler_params=PARAMS,
        name="turn_states",
    )(states)


def state_lines(which, turned, above, below, keep_above, keep_below):
    tile_rows = turned.shape[1]
    width = HALO - which
    at = first_row(which)
    lines = [(HALO - width + k, above[at + k] * keep_above) for k in range(width)]
    lines += [(HALO + k, turned[which, k]) for k in range(tile_rows)]
    lines += [(HALO + tile_rows + k, below[at + k] * keep_below) for k in range(width)]
    return lines


def state_edges_kernel(n_row, turned, above, below, edges):
    keep_above, keep_below = row_mask(n_row)
    for which in range(turned.shape[0]):
        edges[which] = edge_columns(state_lines(which, turned, above, below, keep_above, keep_below))


def state_edges(turned, above, below, n_row):
    stages, _, channels, columns = turned.shape
    return pl.pallas_call(
        functools.partial(state_edges_kernel, n_row),
        out_shape=jax.ShapeDtypeStruct((stages, channels, columns), F32),
        compiler_params=PARAMS,
        name="state_edges",
    )(turned, above, below)


def widen_states_kernel(n_row, turned, above, below, from_left, from_right, wide):
    columns = turned.shape[3]
    keep_above, keep_below = row_mask(n_row)
    for which in range(turned.shape[0]):
        rim = beside(from_left[which], from_right[which])
        for k, line in state_lines(which, turned, above, below, keep_above, keep_below):
            wide[which, k, :, :columns] = line
            wide[which, k, :, columns:] = pltpu.roll(rim, (-8 * k) % LANES, 1)


def widen_states(turned, above, below, from_left, from_right, n_row):
    stages, tile_rows, channels, columns = turned.shape
    return pl.pallas_call(
        functools.partial(widen_states_kernel, n_row),
        out_shape=jax.ShapeDtypeStruct((stages, tile_rows + 2 * HALO, channels, 2 * columns), F32),
        compiler_params=PARAMS,
        name="widen_states",
    )(turned, above, below, from_left, from_right)


def steps_kernel(n_row, canvas, above, below, from_left, from_right, wide, gravity, out, start, middle, after, last):
    tile_rows, channels, columns = canvas.shape
    levels = channels // 3
    total_rows = tile_rows * n_row
    base_row = lax.axis_index("frow") * tile_rows
    keep_above, keep_below = row_mask(n_row)
    rim = beside(from_left[...], from_right[...])
    lines = [(k, above[k] * keep_above) for k in range(HALO)]
    lines += [(HALO + k, canvas[k]) for k in range(tile_rows)]
    lines += [(HALO + tile_rows + k, below[k] * keep_below) for k in range(HALO)]
    for k, line in lines:
        start[k, :, :columns] = line
        start[k, :, columns:] = pltpu.roll(rim, (-8 * k) % LANES, 1)
    pull = jnp.broadcast_to(gravity[...], (levels, 2 * columns))

    def along_x(values):
        return 0.5 * (pltpu.roll(values, 2 * columns - 1, 1) - pltpu.roll(values, 1, 1))

    def field(ref, k, which):
        return ref[k, which * levels : (which + 1) * levels, :]

    def pull_back(stage, adjoint, k):
        a, b, c = (field(adjoint, k, w) for w in range(3))
        a_up, b_up, c_up = (field(adjoint, k - 1, w) for w in range(3))
        a_down, b_down, c_down = (field(adjoint, k + 1, w) for w in range(3))
        state = wide.at[stage]
        h, u, v = (field(state, k, w) for w in range(3))
        u_up, v_up = (field(state, k - 1, w) for w in (1, 2))
        u_down, v_down = (field(state, k + 1, w) for w in (1, 2))
        rotation = coriolis_peak * (2.0 * ((base_row + k - HALO).astype(F32) + 0.5) / total_rows - 1.0)
        a_x = along_x(a)
        a_y = 0.5 * (a_down - a_up)
        height = u * a_x + v * a_y + pull * (along_x(b) + 0.5 * (c_down - c_up))
        east = (
            h * a_x
            + along_x(u * b)
            + 0.5 * (v_down * b_down - v_up * b_up)
            - b * along_x(u)
            - c * along_x(v)
            - rotation * c
        )
        north = (
            h * a_y
            + along_x(u * c)
            + 0.5 * (v_down * c_down - v_up * c_up)
            - b * (0.5 * (u_down - u_up))
            - c * (0.5 * (v_down - v_up))
            + rotation * b
        )
        return (a, b, c), (height, east, north)

    def keep(k):
        row = base_row + k - HALO
        return jnp.where((row >= 0) & (row < total_rows), 1.0, 0.0).astype(F32)

    def half_step(stage, adjoint, result):
        def body(k, _):
            old, change = pull_back(stage, adjoint, k)
            for w in range(3):
                result[k, w * levels : (w + 1) * levels, :] = keep(k) * (
                    0.5 * old[w] + (0.5 * time_step) * change[w]
                )
            return 0

        width = HALO - 1 - stage
        lax.fori_loop(HALO - width, HALO + tile_rows + width, body, 0, unroll=2)

    def full_step(stage, adjoint, mid, store):
        def body(k, _):
            mids, change = pull_back(stage, mid, k)
            for w in range(3):
                store(k, w, 0.5 * field(adjoint, k, w) + mids[w] + time_step * change[w])
            return 0

        width = HALO - 1 - stage
        lax.fori_loop(HALO - width, HALO + tile_rows + width, body, 0, unroll=2)

    def to_after(k, w, value):
        after[k, w * levels : (w + 1) * levels, :] = keep(k) * value

    def to_out(k, w, value):
        out[pl.ds(w * levels * tile_rows + k - HALO, levels, stride=tile_rows), :] = value[:, :columns]

    half_step(0, start, middle)
    full_step(1, start, middle, to_after)
    half_step(2, after, last)
    full_step(3, after, last, to_out)


def steps(canvas, above, below, from_left, from_right, wide, gravity, n_row):
    tile_rows, channels, columns = canvas.shape
    extended = pltpu.VMEM((tile_rows + 2 * HALO, channels, 2 * columns), F32)
    return pl.pallas_call(
        functools.partial(steps_kernel, n_row),
        out_shape=jax.ShapeDtypeStruct((channels * tile_rows, columns), F32),
        scratch_shapes=[extended] * 4,
        compiler_params=PARAMS,
        name="adjoint_steps",
    )(canvas, above, below, from_left, from_right, wide, gravity)


def shifted(values, axis, by):
    count = lax.axis_size(axis)
    return lax.ppermute(values, axis, [(i, (i + by) % count) for i in range(count)])


def from_everyone(packed, channels, capacity, tile_count):
    groups = packed.shape[0]
    rows = channels + 4
    halves = [
        jnp.concatenate(
            [
                packed[:, h * channels : (h + 1) * channels],
                packed[:, 2 * channels + 4 * h : 2 * channels + 4 * h + 4],
            ],
            axis=1,
        )
        for h in range(2)
    ]
    slots = jnp.stack(halves, axis=2).transpose(1, 0, 2, 3).reshape(rows, tile_count, capacity)
    slots = lax.all_to_all(slots, ("frow", "fcol"), split_axis=1, concat_axis=1, tiled=True)
    slots = slots.reshape(rows, groups, 2, LANES).transpose(1, 2, 0, 3)
    return jnp.concatenate(
        [slots[:, 0, :channels], slots[:, 1, :channels], slots[:, 0, channels:], slots[:, 1, channels:]], axis=1
    )


def exchanged(values, offset, n_row, n_col):
    df, dz = offset
    pairs = [(f * n_col + z, (f ^ df) * n_col + (z ^ dz)) for f in range(n_row) for z in range(n_col)]
    return lax.ppermute(values, ("frow", "fcol"), pairs)


def per_device(latlon_cot, dest_tile, base_cell, corner_frac, saved_states, gravity):
    n_row, n_col = lax.axis_size("frow"), lax.axis_size("fcol")
    tile_count = n_row * n_col
    levels = gravity.shape[0]
    tile_rows = saved_states.shape[4]
    columns = saved_states.shape[5]
    channels = 3 * levels
    points = base_cell.shape[0]
    capacity = 2 * points // tile_count

    cot = latlon_cot.reshape(channels, points)
    where = jnp.concatenate(
        [dest_tile.reshape(1, points).astype(F32), base_cell.reshape(1, points).astype(F32), corner_frac], axis=0
    )
    size = (channels, tile_rows, columns)
    if capacity == GROUP and n_row & (n_row - 1) == 0 and n_col & (n_col - 1) == 0:
        offsets = chip_offsets(n_row, n_col)
        partner_cot = exchanged(cot, (1, 0), n_row, n_col)
        partner_where = exchanged(where, (1, 0), n_row, n_col)
        own = pack_chips(cot, where, None, offsets, n_col, tile_rows, columns)
        packed = pack_chips(partner_cot, partner_where, own, offsets, n_col, tile_rows, columns)
        got = [packed[0]] + [
            exchanged(block, offset, n_row, n_col) for block, offset in zip(packed[1:], offsets[1:])
        ]
        total = None
        for begin, end in ((0, 3), (3, 6), (6, len(got))):
            last = end == len(got)
            canvas = scatter(got[begin:end], total, last, *size)
            total = canvas[0]
        canvas, north_rim, south_rim = canvas
    else:
        packed = pack_all(cot, where, capacity, tile_count, tile_rows, columns)
        got = from_everyone(packed, channels, capacity, tile_count)
        canvas, north_rim, south_rim = scatter([got.reshape(-1, LANES)], None, True, *size)

    turned, north, south = turn_states(
        saved_states.reshape(4, channels * tile_rows, columns), (3, 2, 1, 0), channels, tile_rows, columns
    )
    state_above = shifted(south, "frow", 1)
    state_below = shifted(north, "frow", -1)
    edges = state_edges(turned, state_above, state_below, n_row)
    wide = widen_states(
        turned, state_above, state_below, shifted(edges, "fcol", 1), shifted(edges, "fcol", -1), n_row
    )

    above = shifted(south_rim, "frow", 1)
    below = shifted(north_rim, "frow", -1)
    edges = adjoint_edges(canvas, above, below, n_row)
    result = steps(
        canvas,
        above,
        below,
        shifted(edges, "fcol", 1),
        shifted(edges, "fcol", -1),
        wide,
        gravity.reshape(levels, 1),
        n_row,
    )
    return result.reshape(3, levels, tile_rows, columns)


def solution(mesh):
    placed = (
        P(None, None, ("member", "frow", "fcol")),
        P(("frow", "fcol"), None),
        P(("frow", "fcol")),
        P(None, ("frow", "fcol")),
        P(None, None, None, None, ("member", "frow"), "fcol"),
        P(),
    )
    return jax.shard_map(
        per_device,
        mesh=mesh,
        in_specs=placed,
        out_specs=P(None, None, ("member", "frow"), "fcol"),
        check_vma=False,
    )
```

```python
import functools

import jax
import jax.numpy as jnp
from jax import lax
from jax.experimental import pallas as pl
from jax.experimental.pallas import tpu as pltpu
from jax.sharding import PartitionSpec as P

time_step = 0.25
coriolis_peak = 0.8

HALO = 4
GROUP = 256
LANES = 128
F32 = jnp.float32
BF16 = jnp.bfloat16
PARAMS = pltpu.CompilerParams(vmem_limit_bytes=16 * 1024 * 1024)


def split(values):
    high = values.astype(BF16)
    return high, (values - high.astype(F32)).astype(BF16)


def dot_nt(a, b):
    return lax.dot_general(a, b, (((1,), (1,)), ((), ())), preferred_element_type=F32)


def first_of_pair(axis="frow"):
    return lax.rem(lax.axis_index(axis), 2) == 0


def row_masks(n_row):
    at = lax.axis_index("frow")
    return jnp.where(at > 0, 1.0, 0.0).astype(F32), jnp.where(at < n_row - 1, 1.0, 0.0).astype(F32)


def extended_rows(tile, pair, cross, width, lower, masks):
    tile_rows = len(tile)
    lines = [(HALO - width + k, jnp.where(lower, cross[k], pair[k]) * masks[0]) for k in range(width)]
    lines += [(HALO + k, tile[k]) for k in range(tile_rows)]
    lines += [(HALO + tile_rows + k, jnp.where(lower, pair[k], cross[k]) * masks[1]) for k in range(width)]
    return lines


def edge_columns(lines):
    lane = lax.broadcasted_iota(jnp.int32, lines[0][1].shape, 1)
    owner = ((lane + 4) // 8) % 16
    result = jnp.zeros_like(lines[0][1])
    for k, line in lines:
        result = jnp.where(owner == k, pltpu.roll(line, (8 * k) % LANES, 1), result)
    return result


def first_lanes(like):
    return lax.broadcasted_iota(jnp.int32, like.shape, 1) % 8 < 4


def from_sides(one, other, paired):
    if not paired:
        return one, other
    lower = first_of_pair("fcol")
    return jnp.where(lower, other, one), jnp.where(lower, one, other)


def first_row(which):
    return sum(HALO - k for k in range(which))


def prepare_kernel(order, dest, base, frac, states, cot, sent, cross, turned, cot_out, dest_v, base_v, frac_v, states_v, sems):
    moves = ((dest, dest_v), (base, base_v), (frac, frac_v), (states, states_v), (cot, cot_out))
    copies = [pltpu.make_async_copy(source, target, sems.at[i]) for i, (source, target) in enumerate(moves)]
    for copy in copies:
        copy.start()
    for copy in copies[:3]:
        copy.wait()
    lines = dest_v.shape[0]
    sent[:lines, :] = dest_v[...].astype(F32)
    sent[lines : 2 * lines, :] = base_v[...].astype(F32)
    for k in range(2):
        for i in range(lines):
            sent[(2 + k) * lines + i : (2 + k) * lines + i + 1, :] = frac_v[k : k + 1, i * LANES : (i + 1) * LANES]
    copies[3].wait()
    _, tile_rows, channels, _ = turned.shape
    lower = first_of_pair()
    for which, source in enumerate(order):
        for r in range(tile_rows):
            turned[which, r] = states_v[source, pl.ds(r, channels, stride=tile_rows), :]
        width = HALO - which
        for k in range(width):
            top, bottom = turned[which, k], turned[which, tile_rows - width + k]
            at = (first_row(which) + k) * channels
            sent[4 * lines + at : 4 * lines + at + channels, :] = jnp.where(lower, bottom, top)
            cross[at : at + channels, :] = jnp.where(lower, top, bottom)
    copies[4].wait()


def prepare(dest, base, frac, states, cot, order, tile_rows):
    channels, points = cot.shape
    columns = states.shape[2]
    stages = len(order)
    rim = first_row(stages) * channels
    lines = points // LANES
    in_hbm = pl.BlockSpec(memory_space=pltpu.HBM)
    return pl.pallas_call(
        functools.partial(prepare_kernel, order),
        in_specs=[in_hbm] * 5,
        out_shape=(
            jax.ShapeDtypeStruct((4 * lines + rim, LANES), F32),
            jax.ShapeDtypeStruct((rim, columns), F32),
            jax.ShapeDtypeStruct((stages, tile_rows, channels, columns), F32),
            jax.ShapeDtypeStruct(cot.shape, F32),
        ),
        scratch_shapes=[
            pltpu.VMEM(dest.shape, jnp.int32),
            pltpu.VMEM(base.shape, jnp.int32),
            pltpu.VMEM(frac.shape, F32),
            pltpu.VMEM(states.shape, F32),
            pltpu.SemaphoreType.DMA((5,)),
        ],
        compiler_params=PARAMS,
        name="prepare",
    )(*(pltpu.with_memory_space_constraint(x, pltpu.HBM) for x in (dest, base, frac, states, cot)))


def state_rows(which, turned, pair, pair_at, cross, lower, masks):
    _, tile_rows, channels, _ = turned.shape
    width = HALO - which

    def rim(ref, start):
        at = [start + (first_row(which) + k) * channels for k in range(width)]
        return [ref[i : i + channels, :] for i in at]

    tile = [turned[which, r] for r in range(tile_rows)]
    return extended_rows(tile, rim(pair, pair_at), rim(cross, 0), width, lower, masks)


def edge_plan(stages, tile_rows):
    plan, lane = [], 0
    for which in range(stages):
        width = HALO - which
        for k in range(HALO - width, HALO + tile_rows + width):
            count = width - max(HALO - k, k - (HALO + tile_rows - 1), 0)
            if count > 0:
                plan.append((which, k, count, lane))
                lane += count
    return plan


def state_edges(n_row, turned, pair, pair_at, cross):
    stages, tile_rows, channels, _ = turned.shape
    lower, masks = first_of_pair(), row_masks(n_row)
    lane = lax.broadcasted_iota(jnp.int32, (channels, LANES), 1)
    first = last = jnp.zeros((channels, LANES), F32)
    lines = [dict(state_rows(which, turned, pair, pair_at, cross, lower, masks)) for which in range(stages)]
    for which, k, count, at in edge_plan(stages, tile_rows):
        here = (lane >= at) & (lane < at + count)
        first = jnp.where(here, pltpu.roll(lines[which][k], at, 1), first)
        last = jnp.where(here, pltpu.roll(lines[which][k], (at + count) % LANES, 1), last)
    return first, last


def state_edges_kernel(n_row, pair_at, paired, turned, pair, cross, one, other):
    first, last = state_edges(n_row, turned, pair, pair_at, cross)
    if paired:
        lower = first_of_pair("fcol")
        first, last = jnp.where(lower, last, first), jnp.where(lower, first, last)
    one[...], other[...] = first, last


def all_state_edges(n_row, pair_at, paired, turned, pair, cross):
    return pl.pallas_call(
        functools.partial(state_edges_kernel, n_row, pair_at, paired),
        out_shape=[jax.ShapeDtypeStruct((turned.shape[2], LANES), F32)] * 2,
        compiler_params=PARAMS,
        name="state_edges",
    )(turned, pair, cross)


FIELDS = 7


def stage_weight(which):
    return 0.5 * time_step if which % 2 == 0 else time_step


def widen_kernel(n_row, pair_at, edge_at, paired, turned, pair, cross, one, other, gravity, *refs):
    wide, pull = refs[-2:]
    _, tile_rows, channels, columns = turned.shape
    levels = channels // 3
    total_rows = tile_rows * n_row
    base_row = lax.axis_index("frow") * tile_rows
    lower, masks = first_of_pair(), row_masks(n_row)

    level = lax.broadcasted_iota(jnp.int32, pull.shape, 0)
    pulls = jnp.zeros(pull.shape, F32)
    for i in range(levels):
        pulls = jnp.where(level == i, gravity[i], pulls)
    pull[...] = pulls

    def along_x(values):
        return pltpu.roll(values, 2 * columns - 1, 1) - pltpu.roll(values, 1, 1)

    left, right = from_sides(one[edge_at : edge_at + channels, :], other[...], paired)
    lane = lax.broadcasted_iota(jnp.int32, (channels, columns), 1)
    rims = {
        (which, k): jnp.where(
            lane < columns // 2,
            pltpu.roll(right, (-at) % columns, 1),
            pltpu.roll(left, (-at - count) % columns, 1),
        )
        for which, k, count, at in edge_plan(turned.shape[0], tile_rows)
    }

    for which in range(turned.shape[0]):
        weight = stage_weight(which)
        lines = state_rows(which, turned, pair, pair_at, cross, lower, masks)
        first, final = lines[0][0], lines[-1][0]
        for k, line in lines:
            rim = rims.get((which, k), jnp.zeros_like(line))
            scaled = (0.5 * weight) * jnp.concatenate([line, rim], axis=1)
            wide[which, k, :channels, :] = scaled
        for k in range(first + 1, final):
            winds = slice(levels, channels)
            change = along_x(wide[which, k, winds, :])
            slope = wide[which, k + 1, winds, :] - wide[which, k - 1, winds, :]
            row = (base_row + k - HALO).astype(F32)
            rotation = weight * (coriolis_peak * (2.0 * (row + 0.5) / total_rows - 1.0))
            begin = channels
            for value in (change[:levels], change[levels:] + rotation, slope[:levels] - rotation, slope[levels:]):
                wide[which, k, begin : begin + levels, :] = value
                begin += levels


def widen(n_row, pair_at, edge_at, paired, turned, pair, cross, one, other, gravity, after=()):
    stages, tile_rows, channels, columns = turned.shape
    in_vmem = pl.BlockSpec(memory_space=pltpu.VMEM)
    return pl.pallas_call(
        functools.partial(widen_kernel, n_row, pair_at, edge_at, paired),
        in_specs=[in_vmem] * 5 + [pl.BlockSpec(memory_space=pltpu.SMEM)] + [in_vmem] * len(after),
        out_shape=(
            jax.ShapeDtypeStruct((stages, tile_rows + 2 * HALO, channels // 3 * FIELDS, 2 * columns), F32),
            jax.ShapeDtypeStruct((channels // 3, 2 * columns), F32),
        ),
        compiler_params=PARAMS,
        name="widen_states",
    )(turned, pair, cross, one, other, gravity, *after)


def slot_blocks(cot, where, tiles, share, tile_rows, columns, onehot, high, low):
    channels, points = cot.shape
    lines = points // LANES
    groups = tiles.shape[0] // share
    corner = where[lines : 2 * lines, :]
    row = jnp.zeros_like(corner)
    for k in range(1, tile_rows - 1):
        row = row + (corner >= float(k * (columns - 1))).astype(F32)
    col = corner - row * float(columns - 1)
    target = where[:lines, :]
    offsets = [where[k * lines : (k + 1) * lines, :] for k in (2, 3)]

    before = (
        lax.broadcasted_iota(jnp.int32, (GROUP, GROUP), 0)
        < lax.broadcasted_iota(jnp.int32, (GROUP, GROUP), 1)
    ).astype(F32).astype(BF16)
    index = lax.broadcasted_iota(jnp.int32, tiles.shape, 0)
    begin = ((index % share) * (GROUP // share)).astype(F32)
    slots = lax.broadcasted_iota(jnp.int32, (GROUP, GROUP), 0).astype(F32)
    count = jnp.zeros((tiles.shape[0], 1), F32)
    rows = channels + 8
    for b in range(points // GROUP):
        part = slice(b * GROUP, (b + 1) * GROUP)

        def across(values):
            return jnp.concatenate([values[2 * b : 2 * b + 1, :], values[2 * b + 1 : 2 * b + 2, :]], axis=1)

        named = (tiles == across(target)).astype(F32)
        ahead = jnp.dot(named.astype(BF16), before, preferred_element_type=F32)
        lane = jnp.sum(named * (ahead + count + begin), axis=0, keepdims=True)
        count = count + jnp.sum(named, axis=1, keepdims=True)
        onehot[:, part] = (slots == lane).astype(F32).astype(BF16)
        coords = [across(values) for values in (row, col, *offsets)]
        data_high, data_low = split(jnp.concatenate([cot[:, part], *coords, *coords], axis=0))
        for g in range(groups):
            mine = named[g * share : g * share + 1, :]
            for i in range(1, share):
                mine = mine + named[g * share + i : g * share + i + 1, :]
            mine = mine.astype(BF16)
            high[g * rows : (g + 1) * rows, part] = data_high * mine
            low[g * rows : (g + 1) * rows, part] = data_low * mine
    packed = dot_nt(high[...], onehot[...]) + dot_nt(low[...], onehot[...])
    upper = lax.broadcasted_iota(jnp.int32, (8, LANES), 0) < 4
    for g in range(groups):
        block = packed[g * rows : (g + 1) * rows, :]
        yield (
            block[:channels, :LANES],
            block[:channels, LANES:],
            jnp.where(upper, block[channels:, :LANES], block[channels:, LANES:]),
        )


def store_block(out, at, pieces):
    channels = pieces[0].shape[0]
    out[at : at + channels, :] = pieces[0]
    out[at + channels : at + 2 * channels, :] = pieces[1]
    out[at + 2 * channels : at + 2 * channels + 8, :] = pieces[2]


def pack_scratch(channels, points, groups):
    return [
        pltpu.VMEM((GROUP, points), BF16),
        pltpu.VMEM((groups * (channels + 8), points), BF16),
        pltpu.VMEM((groups * (channels + 8), points), BF16),
    ]


def pack_all_kernel(tile_count, share, tile_rows, columns, cot, where, out, *scratch):
    tiles = lax.broadcasted_iota(jnp.int32, (tile_count, GROUP), 0).astype(F32)
    for g, pieces in enumerate(slot_blocks(cot, where, tiles, share, tile_rows, columns, *scratch)):
        store_block(out.at[g], 0, pieces)


def pack_all(cot, where, tile_count, share, tile_rows, columns):
    channels, points = cot.shape
    groups = tile_count // share
    return pl.pallas_call(
        functools.partial(pack_all_kernel, tile_count, share, tile_rows, columns),
        out_shape=jax.ShapeDtypeStruct((groups, 2 * channels + 8, LANES), F32),
        scratch_shapes=pack_scratch(channels, points, groups),
        compiler_params=PARAMS,
        name="pack_points",
    )(cot, where)


NEAR = ((0, 0), (2, 0), (0, 1), (2, 1))
FAR = ((0, 2), (2, 2), (0, 3), (2, 3))


def partner_tiles(partners):
    at_row, at_col = lax.axis_index("frow"), lax.axis_index("fcol")
    n_col = lax.axis_size("fcol")
    index = lax.broadcasted_iota(jnp.int32, (len(partners), GROUP), 0)
    tiles = jnp.zeros(index.shape, jnp.int32)
    for g, (df, dz) in enumerate(partners):
        tiles = jnp.where(index == g, (at_row ^ df) * n_col + (at_col ^ dz), tiles)
    return tiles.astype(F32)


def pack_own_kernel(tiles, tile_rows, columns, cot, where, out, *scratch):
    for g, pieces in enumerate(slot_blocks(cot, where, partner_tiles(tiles), 1, tile_rows, columns, *scratch)):
        store_block(out.at[g], 0, pieces)


def pack_own(tiles, cot, where, tile_rows, columns):
    channels, points = cot.shape
    groups = len(tiles)
    return pl.pallas_call(
        functools.partial(pack_own_kernel, tiles, tile_rows, columns),
        out_shape=jax.ShapeDtypeStruct((groups, 2 * channels + 8, LANES), F32),
        scratch_shapes=pack_scratch(channels, points, groups),
        compiler_params=PARAMS,
        name="pack_own",
    )(cot, where)


def pack_partner_kernel(tiles, tailed, tile_rows, columns, cot, where, own, *refs):
    if tailed is not None:
        tail, *refs = refs
    outs, scratch = refs[:-3], refs[-3:]
    size = own.shape[1]
    blocks = slot_blocks(cot, where, partner_tiles(tiles), 1, tile_rows, columns, *scratch)
    for g, pieces in enumerate(blocks):
        outs[g][:size, :] = own[g]
        store_block(outs[g], size, pieces)
        if tiles[g] == tailed:
            outs[g][2 * size :, :] = tail[...]


def pack_partner(tiles, cot, where, own, tile_rows, columns, tailed=None, tail=None):
    channels, points = cot.shape
    rows = 2 * own.shape[1]
    sizes = [rows + (tail.shape[0] if tile == tailed else 0) for tile in tiles]
    blocks = pl.pallas_call(
        functools.partial(pack_partner_kernel, tiles, tailed, tile_rows, columns),
        out_shape=[jax.ShapeDtypeStruct((size, LANES), F32) for size in sizes],
        scratch_shapes=pack_scratch(channels, points, len(tiles)),
        compiler_params=PARAMS,
        name="pack_partner",
    )(cot, where, own, *([] if tail is None else [tail]))
    return dict(zip(tiles, blocks))


def scatter_kernel(count, first, later, *refs):
    blocks, refs = refs[:count], refs[count:]
    if not first:
        total, refs = refs[0], refs[1:]
    outs, (high, low, weight) = refs[later:-3], refs[-3:]
    part_rows, channels, columns = outs[0].shape
    tile_rows = part_rows * len(outs)
    rows = 2 * channels + 8
    cells = lax.broadcasted_iota(jnp.int32, (columns, LANES), 0).astype(F32)
    lines = lax.broadcasted_iota(jnp.int32, (tile_rows, LANES), 0).astype(F32)

    def hat(index, corner, fraction):
        away = index - corner
        return jnp.where(away == 0.0, 1.0 - fraction, jnp.where(away == 1.0, fraction, 0.0))

    at = 0
    for block in blocks:
        for source in range(block.shape[0] // rows):
            for half in range(2):
                part = slice(at, at + LANES)
                at += LANES
                begin = source * rows + 2 * channels + 4 * half
                coords = block[begin : begin + 4, :]
                row, col, along_rows, along_cols = (coords[k : k + 1, :] for k in range(4))
                weight_high, weight_low = split(hat(cells, col, along_cols))
                weight[:columns, part] = weight_high
                weight[columns:, part] = weight_low
                begin = source * rows + half * channels
                values = block[begin : begin + channels, :]
                row_weight = hat(lines, row, along_rows)
                for r in range(tile_rows):
                    product_high, product_low = split(values * row_weight[r : r + 1, :])
                    high[r * channels : (r + 1) * channels, part] = product_high
                    low[r * channels : (r + 1) * channels, part] = product_low
    both = dot_nt(high[...], weight[...])
    sums = both[:, :columns] + both[:, columns:] + dot_nt(low[...], weight[:columns, :])
    for r in range(tile_rows):
        line = sums[r * channels : (r + 1) * channels, :]
        if not first:
            line = line + total[r]
        outs[r // part_rows][r % part_rows] = line


def scatter(blocks, total, channels, tile_rows, columns, after=(), parts=1):
    slots = sum(block.shape[0] // (2 * channels + 8) for block in blocks) * GROUP
    return pl.pallas_call(
        functools.partial(scatter_kernel, len(blocks), total is None, len(after)),
        out_shape=[jax.ShapeDtypeStruct((tile_rows // parts, channels, columns), F32)] * parts,
        scratch_shapes=[
            pltpu.VMEM((tile_rows * channels, slots), BF16),
            pltpu.VMEM((tile_rows * channels, slots), BF16),
            pltpu.VMEM((2 * columns, slots), BF16),
        ],
        compiler_params=PARAMS,
        name="scatter_points",
    )(*blocks, *([] if total is None else [total]), *after)


def finish_kernel(count, total, *refs):
    parts, (canvas, to_pair, to_cross) = refs[:count], refs[-3:]
    tile_rows = canvas.shape[0]
    for r in range(tile_rows):
        line = total[r]
        if parts:
            size = parts[0].shape[0]
            line = line + parts[r // size][r % size]
        canvas[r] = line
    lower = first_of_pair()
    for k in range(HALO):
        top, bottom = canvas[k], canvas[tile_rows - HALO + k]
        to_pair[k] = jnp.where(lower, bottom, top)
        to_cross[k] = jnp.where(lower, top, bottom)


def finish(total, parts=(), after=()):
    _, channels, columns = total.shape
    rim = jax.ShapeDtypeStruct((HALO, channels, columns), F32)
    return pl.pallas_call(
        functools.partial(finish_kernel, len(parts)),
        out_shape=(jax.ShapeDtypeStruct(total.shape, F32), rim, rim),
        compiler_params=PARAMS,
        name="finish_canvas",
    )(total, *parts, *after)


def adjoint_rows(n_row, canvas, pair, cross):
    tile = [canvas[r] for r in range(canvas.shape[0])]
    rims = ([ref[k] for k in range(HALO)] for ref in (pair, cross))
    return extended_rows(tile, *rims, HALO, first_of_pair(), row_masks(n_row))


def adjoint_edges_kernel(n_row, canvas, pair, cross, edges):
    edges[...] = edge_columns(adjoint_rows(n_row, canvas, pair, cross))


def adjoint_edges(n_row, canvas, pair, cross):
    return pl.pallas_call(
        functools.partial(adjoint_edges_kernel, n_row),
        out_shape=jax.ShapeDtypeStruct(canvas.shape[1:], F32),
        compiler_params=PARAMS,
        name="adjoint_edges",
    )(canvas, pair, cross)


def steps_kernel(n_row, paired, canvas, pair, cross, one, other, gravity, wide, out, start, middle, after, last):
    tile_rows, channels, columns = canvas.shape
    levels = channels // 3
    part = 8
    masks = row_masks(n_row)
    left, right = from_sides(one[...], other[...], paired)
    rim = jnp.where(first_lanes(left), right, left)
    for k, line in adjoint_rows(n_row, canvas, pair, cross):
        start[k, :, :columns] = line
        start[k, :, columns:] = pltpu.roll(rim, (-8 * k) % LANES, 1)

    def along_x(values):
        return pltpu.roll(values, 2 * columns - 1, 1) - pltpu.roll(values, 1, 1)

    def run(stage, adjoint, store):
        width = HALO - 1 - stage
        begin, end = HALO - width, HALO + tile_rows + width
        for low in range(0, levels, part):
            pull = (0.5 * stage_weight(stage)) * gravity[low : low + part, :]

            def state(k, which):
                return wide[stage, k, which * levels + low : which * levels + low + part, :]

            def line(k):
                a, b, c = (adjoint[k, w * levels + low : w * levels + low + part, :] for w in range(3))
                v = state(k, 2)
                return a, b, c, v, v * b, v * c

            up, here = line(begin - 1), line(begin)
            for k in range(begin, end):
                down = line(k + 1)
                a, b, c, v = here[:4]
                h, u = state(k, 0), state(k, 1)
                a_x, a_y = along_x(a), down[0] - up[0]
                height = u * a_x + v * a_y + pull * (along_x(b) + (down[2] - up[2]))
                east = h * a_x + along_x(u * b) + (down[4] - up[4]) - b * state(k, 3) - c * state(k, 4)
                north = h * a_y + along_x(u * c) + (down[5] - up[5]) - b * state(k, 5) - c * state(k, 6)
                for w, (old, change) in enumerate(zip((a, b, c), (height, east, north))):
                    store(k, w, low, old, change)
                up, here = here, down

    def kept(k, value):
        if k < HALO:
            return value * masks[0]
        if k >= HALO + tile_rows:
            return value * masks[1]
        return value

    def half_into(result):
        def store(k, w, low, old, change):
            result[k, w * levels + low : w * levels + low + part, :] = kept(k, 0.5 * old + change)

        return store

    def after_step(adjoint, k, w, low, old, change):
        return 0.5 * adjoint[k, w * levels + low : w * levels + low + part, :] + old + change

    def to_after(k, w, low, old, change):
        after[k, w * levels + low : w * levels + low + part, :] = kept(k, after_step(start, k, w, low, old, change))

    def to_out(k, w, low, old, change):
        place = pl.ds((w * levels + low) * tile_rows + k - HALO, part, stride=tile_rows)
        out[place, :] = after_step(after, k, w, low, old, change)[:, :columns]

    run(0, start, half_into(middle))
    run(1, middle, to_after)
    run(2, after, half_into(last))
    run(3, last, to_out)


def steps(n_row, paired, canvas, pair, cross, one, other, wide, gravity):
    tile_rows, channels, columns = canvas.shape
    extended = pltpu.VMEM((tile_rows + 2 * HALO, channels, 2 * columns), F32)
    return pl.pallas_call(
        functools.partial(steps_kernel, n_row, paired),
        out_shape=jax.ShapeDtypeStruct((channels * tile_rows, columns), F32),
        scratch_shapes=[extended] * 4,
        compiler_params=PARAMS,
        name="adjoint_steps",
    )(canvas, pair, cross, one, other, gravity, wide)


def shifted(values, axis, by):
    count = lax.axis_size(axis)
    return lax.ppermute(values, axis, [(i, (i + by) % count) for i in range(count)])


def exchanged(values, offset):
    n_row, n_col = lax.axis_size("frow"), lax.axis_size("fcol")
    df, dz = offset
    pairs = [(f * n_col + z, (f ^ df) * n_col + (z ^ dz)) for f in range(n_row) for z in range(n_col)]
    return lax.ppermute(values, ("frow", "fcol"), pairs)


def exchanged_across(values):
    n_row = lax.axis_size("frow")
    return lax.ppermute(values, "frow", [(f, ((f + 1) ^ 1) - 1) for f in range(1, n_row - 1)])


def from_everyone(packed, channels, tile_count):
    groups = packed.shape[0]
    rows = channels + 4
    halves = [
        jnp.concatenate(
            [
                packed[:, h * channels : (h + 1) * channels],
                packed[:, 2 * channels + 4 * h : 2 * channels + 4 * h + 4],
            ],
            axis=1,
        )
        for h in range(2)
    ]
    slots = jnp.stack(halves, axis=2).transpose(1, 0, 2, 3).reshape(rows, tile_count, -1)
    slots = lax.all_to_all(slots, ("frow", "fcol"), split_axis=1, concat_axis=1, tiled=True)
    slots = slots.reshape(rows, groups, 2, LANES).transpose(1, 2, 0, 3)
    return jnp.concatenate(
        [slots[:, 0, :channels], slots[:, 1, :channels], slots[:, 0, channels:], slots[:, 1, channels:]], axis=1
    )


def per_device(latlon_cot, dest_tile, base_cell, corner_frac, saved_states, gravity):
    n_row, n_col = lax.axis_size("frow"), lax.axis_size("fcol")
    tile_count = n_row * n_col
    levels = gravity.shape[0]
    tile_rows = saved_states.shape[4]
    columns = saved_states.shape[5]
    channels = 3 * levels
    points = base_cell.shape[0]
    lines = points // LANES
    share = GROUP * tile_count // (2 * points)
    paired = share == 1 and n_row == 4 and n_col == 4
    size = (channels, tile_rows, columns)

    cot = latlon_cot.reshape(channels, points)
    partner_cot = exchanged(cot, (1, 0)) if paired else None
    sent, to_cross, turned, cot = prepare(
        dest_tile.reshape(lines, LANES),
        base_cell.reshape(lines, LANES),
        corner_frac,
        saved_states.reshape(4, channels * tile_rows, columns),
        cot,
        (3, 2, 1, 0),
        tile_rows,
    )
    pair_at = 4 * lines
    pair = exchanged(sent, (1, 0))
    cross = exchanged_across(to_cross)
    if paired:
        own = pack_own(FAR, cot, sent, tile_rows, columns)
        packed = pack_partner(FAR, partner_cot, pair, own, tile_rows, columns)
        got = [packed[0, 2]] + [exchanged(packed[tile], (tile[0], tile[1] ^ 2)) for tile in FAR[1:]]
        one, other = all_state_edges(n_row, pair_at, paired, turned, pair, cross)
        own = pack_own(NEAR, cot, sent, tile_rows, columns)
        packed = pack_partner(NEAR, partner_cot, pair, own, tile_rows, columns, (0, 1), one)
        total = scatter(got[:2], None, *size, [packed[0, 0]])[0]
        far = [exchanged(part, (0, 2)) for part in scatter(got[2:], total, *size, parts=2)]
        got = {tile: exchanged(packed[tile], tile) for tile in NEAR[1:]}
        other = exchanged(other, (0, 3))
        total = scatter([packed[0, 0], got[2, 0]], None, *size)[0]
        total = scatter([got[0, 1], got[2, 1]], total, *size)[0]
        wide, pull = widen(
            n_row, pair_at, 2 * own.shape[1], paired, turned, pair, cross, got[0, 1], other, gravity, [total]
        )
        canvas = finish(total, far, [pull])
    else:
        packed = pack_all(cot, sent, tile_count, share, tile_rows, columns)
        got = from_everyone(packed, channels, tile_count)
        one, other = all_state_edges(n_row, pair_at, paired, turned, pair, cross)
        one, other = shifted(one, "fcol", 1), shifted(other, "fcol", -1)
        wide, pull = widen(n_row, pair_at, 0, paired, turned, pair, cross, one, other, gravity)
        canvas = finish(scatter([got.reshape(-1, LANES)], None, *size)[0])

    canvas, to_pair, to_cross = canvas
    pair, cross = exchanged(to_pair, (1, 0)), exchanged_across(to_cross)
    edges = adjoint_edges(n_row, canvas, pair, cross)
    if paired:
        sides = exchanged(edges, (0, 1)), exchanged(edges, (0, 3))
    else:
        sides = shifted(edges, "fcol", 1), shifted(edges, "fcol", -1)
    result = steps(n_row, paired, canvas, pair, cross, *sides, wide, pull)
    return result.reshape(3, levels, tile_rows, columns)


def solution(mesh):
    placed = (
        P(None, None, ("member", "frow", "fcol")),
        P(("frow", "fcol"), None),
        P(("frow", "fcol")),
        P(None, ("frow", "fcol")),
        P(None, None, None, None, ("member", "frow"), "fcol"),
        P(),
    )
    return jax.shard_map(
        per_device,
        mesh=mesh,
        in_specs=placed,
        out_specs=P(None, None, ("member", "frow"), "fcol"),
        check_vma=False,
    )
```

```python
import functools

import jax
import jax.numpy as jnp
from jax import lax
from jax.experimental import pallas as pl
from jax.experimental.pallas import tpu as pltpu
from jax.sharding import PartitionSpec as P

time_step = 0.25
coriolis_peak = 0.8

HALO = 4
GROUP = 256
LANES = 128
F32 = jnp.float32
BF16 = jnp.bfloat16
PARAMS = pltpu.CompilerParams(vmem_limit_bytes=16 * 1024 * 1024)


def split(values):
    high = values.astype(BF16)
    return high, (values - high.astype(F32)).astype(BF16)


def dot_nt(a, b):
    return lax.dot_general(a, b, (((1,), (1,)), ((), ())), preferred_element_type=F32)


def first_of_pair(axis="frow"):
    return lax.rem(lax.axis_index(axis), 2) == 0


def row_masks(n_row):
    at = lax.axis_index("frow")
    return jnp.where(at > 0, 1.0, 0.0).astype(F32), jnp.where(at < n_row - 1, 1.0, 0.0).astype(F32)


def extended_rows(tile, pair, cross, width, lower, masks):
    tile_rows = len(tile)
    lines = [(HALO - width + k, jnp.where(lower, cross[k], pair[k]) * masks[0]) for k in range(width)]
    lines += [(HALO + k, tile[k]) for k in range(tile_rows)]
    lines += [(HALO + tile_rows + k, jnp.where(lower, pair[k], cross[k]) * masks[1]) for k in range(width)]
    return lines


def edge_columns(lines, result):
    lane = lax.broadcasted_iota(jnp.int32, result.shape, 1)
    owner = ((lane + 4) // 8) % 16
    for k, line in lines:
        result = jnp.where(owner == k, pltpu.roll(line, (8 * k) % LANES, 1), result)
    return result


def first_lanes(like):
    return lax.broadcasted_iota(jnp.int32, like.shape, 1) % 8 < 4


def from_sides(one, other, paired):
    if not paired:
        return one, other
    lower = first_of_pair("fcol")
    return jnp.where(lower, other, one), jnp.where(lower, one, other)


def first_row(which):
    return sum(HALO - k for k in range(which))


def prepare_kernel(order, dest, base, frac, states, cot, sent, cross, turned, cot_out, dest_v, base_v, frac_v, states_v, sems):
    moves = ((dest, dest_v), (base, base_v), (frac, frac_v), (states, states_v), (cot, cot_out))
    copies = [pltpu.make_async_copy(source, target, sems.at[i]) for i, (source, target) in enumerate(moves)]
    for copy in copies:
        copy.start()
    for copy in copies[:3]:
        copy.wait()
    lines = dest_v.shape[0]
    sent[:lines, :] = dest_v[...].astype(F32)
    sent[lines : 2 * lines, :] = base_v[...].astype(F32)
    for k in range(2):
        for i in range(lines):
            sent[(2 + k) * lines + i : (2 + k) * lines + i + 1, :] = frac_v[k : k + 1, i * LANES : (i + 1) * LANES]
    copies[3].wait()
    _, tile_rows, channels, _ = turned.shape
    lower = first_of_pair()
    for which, source in enumerate(order):
        for r in range(tile_rows):
            turned[which, r] = states_v[source, pl.ds(r, channels, stride=tile_rows), :]
        width = HALO - which
        for k in range(width):
            top, bottom = turned[which, k], turned[which, tile_rows - width + k]
            at = (first_row(which) + k) * channels
            sent[4 * lines + at : 4 * lines + at + channels, :] = jnp.where(lower, bottom, top)
            cross[at : at + channels, :] = jnp.where(lower, top, bottom)
    copies[4].wait()


def prepare(dest, base, frac, states, cot, order, tile_rows):
    channels, points = cot.shape
    columns = states.shape[2]
    stages = len(order)
    rim = first_row(stages) * channels
    lines = points // LANES
    in_hbm = pl.BlockSpec(memory_space=pltpu.HBM)
    return pl.pallas_call(
        functools.partial(prepare_kernel, order),
        in_specs=[in_hbm] * 5,
        out_shape=(
            jax.ShapeDtypeStruct((4 * lines + rim, LANES), F32),
            jax.ShapeDtypeStruct((rim, columns), F32),
            jax.ShapeDtypeStruct((stages, tile_rows, channels, columns), F32),
            jax.ShapeDtypeStruct(cot.shape, F32),
        ),
        scratch_shapes=[
            pltpu.VMEM(dest.shape, jnp.int32),
            pltpu.VMEM(base.shape, jnp.int32),
            pltpu.VMEM(frac.shape, F32),
            pltpu.VMEM(states.shape, F32),
            pltpu.SemaphoreType.DMA((5,)),
        ],
        compiler_params=PARAMS,
        name="prepare",
    )(*(pltpu.with_memory_space_constraint(x, pltpu.HBM) for x in (dest, base, frac, states, cot)))


def state_rows(which, turned, pair, pair_at, cross, lower, masks):
    _, tile_rows, channels, _ = turned.shape
    width = HALO - which

    def rim(ref, start):
        at = [start + (first_row(which) + k) * channels for k in range(width)]
        return [ref[i : i + channels, :] for i in at]

    tile = [turned[which, r] for r in range(tile_rows)]
    return extended_rows(tile, rim(pair, pair_at), rim(cross, 0), width, lower, masks)


def edge_plan(stages, tile_rows):
    plan, lane = [], 0
    for which in range(stages):
        width = HALO - which
        for k in range(HALO - width, HALO + tile_rows + width):
            count = width - max(HALO - k, k - (HALO + tile_rows - 1), 0)
            if count > 0:
                plan.append((which, k, count, lane))
                lane += count
    return plan


def state_edges(n_row, turned, pair, pair_at, cross):
    stages, tile_rows, channels, _ = turned.shape
    lower, masks = first_of_pair(), row_masks(n_row)
    lane = lax.broadcasted_iota(jnp.int32, (channels, LANES), 1)
    first = last = jnp.zeros((channels, LANES), F32)
    lines = [dict(state_rows(which, turned, pair, pair_at, cross, lower, masks)) for which in range(stages)]
    for which, k, count, at in edge_plan(stages, tile_rows):
        here = (lane >= at) & (lane < at + count)
        first = jnp.where(here, pltpu.roll(lines[which][k], at, 1), first)
        last = jnp.where(here, pltpu.roll(lines[which][k], (at + count) % LANES, 1), last)
    return first, last


def state_edges_kernel(n_row, pair_at, paired, turned, pair, cross, *refs):
    one, other = refs[-2:]
    first, last = state_edges(n_row, turned, pair, pair_at, cross)
    if paired:
        lower = first_of_pair("fcol")
        first, last = jnp.where(lower, last, first), jnp.where(lower, first, last)
    one[...], other[...] = first, last


def all_state_edges(n_row, pair_at, paired, turned, pair, cross, after=()):
    return pl.pallas_call(
        functools.partial(state_edges_kernel, n_row, pair_at, paired),
        out_shape=[jax.ShapeDtypeStruct((turned.shape[2], LANES), F32)] * 2,
        compiler_params=PARAMS,
        name="state_edges",
    )(turned, pair, cross, *after)


FIELDS = 7


def stage_weight(which):
    return 0.5 * time_step if which % 2 == 0 else time_step


def widen_kernel(n_row, pair_at, paired, turned, pair, cross, one, other, gravity, *refs):
    wide, pull = refs[-2:]
    _, tile_rows, channels, columns = turned.shape
    levels = channels // 3
    total_rows = tile_rows * n_row
    base_row = lax.axis_index("frow") * tile_rows
    lower, masks = first_of_pair(), row_masks(n_row)

    level = lax.broadcasted_iota(jnp.int32, pull.shape, 0)
    pulls = jnp.zeros(pull.shape, F32)
    for i in range(levels):
        pulls = jnp.where(level == i, gravity[i], pulls)
    pull[...] = pulls

    def along_x(values):
        return pltpu.roll(values, 2 * columns - 1, 1) - pltpu.roll(values, 1, 1)

    left, right = from_sides(one[...], other[...], paired)
    lane = lax.broadcasted_iota(jnp.int32, (channels, columns), 1)
    rims = {
        (which, k): jnp.where(
            lane < columns // 2,
            pltpu.roll(right, (-at) % columns, 1),
            pltpu.roll(left, (-at - count) % columns, 1),
        )
        for which, k, count, at in edge_plan(turned.shape[0], tile_rows)
    }

    for which in range(turned.shape[0]):
        weight = stage_weight(which)
        lines = state_rows(which, turned, pair, pair_at, cross, lower, masks)
        first, final = lines[0][0], lines[-1][0]
        for k, line in lines:
            rim = rims.get((which, k), jnp.zeros_like(line))
            scaled = (0.5 * weight) * jnp.concatenate([line, rim], axis=1)
            wide[which, k, :channels, :] = scaled
        for k in range(first + 1, final):
            winds = slice(levels, channels)
            change = along_x(wide[which, k, winds, :])
            slope = wide[which, k + 1, winds, :] - wide[which, k - 1, winds, :]
            row = (base_row + k - HALO).astype(F32)
            rotation = weight * (coriolis_peak * (2.0 * (row + 0.5) / total_rows - 1.0))
            begin = channels
            for value in (change[:levels], change[levels:] + rotation, slope[:levels] - rotation, slope[levels:]):
                wide[which, k, begin : begin + levels, :] = value
                begin += levels


def widen(n_row, pair_at, paired, turned, pair, cross, one, other, gravity, after=()):
    stages, tile_rows, channels, columns = turned.shape
    in_vmem = pl.BlockSpec(memory_space=pltpu.VMEM)
    return pl.pallas_call(
        functools.partial(widen_kernel, n_row, pair_at, paired),
        in_specs=[in_vmem] * 5 + [pl.BlockSpec(memory_space=pltpu.SMEM)] + [in_vmem] * len(after),
        out_shape=(
            jax.ShapeDtypeStruct((stages, tile_rows + 2 * HALO, channels // 3 * FIELDS, 2 * columns), F32),
            jax.ShapeDtypeStruct((channels // 3, 2 * columns), F32),
        ),
        compiler_params=PARAMS,
        name="widen_states",
    )(turned, pair, cross, one, other, gravity, *after)


def slot_blocks(cot, where, tiles, share, tile_rows, columns, onehot, parts):
    channels, points = cot.shape
    lines = points // LANES
    groups = tiles.shape[0] // share
    corner = where[lines : 2 * lines, :]
    row = jnp.zeros_like(corner)
    for k in range(1, tile_rows - 1):
        row = row + (corner >= float(k * (columns - 1))).astype(F32)
    col = corner - row * float(columns - 1)
    target = where[:lines, :]
    offsets = [where[k * lines : (k + 1) * lines, :] for k in (2, 3)]

    before = (
        lax.broadcasted_iota(jnp.int32, (GROUP, GROUP), 0)
        < lax.broadcasted_iota(jnp.int32, (GROUP, GROUP), 1)
    ).astype(F32).astype(BF16)
    index = lax.broadcasted_iota(jnp.int32, tiles.shape, 0)
    begin = ((index % share) * (GROUP // share)).astype(F32)
    slots = lax.broadcasted_iota(jnp.int32, (GROUP, GROUP), 0).astype(F32)
    count = jnp.zeros((tiles.shape[0], 1), F32)
    rows = channels + 8
    for b in range(points // GROUP):
        part = slice(b * GROUP, (b + 1) * GROUP)

        def across(values):
            return jnp.concatenate([values[2 * b : 2 * b + 1, :], values[2 * b + 1 : 2 * b + 2, :]], axis=1)

        named = (tiles == across(target)).astype(F32)
        ahead = jnp.dot(named.astype(BF16), before, preferred_element_type=F32)
        lane = jnp.sum(named * (ahead + count + begin), axis=0, keepdims=True)
        count = count + jnp.sum(named, axis=1, keepdims=True)
        onehot[:, part] = (slots == lane).astype(F32).astype(BF16)
        coords = [across(values) for values in (row, col, *offsets)]
        data_high, data_low = split(jnp.concatenate([cot[:, part], *coords, *coords], axis=0))
        for g in range(groups):
            mine = named[g * share : g * share + 1, :]
            for i in range(1, share):
                mine = mine + named[g * share + i : g * share + i + 1, :]
            mine = mine.astype(BF16)
            parts[g * rows : (g + 1) * rows, part] = data_high * mine
            parts[(groups + g) * rows : (groups + g + 1) * rows, part] = data_low * mine
    both = dot_nt(parts[...], onehot[...])
    packed = both[: groups * rows, :] + both[groups * rows :, :]
    upper = lax.broadcasted_iota(jnp.int32, (8, LANES), 0) < 4
    for g in range(groups):
        block = packed[g * rows : (g + 1) * rows, :]
        yield (
            block[:channels, :LANES],
            block[:channels, LANES:],
            jnp.where(upper, block[channels:, :LANES], block[channels:, LANES:]),
        )


def store_block(out, at, pieces):
    channels = pieces[0].shape[0]
    out[at : at + channels, :] = pieces[0]
    out[at + channels : at + 2 * channels, :] = pieces[1]
    out[at + 2 * channels : at + 2 * channels + 8, :] = pieces[2]


def pack_scratch(channels, points, groups):
    return [
        pltpu.VMEM((GROUP, points), BF16),
        pltpu.VMEM((2 * groups * (channels + 8), points), BF16),
    ]


def pack_all_kernel(tile_count, share, tile_rows, columns, cot, where, out, *scratch):
    tiles = lax.broadcasted_iota(jnp.int32, (tile_count, GROUP), 0).astype(F32)
    for g, pieces in enumerate(slot_blocks(cot, where, tiles, share, tile_rows, columns, *scratch)):
        store_block(out.at[g], 0, pieces)


def pack_all(cot, where, tile_count, share, tile_rows, columns):
    channels, points = cot.shape
    groups = tile_count // share
    return pl.pallas_call(
        functools.partial(pack_all_kernel, tile_count, share, tile_rows, columns),
        out_shape=jax.ShapeDtypeStruct((groups, 2 * channels + 8, LANES), F32),
        scratch_shapes=pack_scratch(channels, points, groups),
        compiler_params=PARAMS,
        name="pack_points",
    )(cot, where)


NEAR = ((0, 0), (2, 0), (0, 1), (2, 1))
FAR = ((0, 2), (2, 2), (0, 3), (2, 3))


def partner_tiles(partners):
    at_row, at_col = lax.axis_index("frow"), lax.axis_index("fcol")
    n_col = lax.axis_size("fcol")
    index = lax.broadcasted_iota(jnp.int32, (len(partners), GROUP), 0)
    tiles = jnp.zeros(index.shape, jnp.int32)
    for g, (df, dz) in enumerate(partners):
        tiles = jnp.where(index == g, (at_row ^ df) * n_col + (at_col ^ dz), tiles)
    return tiles.astype(F32)


def pack_chip_kernel(tiles, tile_rows, columns, cot, where, pair_cot, pair_where, *refs):
    outs, scratch = refs[-4 - len(tiles) : -4], refs[-4:]
    begin = 0
    for i, points in enumerate(((cot, where), (pair_cot, pair_where))):
        blocks = slot_blocks(*points, partner_tiles(tiles), 1, tile_rows, columns, *scratch[2 * i : 2 * i + 2])
        for out, pieces in zip(outs, blocks):
            store_block(out, begin, pieces)
        begin += 2 * cot.shape[0] + 8


def pack_chip(tiles, points, tile_rows, columns, after=()):
    channels, count = points[0].shape
    return pl.pallas_call(
        functools.partial(pack_chip_kernel, tiles, tile_rows, columns),
        out_shape=[jax.ShapeDtypeStruct((2 * (2 * channels + 8), LANES), F32)] * len(tiles),
        scratch_shapes=pack_scratch(channels, count, len(tiles)) * 2,
        compiler_params=PARAMS,
        name="pack_chip",
    )(*points, *after)


def scatter_kernel(count, first, later, *refs):
    blocks, refs = refs[:count], refs[count:]
    if not first:
        total, refs = refs[0], refs[1:]
    outs, (parts, weight) = refs[later:-2], refs[-2:]
    part_rows, channels, columns = outs[0].shape
    tile_rows = part_rows * len(outs)
    rows = 2 * channels + 8
    cells = lax.broadcasted_iota(jnp.int32, (columns, LANES), 0).astype(F32)
    lines = lax.broadcasted_iota(jnp.int32, (tile_rows, LANES), 0).astype(F32)

    def hat(index, corner, fraction):
        away = index - corner
        return jnp.where(away == 0.0, 1.0 - fraction, jnp.where(away == 1.0, fraction, 0.0))

    at = 0
    for block in blocks:
        for source in range(block.shape[0] // rows):
            for half in range(2):
                part = slice(at, at + LANES)
                at += LANES
                begin = source * rows + 2 * channels + 4 * half
                coords = block[begin : begin + 4, :]
                row, col, along_rows, along_cols = (coords[k : k + 1, :] for k in range(4))
                weight_high, weight_low = split(hat(cells, col, along_cols))
                weight[:columns, part] = weight_high
                weight[columns:, part] = weight_low
                begin = source * rows + half * channels
                values = block[begin : begin + channels, :]
                row_weight = hat(lines, row, along_rows)
                for r in range(tile_rows):
                    product_high, product_low = split(values * row_weight[r : r + 1, :])
                    parts[r * channels : (r + 1) * channels, part] = product_high
                    parts[(tile_rows + r) * channels : (tile_rows + r + 1) * channels, part] = product_low
    both = dot_nt(parts[...], weight[...])
    sums = both[:, :columns] + both[:, columns:]
    sums = sums[: tile_rows * channels, :] + sums[tile_rows * channels :, :]
    for r in range(tile_rows):
        line = sums[r * channels : (r + 1) * channels, :]
        if not first:
            line = line + total[r]
        outs[r // part_rows][r % part_rows] = line


def scatter(blocks, total, channels, tile_rows, columns, after=(), parts=1):
    slots = sum(block.shape[0] // (2 * channels + 8) for block in blocks) * GROUP
    return pl.pallas_call(
        functools.partial(scatter_kernel, len(blocks), total is None, len(after)),
        out_shape=[jax.ShapeDtypeStruct((tile_rows // parts, channels, columns), F32)] * parts,
        scratch_shapes=[
            pltpu.VMEM((2 * tile_rows * channels, slots), BF16),
            pltpu.VMEM((2 * columns, slots), BF16),
        ],
        compiler_params=PARAMS,
        name="scatter_points",
    )(*blocks, *([] if total is None else [total]), *after)


def finish_kernel(count, total, *refs):
    parts, (canvas, to_pair, to_cross) = refs[:count], refs[-3:]
    tile_rows = canvas.shape[0]
    for r in range(tile_rows):
        line = total[r]
        if parts:
            size = parts[0].shape[0]
            line = line + parts[r // size][r % size]
        canvas[r] = line
    lower = first_of_pair()
    for k in range(HALO):
        top, bottom = canvas[k], canvas[tile_rows - HALO + k]
        to_pair[k] = jnp.where(lower, bottom, top)
        to_cross[k] = jnp.where(lower, top, bottom)


def finish(total, parts=(), after=()):
    _, channels, columns = total.shape
    rim = jax.ShapeDtypeStruct((HALO, channels, columns), F32)
    return pl.pallas_call(
        functools.partial(finish_kernel, len(parts)),
        out_shape=(jax.ShapeDtypeStruct(total.shape, F32), rim, rim),
        compiler_params=PARAMS,
        name="finish_canvas",
    )(total, *parts, *after)


def adjoint_rows(n_row, canvas, pair, cross):
    tile = [canvas[r] for r in range(canvas.shape[0])]
    rims = ([ref[k] for k in range(HALO)] for ref in (pair, cross))
    return extended_rows(tile, *rims, HALO, first_of_pair(), row_masks(n_row))


def cross_edges_kernel(canvas, cross, *refs):
    edges = refs[-1]
    lower = first_of_pair()
    tile_rows = canvas.shape[0]
    empty = jnp.zeros(edges.shape, F32)
    lines = [(k, jnp.where(lower, cross[k], empty)) for k in range(HALO)]
    lines += [(HALO + r, canvas[r]) for r in range(tile_rows)]
    lines += [(HALO + tile_rows + k, jnp.where(lower, empty, cross[k])) for k in range(HALO)]
    edges[...] = edge_columns(lines, empty)


def pair_edges_kernel(n_row, tile_rows, partial, pair, edges):
    lower, masks = first_of_pair(), row_masks(n_row)
    result = partial[...]
    empty = jnp.zeros(edges.shape, F32)
    lane = lax.broadcasted_iota(jnp.int32, edges.shape, 1)
    row = ((lane + 4) // 8) % 16
    result = jnp.where(row < HALO, masks[0], jnp.where(row < HALO + tile_rows, 1.0, masks[1])) * result
    lines = [(k, jnp.where(lower, empty, pair[k])) for k in range(HALO)]
    lines += [(HALO + tile_rows + k, jnp.where(lower, pair[k], empty)) for k in range(HALO)]
    edges[...] = result + edge_columns(lines, empty)


def adjoint_edges(n_row, canvas, pair, cross, after=()):
    tile_rows, channels, _ = canvas.shape
    edges = jax.ShapeDtypeStruct((channels, LANES), F32)
    partial = pl.pallas_call(
        cross_edges_kernel, out_shape=edges, compiler_params=PARAMS, name="cross_edges"
    )(canvas, cross, *after)
    return pl.pallas_call(
        functools.partial(pair_edges_kernel, n_row, tile_rows),
        out_shape=edges,
        compiler_params=PARAMS,
        name="pair_edges",
    )(partial, pair)


def steps_kernel(n_row, paired, canvas, pair, cross, one, other, gravity, wide, out, start, middle, after, last):
    tile_rows, channels, columns = canvas.shape
    levels = channels // 3
    part = 8
    masks = row_masks(n_row)
    left, right = from_sides(one[...], other[...], paired)
    rim = jnp.where(first_lanes(left), right, left)
    for k, line in adjoint_rows(n_row, canvas, pair, cross):
        start[k, :, :columns] = line
        start[k, :, columns:] = pltpu.roll(rim, (-8 * k) % LANES, 1)

    def along_x(values):
        return pltpu.roll(values, 2 * columns - 1, 1) - pltpu.roll(values, 1, 1)

    def run(stage, adjoint, store):
        width = HALO - 1 - stage
        begin, end = HALO - width, HALO + tile_rows + width
        for low in range(0, levels, part):
            pull = (0.5 * stage_weight(stage)) * gravity[low : low + part, :]

            def state(k, which):
                return wide[stage, k, which * levels + low : which * levels + low + part, :]

            def line(k):
                a, b, c = (adjoint[k, w * levels + low : w * levels + low + part, :] for w in range(3))
                v = state(k, 2)
                return a, b, c, v, v * b, v * c

            up, here = line(begin - 1), line(begin)
            for k in range(begin, end):
                down = line(k + 1)
                a, b, c, v = here[:4]
                h, u = state(k, 0), state(k, 1)
                a_x, a_y = along_x(a), down[0] - up[0]
                height = u * a_x + v * a_y + pull * (along_x(b) + (down[2] - up[2]))
                east = h * a_x + along_x(u * b) + (down[4] - up[4]) - b * state(k, 3) - c * state(k, 4)
                north = h * a_y + along_x(u * c) + (down[5] - up[5]) - b * state(k, 5) - c * state(k, 6)
                for w, (old, change) in enumerate(zip((a, b, c), (height, east, north))):
                    store(k, w, low, old, change)
                up, here = here, down

    def kept(k, value):
        if k < HALO:
            return value * masks[0]
        if k >= HALO + tile_rows:
            return value * masks[1]
        return value

    def half_into(result):
        def store(k, w, low, old, change):
            result[k, w * levels + low : w * levels + low + part, :] = kept(k, 0.5 * old + change)

        return store

    def after_step(adjoint, k, w, low, old, change):
        return 0.5 * adjoint[k, w * levels + low : w * levels + low + part, :] + old + change

    def to_after(k, w, low, old, change):
        after[k, w * levels + low : w * levels + low + part, :] = kept(k, after_step(start, k, w, low, old, change))

    def to_out(k, w, low, old, change):
        place = pl.ds((w * levels + low) * tile_rows + k - HALO, part, stride=tile_rows)
        out[place, :] = after_step(after, k, w, low, old, change)[:, :columns]

    run(0, start, half_into(middle))
    run(1, middle, to_after)
    run(2, after, half_into(last))
    run(3, last, to_out)


def steps(n_row, paired, canvas, pair, cross, one, other, wide, gravity):
    tile_rows, channels, columns = canvas.shape
    extended = pltpu.VMEM((tile_rows + 2 * HALO, channels, 2 * columns), F32)
    return pl.pallas_call(
        functools.partial(steps_kernel, n_row, paired),
        out_shape=jax.ShapeDtypeStruct((channels * tile_rows, columns), F32),
        scratch_shapes=[extended] * 4,
        compiler_params=PARAMS,
        name="adjoint_steps",
    )(canvas, pair, cross, one, other, gravity, wide)


def shifted(values, axis, by):
    count = lax.axis_size(axis)
    return lax.ppermute(values, axis, [(i, (i + by) % count) for i in range(count)])


def exchanged(values, offset):
    n_row, n_col = lax.axis_size("frow"), lax.axis_size("fcol")
    df, dz = offset
    pairs = [(f * n_col + z, (f ^ df) * n_col + (z ^ dz)) for f in range(n_row) for z in range(n_col)]
    return lax.ppermute(values, ("frow", "fcol"), pairs)


def exchanged_across(values):
    n_row = lax.axis_size("frow")
    return lax.ppermute(values, "frow", [(f, ((f + 1) ^ 1) - 1) for f in range(1, n_row - 1)])


def from_everyone(packed, channels, tile_count):
    groups = packed.shape[0]
    rows = channels + 4
    halves = [
        jnp.concatenate(
            [
                packed[:, h * channels : (h + 1) * channels],
                packed[:, 2 * channels + 4 * h : 2 * channels + 4 * h + 4],
            ],
            axis=1,
        )
        for h in range(2)
    ]
    slots = jnp.stack(halves, axis=2).transpose(1, 0, 2, 3).reshape(rows, tile_count, -1)
    slots = lax.all_to_all(slots, ("frow", "fcol"), split_axis=1, concat_axis=1, tiled=True)
    slots = slots.reshape(rows, groups, 2, LANES).transpose(1, 2, 0, 3)
    return jnp.concatenate(
        [slots[:, 0, :channels], slots[:, 1, :channels], slots[:, 0, channels:], slots[:, 1, channels:]], axis=1
    )


def per_device(latlon_cot, dest_tile, base_cell, corner_frac, saved_states, gravity):
    n_row, n_col = lax.axis_size("frow"), lax.axis_size("fcol")
    tile_count = n_row * n_col
    levels = gravity.shape[0]
    tile_rows = saved_states.shape[4]
    columns = saved_states.shape[5]
    channels = 3 * levels
    points = base_cell.shape[0]
    lines = points // LANES
    share = GROUP * tile_count // (2 * points)
    paired = share == 1 and n_row == 4 and n_col == 4
    size = (channels, tile_rows, columns)

    cot = latlon_cot.reshape(channels, points)
    partner_cot = exchanged(cot, (1, 0)) if paired else None
    sent, to_cross, turned, cot = prepare(
        dest_tile.reshape(lines, LANES),
        base_cell.reshape(lines, LANES),
        corner_frac,
        saved_states.reshape(4, channels * tile_rows, columns),
        cot,
        (3, 2, 1, 0),
        tile_rows,
    )
    pair_at = 4 * lines
    pair = exchanged(sent, (1, 0))
    cross = exchanged_across(to_cross)
    if paired:
        chip_points = cot, sent, partner_cot, pair
        packed = pack_chip(FAR, chip_points, tile_rows, columns)
        got = [packed[0]] + [exchanged(block, (df, dz ^ 2)) for block, (df, dz) in zip(packed[1:], FAR[1:])]
        packed = pack_chip(NEAR, chip_points, tile_rows, columns, [cross, packed[0]])
        total = scatter(got[:2], None, *size, packed[:1])[0]
        sums = scatter(got[2:], total, *size, parts=2)
        far = [exchanged(part, (0, 2)) for part in sums]
        got = [packed[0]] + [exchanged(block, tile) for block, tile in zip(packed[1:], NEAR[1:])]
        one, other = all_state_edges(n_row, pair_at, paired, turned, pair, cross, sums)
        one, other = exchanged(one, (0, 1)), exchanged(other, (0, 3))
        total = scatter(got[:2], None, *size)[0]
        total = scatter(got[2:], total, *size)[0]
        wide, pull = widen(n_row, pair_at, paired, turned, pair, cross, one, other, gravity)
        canvas = finish(total, far, [one, other])
    else:
        packed = pack_all(cot, sent, tile_count, share, tile_rows, columns)
        got = from_everyone(packed, channels, tile_count)
        one, other = all_state_edges(n_row, pair_at, paired, turned, pair, cross)
        one, other = shifted(one, "fcol", 1), shifted(other, "fcol", -1)
        wide, pull = widen(n_row, pair_at, paired, turned, pair, cross, one, other, gravity)
        canvas = finish(scatter([got.reshape(-1, LANES)], None, *size)[0])

    canvas, to_pair, to_cross = canvas
    pair, cross = exchanged(to_pair, (1, 0)), exchanged_across(to_cross)
    edges = adjoint_edges(n_row, canvas, pair, cross, [pull])
    if paired:
        sides = exchanged(edges, (0, 1)), exchanged(edges, (0, 3))
    else:
        sides = shifted(edges, "fcol", 1), shifted(edges, "fcol", -1)
    result = steps(n_row, paired, canvas, pair, cross, *sides, wide, pull)
    return result.reshape(3, levels, tile_rows, columns)


def solution(mesh):
    placed = (
        P(None, None, ("member", "frow", "fcol")),
        P(("frow", "fcol"), None),
        P(("frow", "fcol")),
        P(None, ("frow", "fcol")),
        P(None, None, None, None, ("member", "frow"), "fcol"),
        P(),
    )
    return jax.shard_map(
        per_device,
        mesh=mesh,
        in_specs=placed,
        out_specs=P(None, None, ("member", "frow"), "fcol"),
        check_vma=False,
    )
```

```python
import functools

import jax
import jax.numpy as jnp
from jax import lax
from jax.experimental import pallas as pl
from jax.experimental.pallas import tpu as pltpu
from jax.sharding import PartitionSpec as P

time_step = 0.25
coriolis_peak = 0.8

HALO = 4
GROUP = 256
LANES = 128
F32 = jnp.float32
BF16 = jnp.bfloat16
PARAMS = pltpu.CompilerParams(vmem_limit_bytes=16 * 1024 * 1024)


def split(values):
    high = values.astype(BF16)
    return high, (values - high.astype(F32)).astype(BF16)


def dot_nt(a, b):
    return lax.dot_general(a, b, (((1,), (1,)), ((), ())), preferred_element_type=F32)


def first_of_pair(axis="frow"):
    return lax.rem(lax.axis_index(axis), 2) == 0


def row_masks(n_row):
    at = lax.axis_index("frow")
    return jnp.where(at > 0, 1.0, 0.0).astype(F32), jnp.where(at < n_row - 1, 1.0, 0.0).astype(F32)


def extended_rows(tile, pair, cross, width, lower, masks):
    tile_rows = len(tile)
    lines = [(HALO - width + k, jnp.where(lower, cross[k], pair[k]) * masks[0]) for k in range(width)]
    lines += [(HALO + k, tile[k]) for k in range(tile_rows)]
    lines += [(HALO + tile_rows + k, jnp.where(lower, pair[k], cross[k]) * masks[1]) for k in range(width)]
    return lines


def edge_columns(lines, result):
    lane = lax.broadcasted_iota(jnp.int32, result.shape, 1)
    owner = ((lane + 4) // 8) % 16
    for k, line in lines:
        result = jnp.where(owner == k, pltpu.roll(line, (8 * k) % LANES, 1), result)
    return result


def first_lanes(like):
    return lax.broadcasted_iota(jnp.int32, like.shape, 1) % 8 < 4


def from_sides(one, other, paired):
    if not paired:
        return one, other
    lower = first_of_pair("fcol")
    return jnp.where(lower, other, one), jnp.where(lower, one, other)


def first_row(which):
    return sum(HALO - k for k in range(which))


def prepare_kernel(order, dest, base, frac, states, cot, sent, cross, turned, cot_out, dest_v, base_v, frac_v, states_v, sems):
    moves = ((dest, dest_v), (base, base_v), (frac, frac_v), (states, states_v), (cot, cot_out))
    copies = [pltpu.make_async_copy(source, target, sems.at[i]) for i, (source, target) in enumerate(moves)]
    for copy in copies:
        copy.start()
    for copy in copies[:3]:
        copy.wait()
    lines = dest_v.shape[0]
    sent[:lines, :] = dest_v[...].astype(F32)
    sent[lines : 2 * lines, :] = base_v[...].astype(F32)
    for k in range(2):
        for i in range(lines):
            sent[(2 + k) * lines + i : (2 + k) * lines + i + 1, :] = frac_v[k : k + 1, i * LANES : (i + 1) * LANES]
    copies[3].wait()
    _, tile_rows, channels, _ = turned.shape
    lower = first_of_pair()
    for which, source in enumerate(order):
        for r in range(tile_rows):
            turned[which, r] = states_v[source, pl.ds(r, channels, stride=tile_rows), :]
        width = HALO - which
        for k in range(width):
            top, bottom = turned[which, k], turned[which, tile_rows - width + k]
            at = (first_row(which) + k) * channels
            sent[4 * lines + at : 4 * lines + at + channels, :] = jnp.where(lower, bottom, top)
            cross[at : at + channels, :] = jnp.where(lower, top, bottom)
    copies[4].wait()


def prepare(dest, base, frac, states, cot, order, tile_rows):
    channels, points = cot.shape
    columns = states.shape[2]
    stages = len(order)
    rim = first_row(stages) * channels
    lines = points // LANES
    in_hbm = pl.BlockSpec(memory_space=pltpu.HBM)
    return pl.pallas_call(
        functools.partial(prepare_kernel, order),
        in_specs=[in_hbm] * 5,
        out_shape=(
            jax.ShapeDtypeStruct((4 * lines + rim, LANES), F32),
            jax.ShapeDtypeStruct((rim, columns), F32),
            jax.ShapeDtypeStruct((stages, tile_rows, channels, columns), F32),
            jax.ShapeDtypeStruct(cot.shape, F32),
        ),
        scratch_shapes=[
            pltpu.VMEM(dest.shape, jnp.int32),
            pltpu.VMEM(base.shape, jnp.int32),
            pltpu.VMEM(frac.shape, F32),
            pltpu.VMEM(states.shape, F32),
            pltpu.SemaphoreType.DMA((5,)),
        ],
        compiler_params=PARAMS,
        name="prepare",
    )(*(pltpu.with_memory_space_constraint(x, pltpu.HBM) for x in (dest, base, frac, states, cot)))


def state_rows(which, turned, pair, pair_at, cross, lower, masks):
    _, tile_rows, channels, _ = turned.shape
    width = HALO - which

    def rim(ref, start):
        at = [start + (first_row(which) + k) * channels for k in range(width)]
        return [ref[i : i + channels, :] for i in at]

    tile = [turned[which, r] for r in range(tile_rows)]
    return extended_rows(tile, rim(pair, pair_at), rim(cross, 0), width, lower, masks)


def edge_plan(stages, tile_rows):
    plan, lane = [], 0
    for which in range(stages):
        width = HALO - which
        for k in range(HALO - width, HALO + tile_rows + width):
            count = width - max(HALO - k, k - (HALO + tile_rows - 1), 0)
            if count > 0:
                plan.append((which, k, count, lane))
                lane += count
    return plan


def state_edges(n_row, turned, pair, pair_at, cross):
    stages, tile_rows, channels, _ = turned.shape
    lower, masks = first_of_pair(), row_masks(n_row)
    lane = lax.broadcasted_iota(jnp.int32, (channels, LANES), 1)
    first = last = jnp.zeros((channels, LANES), F32)
    lines = [dict(state_rows(which, turned, pair, pair_at, cross, lower, masks)) for which in range(stages)]
    for which, k, count, at in edge_plan(stages, tile_rows):
        here = (lane >= at) & (lane < at + count)
        first = jnp.where(here, pltpu.roll(lines[which][k], at, 1), first)
        last = jnp.where(here, pltpu.roll(lines[which][k], (at + count) % LANES, 1), last)
    return first, last


def state_edges_kernel(n_row, pair_at, paired, turned, pair, cross, *refs):
    one, other = refs[-2:]
    first, last = state_edges(n_row, turned, pair, pair_at, cross)
    if paired:
        lower = first_of_pair("fcol")
        first, last = jnp.where(lower, last, first), jnp.where(lower, first, last)
    one[...], other[...] = first, last


def all_state_edges(n_row, pair_at, paired, turned, pair, cross, after=()):
    return pl.pallas_call(
        functools.partial(state_edges_kernel, n_row, pair_at, paired),
        out_shape=[jax.ShapeDtypeStruct((turned.shape[2], LANES), F32)] * 2,
        compiler_params=PARAMS,
        name="state_edges",
    )(turned, pair, cross, *after)


FIELDS = 7


def stage_weight(which):
    return 0.5 * time_step if which % 2 == 0 else time_step


def store_fields(wide, which, lines, levels, base_row, total_rows):
    weight = stage_weight(which)
    channels = 3 * levels
    for k, line in lines:
        wide[which, k, :channels, :] = (0.5 * weight) * line
    winds = slice(levels, channels)
    for k in range(lines[0][0] + 1, lines[-1][0]):
        values = wide[which, k, winds, :]
        change = pltpu.roll(values, LANES - 1, 1) - pltpu.roll(values, 1, 1)
        slope = wide[which, k + 1, winds, :] - wide[which, k - 1, winds, :]
        rotation = weight * (coriolis_peak * (2.0 * ((base_row + k - HALO).astype(F32) + 0.5) / total_rows - 1.0))
        begin = channels
        for value in (change[:levels], change[levels:] + rotation, slope[:levels] - rotation, slope[levels:]):
            wide[which, k, begin : begin + levels, :] = value
            begin += levels


def tile_fields_kernel(n_row, pair_at, turned, pair, cross, gravity, *refs):
    wide, pull = refs[-2:]
    stages, tile_rows, channels, _ = turned.shape
    levels = channels // 3
    level = lax.broadcasted_iota(jnp.int32, pull.shape, 0)
    pulls = jnp.zeros(pull.shape, F32)
    for i in range(levels):
        pulls = jnp.where(level == i, gravity[i], pulls)
    pull[...] = pulls
    lower, masks = first_of_pair(), row_masks(n_row)
    for which in range(stages):
        lines = state_rows(which, turned, pair, pair_at, cross, lower, masks)
        store_fields(wide, which, lines, levels, lax.axis_index("frow") * tile_rows, tile_rows * n_row)


def tile_fields(n_row, pair_at, turned, pair, cross, gravity, after=()):
    stages, tile_rows, channels, columns = turned.shape
    in_vmem = pl.BlockSpec(memory_space=pltpu.VMEM)
    return pl.pallas_call(
        functools.partial(tile_fields_kernel, n_row, pair_at),
        in_specs=[in_vmem] * 3 + [pl.BlockSpec(memory_space=pltpu.SMEM)] + [in_vmem] * len(after),
        out_shape=(
            jax.ShapeDtypeStruct((stages, tile_rows + 2 * HALO, channels // 3 * FIELDS, columns), F32),
            jax.ShapeDtypeStruct((channels // 3, columns), F32),
        ),
        compiler_params=PARAMS,
        name="tile_fields",
    )(turned, pair, cross, gravity, *after)


PART = 8
BEYOND_AT = 32


def edge_windows(line):
    lane = lax.broadcasted_iota(jnp.int32, line.shape, 1)
    return jnp.where((lane >= BEYOND_AT // 2) & (lane < 2 * BEYOND_AT), pltpu.roll(line, BEYOND_AT, 1), line)


def with_rim(window, rim):
    lane = lax.broadcasted_iota(jnp.int32, window.shape, 1)
    beyond = (lane >= LANES - HALO) | ((lane >= BEYOND_AT) & (lane < BEYOND_AT + HALO))
    return jnp.where(beyond, rim, window)


def edge_fields_kernel(n_row, pair_at, paired, turned, pair, cross, one, other, wide):
    stages, tile_rows, channels, columns = turned.shape
    lower, masks = first_of_pair(), row_masks(n_row)
    left, right = from_sides(one[...], other[...], paired)
    lane = lax.broadcasted_iota(jnp.int32, (channels, columns), 1)
    rims = {
        (which, k): jnp.where(
            lane < columns // 2,
            pltpu.roll(right, (BEYOND_AT - at) % columns, 1),
            pltpu.roll(left, (-at - count) % columns, 1),
        )
        for which, k, count, at in edge_plan(stages, tile_rows)
    }
    for which in range(stages):
        lines = [
            (k, with_rim(edge_windows(line), rims.get((which, k), line)))
            for k, line in state_rows(which, turned, pair, pair_at, cross, lower, masks)
        ]
        store_fields(wide, which, lines, channels // 3, lax.axis_index("frow") * tile_rows, tile_rows * n_row)


def edge_fields(n_row, pair_at, paired, turned, pair, cross, one, other):
    stages, tile_rows, channels, columns = turned.shape
    return pl.pallas_call(
        functools.partial(edge_fields_kernel, n_row, pair_at, paired),
        out_shape=jax.ShapeDtypeStruct((stages, tile_rows + 2 * HALO, channels // 3 * FIELDS, columns), F32),
        compiler_params=PARAMS,
        name="edge_fields",
    )(turned, pair, cross, one, other)


def slot_blocks(cot, where, tiles, share, tile_rows, columns, onehot, parts):
    channels, points = cot.shape
    lines = points // LANES
    groups = tiles.shape[0] // share
    corner = where[lines : 2 * lines, :]
    row = jnp.zeros_like(corner)
    for k in range(1, tile_rows - 1):
        row = row + (corner >= float(k * (columns - 1))).astype(F32)
    col = corner - row * float(columns - 1)
    target = where[:lines, :]
    offsets = [where[k * lines : (k + 1) * lines, :] for k in (2, 3)]

    before = (
        lax.broadcasted_iota(jnp.int32, (GROUP, GROUP), 0)
        < lax.broadcasted_iota(jnp.int32, (GROUP, GROUP), 1)
    ).astype(F32).astype(BF16)
    index = lax.broadcasted_iota(jnp.int32, tiles.shape, 0)
    begin = ((index % share) * (GROUP // share)).astype(F32)
    slots = lax.broadcasted_iota(jnp.int32, (GROUP, GROUP), 0).astype(F32).astype(BF16)
    one, zero = jnp.ones(slots.shape, BF16), jnp.zeros(slots.shape, BF16)
    count = jnp.zeros((tiles.shape[0], 1), F32)
    rows = channels + 8
    for b in range(points // GROUP):
        part = slice(b * GROUP, (b + 1) * GROUP)

        def across(values):
            return jnp.concatenate([values[2 * b : 2 * b + 1, :], values[2 * b + 1 : 2 * b + 2, :]], axis=1)

        named = (tiles == across(target)).astype(F32)
        ahead = jnp.dot(named.astype(BF16), before, preferred_element_type=F32)
        lane = jnp.sum(named * (ahead + count + begin), axis=0, keepdims=True)
        count = count + jnp.sum(named, axis=1, keepdims=True)
        onehot[:, part] = jnp.where(slots == lane.astype(BF16), one, zero)
        coords = [across(values) for values in (row, col, *offsets)]
        data_high, data_low = split(jnp.concatenate([cot[:, part], *coords, *coords], axis=0))
        for g in range(groups):
            mine = named[g * share : g * share + 1, :]
            for i in range(1, share):
                mine = mine + named[g * share + i : g * share + i + 1, :]
            mine = mine.astype(BF16)
            parts[g * rows : (g + 1) * rows, part] = data_high * mine
            parts[(groups + g) * rows : (groups + g + 1) * rows, part] = data_low * mine
    both = dot_nt(parts[...], onehot[...])
    packed = both[: groups * rows, :] + both[groups * rows :, :]
    upper = lax.broadcasted_iota(jnp.int32, (8, LANES), 0) < 4
    for g in range(groups):
        block = packed[g * rows : (g + 1) * rows, :]
        yield (
            block[:channels, :LANES],
            block[:channels, LANES:],
            jnp.where(upper, block[channels:, :LANES], block[channels:, LANES:]),
        )


def store_block(out, at, pieces):
    channels = pieces[0].shape[0]
    out[at : at + channels, :] = pieces[0]
    out[at + channels : at + 2 * channels, :] = pieces[1]
    out[at + 2 * channels : at + 2 * channels + 8, :] = pieces[2]


def pack_scratch(channels, points, groups):
    return [
        pltpu.VMEM((GROUP, points), BF16),
        pltpu.VMEM((2 * groups * (channels + 8), points), BF16),
    ]


def pack_all_kernel(tile_count, share, tile_rows, columns, cot, where, out, *scratch):
    tiles = lax.broadcasted_iota(jnp.int32, (tile_count, GROUP), 0).astype(F32)
    for g, pieces in enumerate(slot_blocks(cot, where, tiles, share, tile_rows, columns, *scratch)):
        store_block(out.at[g], 0, pieces)


def pack_all(cot, where, tile_count, share, tile_rows, columns):
    channels, points = cot.shape
    groups = tile_count // share
    return pl.pallas_call(
        functools.partial(pack_all_kernel, tile_count, share, tile_rows, columns),
        out_shape=jax.ShapeDtypeStruct((groups, 2 * channels + 8, LANES), F32),
        scratch_shapes=pack_scratch(channels, points, groups),
        compiler_params=PARAMS,
        name="pack_points",
    )(cot, where)


NEAR = ((0, 0), (2, 0), (0, 1), (2, 1))
FAR = ((0, 2), (2, 2), (0, 3), (2, 3))


def partner_tiles(partners):
    at_row, at_col = lax.axis_index("frow"), lax.axis_index("fcol")
    n_col = lax.axis_size("fcol")
    index = lax.broadcasted_iota(jnp.int32, (len(partners), GROUP), 0)
    tiles = jnp.zeros(index.shape, jnp.int32)
    for g, (df, dz) in enumerate(partners):
        tiles = jnp.where(index == g, (at_row ^ df) * n_col + (at_col ^ dz), tiles)
    return tiles.astype(F32)


def pack_chip_kernel(tiles, tile_rows, columns, cot, where, pair_cot, pair_where, *refs):
    outs, scratch = refs[-4 - len(tiles) : -4], refs[-4:]
    begin = 0
    for i, points in enumerate(((cot, where), (pair_cot, pair_where))):
        blocks = slot_blocks(*points, partner_tiles(tiles), 1, tile_rows, columns, *scratch[2 * i : 2 * i + 2])
        for out, pieces in zip(outs, blocks):
            store_block(out, begin, pieces)
        begin += 2 * cot.shape[0] + 8


def pack_chip(tiles, points, tile_rows, columns, after=()):
    channels, count = points[0].shape
    return pl.pallas_call(
        functools.partial(pack_chip_kernel, tiles, tile_rows, columns),
        out_shape=[jax.ShapeDtypeStruct((2 * (2 * channels + 8), LANES), F32)] * len(tiles),
        scratch_shapes=pack_scratch(channels, count, len(tiles)) * 2,
        compiler_params=PARAMS,
        name="pack_chip",
    )(*points, *after)


def scatter_kernel(count, first, later, *refs):
    blocks, refs = refs[:count], refs[count:]
    if not first:
        total, refs = refs[0], refs[1:]
    outs, (parts, weight) = refs[later:-2], refs[-2:]
    part_rows, channels, columns = outs[0].shape
    tile_rows = part_rows * len(outs)
    rows = 2 * channels + 8
    cells = lax.broadcasted_iota(jnp.int32, (columns, LANES), 0).astype(F32)
    lines = lax.broadcasted_iota(jnp.int32, (tile_rows, LANES), 0).astype(F32)

    def hat(index, corner, fraction):
        away = index - corner
        return jnp.where(away == 0.0, 1.0 - fraction, jnp.where(away == 1.0, fraction, 0.0))

    at = 0
    for block in blocks:
        for source in range(block.shape[0] // rows):
            for half in range(2):
                part = slice(at, at + LANES)
                at += LANES
                begin = source * rows + 2 * channels + 4 * half
                coords = block[begin : begin + 4, :]
                row, col, along_rows, along_cols = (coords[k : k + 1, :] for k in range(4))
                weight_high, weight_low = split(hat(cells, col, along_cols))
                weight[:columns, part] = weight_high
                weight[columns:, part] = weight_low
                begin = source * rows + half * channels
                values = block[begin : begin + channels, :]
                row_weight = hat(lines, row, along_rows)
                for r in range(tile_rows):
                    product_high, product_low = split(values * row_weight[r : r + 1, :])
                    parts[r * channels : (r + 1) * channels, part] = product_high
                    parts[(tile_rows + r) * channels : (tile_rows + r + 1) * channels, part] = product_low
    both = dot_nt(parts[...], weight[...])
    sums = both[:, :columns] + both[:, columns:]
    sums = sums[: tile_rows * channels, :] + sums[tile_rows * channels :, :]
    for r in range(tile_rows):
        line = sums[r * channels : (r + 1) * channels, :]
        if not first:
            line = line + total[r]
        outs[r // part_rows][r % part_rows] = line


def scatter(blocks, total, channels, tile_rows, columns, after=(), parts=1):
    slots = sum(block.shape[0] // (2 * channels + 8) for block in blocks) * GROUP
    return pl.pallas_call(
        functools.partial(scatter_kernel, len(blocks), total is None, len(after)),
        out_shape=[jax.ShapeDtypeStruct((tile_rows // parts, channels, columns), F32)] * parts,
        scratch_shapes=[
            pltpu.VMEM((2 * tile_rows * channels, slots), BF16),
            pltpu.VMEM((2 * columns, slots), BF16),
        ],
        compiler_params=PARAMS,
        name="scatter_points",
    )(*blocks, *([] if total is None else [total]), *after)


def finish_kernel(count, total, *refs):
    parts, (canvas, to_pair, to_cross) = refs[:count], refs[-3:]
    tile_rows = canvas.shape[0]
    for r in range(tile_rows):
        line = total[r]
        if parts:
            size = parts[0].shape[0]
            line = line + parts[r // size][r % size]
        canvas[r] = line
    lower = first_of_pair()
    for k in range(HALO):
        top, bottom = canvas[k], canvas[tile_rows - HALO + k]
        to_pair[k] = jnp.where(lower, bottom, top)
        to_cross[k] = jnp.where(lower, top, bottom)


def finish(total, parts=(), after=()):
    _, channels, columns = total.shape
    rim = jax.ShapeDtypeStruct((HALO, channels, columns), F32)
    return pl.pallas_call(
        functools.partial(finish_kernel, len(parts)),
        out_shape=(jax.ShapeDtypeStruct(total.shape, F32), rim, rim),
        compiler_params=PARAMS,
        name="finish_canvas",
    )(total, *parts, *after)


def adjoint_rows(n_row, canvas, pair, cross):
    tile = [canvas[r] for r in range(canvas.shape[0])]
    rims = ([ref[k] for k in range(HALO)] for ref in (pair, cross))
    return extended_rows(tile, *rims, HALO, first_of_pair(), row_masks(n_row))


def cross_edges_kernel(canvas, cross, *refs):
    edges = refs[-1]
    lower = first_of_pair()
    tile_rows = canvas.shape[0]
    empty = jnp.zeros(edges.shape, F32)
    lines = [(k, jnp.where(lower, cross[k], empty)) for k in range(HALO)]
    lines += [(HALO + r, canvas[r]) for r in range(tile_rows)]
    lines += [(HALO + tile_rows + k, jnp.where(lower, empty, cross[k])) for k in range(HALO)]
    edges[...] = edge_columns(lines, empty)


def pair_edges_kernel(n_row, tile_rows, partial, pair, edges):
    lower, masks = first_of_pair(), row_masks(n_row)
    result = partial[...]
    empty = jnp.zeros(edges.shape, F32)
    lane = lax.broadcasted_iota(jnp.int32, edges.shape, 1)
    row = ((lane + 4) // 8) % 16
    result = jnp.where(row < HALO, masks[0], jnp.where(row < HALO + tile_rows, 1.0, masks[1])) * result
    lines = [(k, jnp.where(lower, empty, pair[k])) for k in range(HALO)]
    lines += [(HALO + tile_rows + k, jnp.where(lower, pair[k], empty)) for k in range(HALO)]
    edges[...] = result + edge_columns(lines, empty)


def adjoint_edges(n_row, canvas, pair, cross, after=()):
    tile_rows, channels, _ = canvas.shape
    edges = jax.ShapeDtypeStruct((channels, LANES), F32)
    partial = pl.pallas_call(
        cross_edges_kernel, out_shape=edges, compiler_params=PARAMS, name="cross_edges"
    )(canvas, cross, *after)
    return pl.pallas_call(
        functools.partial(pair_edges_kernel, n_row, tile_rows),
        out_shape=edges,
        compiler_params=PARAMS,
        name="pair_edges",
    )(partial, pair)


def run_stages(wide, gravity, levels, masks, tile_rows, buffers, store):
    start, middle, after, last = buffers

    def along_x(values):
        return pltpu.roll(values, LANES - 1, 1) - pltpu.roll(values, 1, 1)

    def run(stage, adjoint, put):
        width = HALO - 1 - stage
        begin, end = HALO - width, HALO + tile_rows + width
        for low in range(0, levels, PART):
            pull = (0.5 * stage_weight(stage)) * gravity[low : low + PART, :]

            def state(k, which):
                return wide[stage, k, which * levels + low : which * levels + low + PART, :]

            def line(k):
                a, b, c = (adjoint[k, w * levels + low : w * levels + low + PART, :] for w in range(3))
                v = state(k, 2)
                return a, b, c, v, v * b, v * c

            up, here = line(begin - 1), line(begin)
            for k in range(begin, end):
                down = line(k + 1)
                a, b, c, v = here[:4]
                h, u = state(k, 0), state(k, 1)
                a_x, a_y = along_x(a), down[0] - up[0]
                height = u * a_x + v * a_y + pull * (along_x(b) + (down[2] - up[2]))
                east = h * a_x + along_x(u * b) + (down[4] - up[4]) - b * state(k, 3) - c * state(k, 4)
                north = h * a_y + along_x(u * c) + (down[5] - up[5]) - b * state(k, 5) - c * state(k, 6)
                for w, (old, change) in enumerate(zip((a, b, c), (height, east, north))):
                    put(k, w, low, old, change)
                up, here = here, down

    def kept(k, value):
        if k < HALO:
            return value * masks[0]
        if k >= HALO + tile_rows:
            return value * masks[1]
        return value

    def half_into(result):
        def put(k, w, low, old, change):
            result[k, w * levels + low : w * levels + low + PART, :] = kept(k, 0.5 * old + change)

        return put

    def after_step(adjoint, k, w, low, old, change):
        return 0.5 * adjoint[k, w * levels + low : w * levels + low + PART, :] + old + change

    def to_after(k, w, low, old, change):
        after[k, w * levels + low : w * levels + low + PART, :] = kept(k, after_step(start, k, w, low, old, change))

    def to_end(k, w, low, old, change):
        store(k - HALO, w, low, after_step(after, k, w, low, old, change))

    run(0, start, half_into(middle))
    run(1, middle, to_after)
    run(2, after, half_into(last))
    run(3, last, to_end)


def tile_steps_kernel(n_row, canvas, pair, cross, wide, gravity, out, windows, *buffers):
    tile_rows, channels, _ = canvas.shape
    levels = channels // 3
    for k, line in adjoint_rows(n_row, canvas, pair, cross):
        buffers[0][k] = line
        windows[k] = edge_windows(line)

    def store(r, w, low, value):
        out[r, w * levels + low : w * levels + low + PART, :] = value

    run_stages(wide, gravity, levels, row_masks(n_row), tile_rows, buffers, store)


def tile_steps(n_row, canvas, pair, cross, wide, gravity):
    tile_rows, channels, columns = canvas.shape
    return pl.pallas_call(
        functools.partial(tile_steps_kernel, n_row),
        out_shape=(
            jax.ShapeDtypeStruct(canvas.shape, F32),
            jax.ShapeDtypeStruct((tile_rows + 2 * HALO, channels, columns), F32),
        ),
        scratch_shapes=[pltpu.VMEM((tile_rows + 2 * HALO, channels, columns), F32)] * 4,
        compiler_params=PARAMS,
        name="tile_steps",
    )(canvas, pair, cross, wide, gravity)


def edge_steps_kernel(n_row, paired, windows, one, other, wide, gravity, inner, out, *buffers):
    *buffers, result = buffers
    tile_rows, channels, _ = inner.shape
    levels = channels // 3
    left, right = from_sides(one[...], other[...], paired)
    rims = jnp.where(first_lanes(left), pltpu.roll(right, BEYOND_AT, 1), left)
    for k in range(tile_rows + 2 * HALO):
        buffers[0][k] = with_rim(windows[k], pltpu.roll(rims, (-8 * k) % LANES, 1))
    lane = lax.broadcasted_iota(jnp.int32, (PART, LANES), 1)

    def store(r, w, low, value):
        result[r, w * levels + low : w * levels + low + PART, :] = value

    run_stages(wide, gravity, levels, row_masks(n_row), tile_rows, buffers, store)
    for r in range(tile_rows):
        for begin in range(0, channels, PART):
            value = result[r, begin : begin + PART, :]
            final = pltpu.roll(value, LANES - BEYOND_AT, 1)
            line = jnp.where(lane >= LANES - HALO, final, inner[r, begin : begin + PART, :])
            out[pl.ds(begin * tile_rows + r, PART, stride=tile_rows), :] = jnp.where(lane < HALO, value, line)


def edge_steps(n_row, paired, windows, one, other, wide, gravity, inner):
    tile_rows, channels, columns = inner.shape
    return pl.pallas_call(
        functools.partial(edge_steps_kernel, n_row, paired),
        out_shape=jax.ShapeDtypeStruct((channels * tile_rows, columns), F32),
        scratch_shapes=[pltpu.VMEM(windows.shape, F32)] * 4 + [pltpu.VMEM(inner.shape, F32)],
        compiler_params=PARAMS,
        name="edge_steps",
    )(windows, one, other, wide, gravity, inner)


def shifted(values, axis, by):
    count = lax.axis_size(axis)
    return lax.ppermute(values, axis, [(i, (i + by) % count) for i in range(count)])


def exchanged(values, offset):
    n_row, n_col = lax.axis_size("frow"), lax.axis_size("fcol")
    df, dz = offset
    pairs = [(f * n_col + z, (f ^ df) * n_col + (z ^ dz)) for f in range(n_row) for z in range(n_col)]
    return lax.ppermute(values, ("frow", "fcol"), pairs)


def exchanged_across(values):
    n_row = lax.axis_size("frow")
    return lax.ppermute(values, "frow", [(f, ((f + 1) ^ 1) - 1) for f in range(1, n_row - 1)])


def from_everyone(packed, channels, tile_count):
    groups = packed.shape[0]
    rows = channels + 4
    halves = [
        jnp.concatenate(
            [
                packed[:, h * channels : (h + 1) * channels],
                packed[:, 2 * channels + 4 * h : 2 * channels + 4 * h + 4],
            ],
            axis=1,
        )
        for h in range(2)
    ]
    slots = jnp.stack(halves, axis=2).transpose(1, 0, 2, 3).reshape(rows, tile_count, -1)
    slots = lax.all_to_all(slots, ("frow", "fcol"), split_axis=1, concat_axis=1, tiled=True)
    slots = slots.reshape(rows, groups, 2, LANES).transpose(1, 2, 0, 3)
    return jnp.concatenate(
        [slots[:, 0, :channels], slots[:, 1, :channels], slots[:, 0, channels:], slots[:, 1, channels:]], axis=1
    )


def per_device(latlon_cot, dest_tile, base_cell, corner_frac, saved_states, gravity):
    n_row, n_col = lax.axis_size("frow"), lax.axis_size("fcol")
    tile_count = n_row * n_col
    levels = gravity.shape[0]
    tile_rows = saved_states.shape[4]
    columns = saved_states.shape[5]
    channels = 3 * levels
    points = base_cell.shape[0]
    lines = points // LANES
    share = GROUP * tile_count // (2 * points)
    paired = share == 1 and n_row == 4 and n_col == 4
    size = (channels, tile_rows, columns)

    cot = latlon_cot.reshape(channels, points)
    partner_cot = exchanged(cot, (1, 0)) if paired else None
    sent, to_cross, turned, cot = prepare(
        dest_tile.reshape(lines, LANES),
        base_cell.reshape(lines, LANES),
        corner_frac,
        saved_states.reshape(4, channels * tile_rows, columns),
        cot,
        (3, 2, 1, 0),
        tile_rows,
    )
    pair_at = 4 * lines
    pair = exchanged(sent, (1, 0))
    cross = exchanged_across(to_cross)
    if paired:
        chip_points = cot, sent, partner_cot, pair
        packed = pack_chip(FAR, chip_points, tile_rows, columns)
        got = [packed[0]] + [exchanged(block, (df, dz ^ 2)) for block, (df, dz) in zip(packed[1:], FAR[1:])]
        packed = pack_chip(NEAR, chip_points, tile_rows, columns, [cross, packed[0]])
        total = scatter(got[:2], None, *size, packed[:1])[0]
        sums = scatter(got[2:], total, *size, parts=2)
        far = [exchanged(part, (0, 2)) for part in sums]
        got = [packed[0]] + [exchanged(block, tile) for block, tile in zip(packed[1:], NEAR[1:])]
        one, other = all_state_edges(n_row, pair_at, paired, turned, pair, cross, sums)
        one, other = exchanged(one, (0, 1)), exchanged(other, (0, 3))
        total = scatter(got[:2], None, *size)[0]
        total = scatter(got[2:], total, *size)[0]
        fields, pull = tile_fields(n_row, pair_at, turned, pair, cross, gravity, [total])
        canvas = finish(total, far, [one, other, pull])
    else:
        packed = pack_all(cot, sent, tile_count, share, tile_rows, columns)
        got = from_everyone(packed, channels, tile_count)
        one, other = all_state_edges(n_row, pair_at, paired, turned, pair, cross)
        one, other = shifted(one, "fcol", 1), shifted(other, "fcol", -1)
        fields, pull = tile_fields(n_row, pair_at, turned, pair, cross, gravity)
        canvas = finish(scatter([got.reshape(-1, LANES)], None, *size)[0])

    near_edges = edge_fields(n_row, pair_at, paired, turned, pair, cross, one, other)
    canvas, to_pair, to_cross = canvas
    pair, cross = exchanged(to_pair, (1, 0)), exchanged_across(to_cross)
    edges = adjoint_edges(n_row, canvas, pair, cross, [near_edges])
    if paired:
        sides = exchanged(edges, (0, 1)), exchanged(edges, (0, 3))
    else:
        sides = shifted(edges, "fcol", 1), shifted(edges, "fcol", -1)
    inner, windows = tile_steps(n_row, canvas, pair, cross, fields, pull)
    result = edge_steps(n_row, paired, windows, *sides, near_edges, pull, inner)
    return result.reshape(3, levels, tile_rows, columns)


def solution(mesh):
    placed = (
        P(None, None, ("member", "frow", "fcol")),
        P(("frow", "fcol"), None),
        P(("frow", "fcol")),
        P(None, ("frow", "fcol")),
        P(None, None, None, None, ("member", "frow"), "fcol"),
        P(),
    )
    return jax.shard_map(
        per_device,
        mesh=mesh,
        in_specs=placed,
        out_specs=P(None, None, ("member", "frow"), "fcol"),
        check_vma=False,
    )
```

```python
import functools

import jax
import jax.numpy as jnp
from jax import lax
from jax.experimental import pallas as pl
from jax.experimental.pallas import tpu as pltpu
from jax.sharding import PartitionSpec as P

time_step = 0.25
coriolis_peak = 0.8

HALO = 4
GROUP = 256
LANES = 128
F32 = jnp.float32
BF16 = jnp.bfloat16
PARAMS = pltpu.CompilerParams(vmem_limit_bytes=16 * 1024 * 1024)


def split(values):
    high = values.astype(BF16)
    return high, (values - high.astype(F32)).astype(BF16)


def dot_nt(a, b):
    return lax.dot_general(a, b, (((1,), (1,)), ((), ())), preferred_element_type=F32)


def first_of_pair(axis="frow"):
    return lax.rem(lax.axis_index(axis), 2) == 0


def row_masks(n_row):
    at = lax.axis_index("frow")
    return jnp.where(at > 0, 1.0, 0.0).astype(F32), jnp.where(at < n_row - 1, 1.0, 0.0).astype(F32)


def extended_rows(tile, pair, cross, width, lower, masks):
    tile_rows = len(tile)
    lines = [(HALO - width + k, jnp.where(lower, cross[k], pair[k]) * masks[0]) for k in range(width)]
    lines += [(HALO + k, tile[k]) for k in range(tile_rows)]
    lines += [(HALO + tile_rows + k, jnp.where(lower, pair[k], cross[k]) * masks[1]) for k in range(width)]
    return lines


def edge_columns(lines, result):
    lane = lax.broadcasted_iota(jnp.int32, result.shape, 1)
    owner = ((lane + 4) // 8) % 16
    for k, line in lines:
        result = jnp.where(owner == k, pltpu.roll(line, (8 * k) % LANES, 1), result)
    return result


def first_lanes(like):
    return lax.broadcasted_iota(jnp.int32, like.shape, 1) % 8 < 4


def from_sides(one, other, paired):
    if not paired:
        return one, other
    lower = first_of_pair("fcol")
    return jnp.where(lower, other, one), jnp.where(lower, one, other)


def first_row(which):
    return sum(HALO - k for k in range(which))


def prepare_kernel(order, dest, base, frac, states, cot, sent, cross, turned, cot_out, dest_v, base_v, frac_v, states_v, sems):
    moves = ((dest, dest_v), (base, base_v), (frac, frac_v), (states, states_v), (cot, cot_out))
    copies = [pltpu.make_async_copy(source, target, sems.at[i]) for i, (source, target) in enumerate(moves)]
    for copy in copies:
        copy.start()
    for copy in copies[:3]:
        copy.wait()
    lines = dest_v.shape[0]
    sent[:lines, :] = dest_v[...].astype(F32)
    sent[lines : 2 * lines, :] = base_v[...].astype(F32)
    for k in range(2):
        for i in range(lines):
            sent[(2 + k) * lines + i : (2 + k) * lines + i + 1, :] = frac_v[k : k + 1, i * LANES : (i + 1) * LANES]
    copies[3].wait()
    _, tile_rows, channels, _ = turned.shape
    lower = first_of_pair()
    for which, source in enumerate(order):
        for r in range(tile_rows):
            turned[which, r] = states_v[source, pl.ds(r, channels, stride=tile_rows), :]
        width = HALO - which
        for k in range(width):
            top, bottom = turned[which, k], turned[which, tile_rows - width + k]
            at = (first_row(which) + k) * channels
            sent[4 * lines + at : 4 * lines + at + channels, :] = jnp.where(lower, bottom, top)
            cross[at : at + channels, :] = jnp.where(lower, top, bottom)
    copies[4].wait()


def prepare(dest, base, frac, states, cot, order, tile_rows):
    channels, points = cot.shape
    columns = states.shape[2]
    stages = len(order)
    rim = first_row(stages) * channels
    lines = points // LANES
    in_hbm = pl.BlockSpec(memory_space=pltpu.HBM)
    return pl.pallas_call(
        functools.partial(prepare_kernel, order),
        in_specs=[in_hbm] * 5,
        out_shape=(
            jax.ShapeDtypeStruct((4 * lines + rim, LANES), F32),
            jax.ShapeDtypeStruct((rim, columns), F32),
            jax.ShapeDtypeStruct((stages, tile_rows, channels, columns), F32),
            jax.ShapeDtypeStruct(cot.shape, F32),
        ),
        scratch_shapes=[
            pltpu.VMEM(dest.shape, jnp.int32),
            pltpu.VMEM(base.shape, jnp.int32),
            pltpu.VMEM(frac.shape, F32),
            pltpu.VMEM(states.shape, F32),
            pltpu.SemaphoreType.DMA((5,)),
        ],
        compiler_params=PARAMS,
        name="prepare",
    )(*(pltpu.with_memory_space_constraint(x, pltpu.HBM) for x in (dest, base, frac, states, cot)))


def state_rows(which, turned, pair, pair_at, cross, lower, masks):
    _, tile_rows, channels, _ = turned.shape
    width = HALO - which

    def rim(ref, start):
        at = [start + (first_row(which) + k) * channels for k in range(width)]
        return [ref[i : i + channels, :] for i in at]

    tile = [turned[which, r] for r in range(tile_rows)]
    return extended_rows(tile, rim(pair, pair_at), rim(cross, 0), width, lower, masks)


def edge_plan(stages, tile_rows):
    plan, lane = [], 0
    for which in range(stages):
        width = HALO - which
        for k in range(HALO - width, HALO + tile_rows + width):
            count = width - max(HALO - k, k - (HALO + tile_rows - 1), 0)
            if count > 0:
                plan.append((which, k, count, lane))
                lane += count
    return plan


def state_edges(n_row, turned, pair, pair_at, cross):
    stages, tile_rows, channels, _ = turned.shape
    lower, masks = first_of_pair(), row_masks(n_row)
    lane = lax.broadcasted_iota(jnp.int32, (channels, LANES), 1)
    first = last = jnp.zeros((channels, LANES), F32)
    lines = [dict(state_rows(which, turned, pair, pair_at, cross, lower, masks)) for which in range(stages)]
    for which, k, count, at in edge_plan(stages, tile_rows):
        here = (lane >= at) & (lane < at + count)
        first = jnp.where(here, pltpu.roll(lines[which][k], at, 1), first)
        last = jnp.where(here, pltpu.roll(lines[which][k], (at + count) % LANES, 1), last)
    return first, last


def state_edges_kernel(n_row, pair_at, paired, turned, pair, cross, *refs):
    one, other = refs[-2:]
    first, last = state_edges(n_row, turned, pair, pair_at, cross)
    if paired:
        lower = first_of_pair("fcol")
        first, last = jnp.where(lower, last, first), jnp.where(lower, first, last)
    one[...], other[...] = first, last


def all_state_edges(n_row, pair_at, paired, turned, pair, cross, after=()):
    return pl.pallas_call(
        functools.partial(state_edges_kernel, n_row, pair_at, paired),
        out_shape=[jax.ShapeDtypeStruct((turned.shape[2], LANES), F32)] * 2,
        compiler_params=PARAMS,
        name="state_edges",
    )(turned, pair, cross, *after)


FIELDS = 7


def stage_weight(which):
    return 0.5 * time_step if which % 2 == 0 else time_step


def store_fields(wide, which, lines, levels, base_row, total_rows):
    weight = stage_weight(which)
    channels = 3 * levels
    for k, line in lines:
        wide[which, k, :channels, :] = (0.5 * weight) * line
    winds = slice(levels, channels)
    for k in range(lines[0][0] + 1, lines[-1][0]):
        values = wide[which, k, winds, :]
        change = pltpu.roll(values, LANES - 1, 1) - pltpu.roll(values, 1, 1)
        slope = wide[which, k + 1, winds, :] - wide[which, k - 1, winds, :]
        rotation = weight * (coriolis_peak * (2.0 * ((base_row + k - HALO).astype(F32) + 0.5) / total_rows - 1.0))
        begin = channels
        for value in (change[:levels], change[levels:] + rotation, slope[:levels] - rotation, slope[levels:]):
            wide[which, k, begin : begin + levels, :] = value
            begin += levels


def tile_fields_kernel(n_row, pair_at, turned, pair, cross, gravity, *refs):
    wide, pull = refs[-2:]
    stages, tile_rows, channels, _ = turned.shape
    levels = channels // 3
    level = lax.broadcasted_iota(jnp.int32, pull.shape, 0)
    pulls = jnp.zeros(pull.shape, F32)
    for i in range(levels):
        pulls = jnp.where(level == i, gravity[i], pulls)
    pull[...] = pulls
    lower, masks = first_of_pair(), row_masks(n_row)
    for which in range(stages):
        lines = state_rows(which, turned, pair, pair_at, cross, lower, masks)
        store_fields(wide, which, lines, levels, lax.axis_index("frow") * tile_rows, tile_rows * n_row)


def tile_fields(n_row, pair_at, turned, pair, cross, gravity, after=()):
    stages, tile_rows, channels, columns = turned.shape
    in_vmem = pl.BlockSpec(memory_space=pltpu.VMEM)
    return pl.pallas_call(
        functools.partial(tile_fields_kernel, n_row, pair_at),
        in_specs=[in_vmem] * 3 + [pl.BlockSpec(memory_space=pltpu.SMEM)] + [in_vmem] * len(after),
        out_shape=(
            jax.ShapeDtypeStruct((stages, tile_rows + 2 * HALO, channels // 3 * FIELDS, columns), F32),
            jax.ShapeDtypeStruct((channels // 3, columns), F32),
        ),
        compiler_params=PARAMS,
        name="tile_fields",
    )(turned, pair, cross, gravity, *after)


PART = 8
BEYOND_AT = 32


def edge_windows(line):
    lane = lax.broadcasted_iota(jnp.int32, line.shape, 1)
    return jnp.where((lane >= BEYOND_AT // 2) & (lane < 2 * BEYOND_AT), pltpu.roll(line, BEYOND_AT, 1), line)


def with_rim(window, rim):
    lane = lax.broadcasted_iota(jnp.int32, window.shape, 1)
    beyond = (lane >= LANES - HALO) | ((lane >= BEYOND_AT) & (lane < BEYOND_AT + HALO))
    return jnp.where(beyond, rim, window)


def edge_fields_kernel(n_row, pair_at, paired, turned, pair, cross, one, other, wide):
    stages, tile_rows, channels, columns = turned.shape
    lower, masks = first_of_pair(), row_masks(n_row)
    left, right = from_sides(one[...], other[...], paired)
    lane = lax.broadcasted_iota(jnp.int32, (channels, columns), 1)
    rims = {
        (which, k): jnp.where(
            lane < columns // 2,
            pltpu.roll(right, (BEYOND_AT - at) % columns, 1),
            pltpu.roll(left, (-at - count) % columns, 1),
        )
        for which, k, count, at in edge_plan(stages, tile_rows)
    }
    for which in range(stages):
        lines = [
            (k, with_rim(edge_windows(line), rims.get((which, k), line)))
            for k, line in state_rows(which, turned, pair, pair_at, cross, lower, masks)
        ]
        store_fields(wide, which, lines, channels // 3, lax.axis_index("frow") * tile_rows, tile_rows * n_row)


def edge_fields(n_row, pair_at, paired, turned, pair, cross, one, other):
    stages, tile_rows, channels, columns = turned.shape
    return pl.pallas_call(
        functools.partial(edge_fields_kernel, n_row, pair_at, paired),
        out_shape=jax.ShapeDtypeStruct((stages, tile_rows + 2 * HALO, channels // 3 * FIELDS, columns), F32),
        compiler_params=PARAMS,
        name="edge_fields",
    )(turned, pair, cross, one, other)


def slot_blocks(cot, where, tiles, share, groups, tile_rows, columns, onehot, parts):
    channels, points = cot.shape
    lines = points // LANES
    named_tiles = tiles.shape[0]
    corner = where[lines : 2 * lines, :]
    row = jnp.zeros_like(corner)
    for k in range(1, tile_rows - 1):
        row = row + (corner >= float(k * (columns - 1))).astype(F32)
    col = corner - row * float(columns - 1)
    target = where[:lines, :]
    offsets = [where[k * lines : (k + 1) * lines, :] for k in (2, 3)]

    before = (
        lax.broadcasted_iota(jnp.int32, (GROUP, GROUP), 0)
        < lax.broadcasted_iota(jnp.int32, (GROUP, GROUP), 1)
    ).astype(F32).astype(BF16)
    index = lax.broadcasted_iota(jnp.int32, tiles.shape, 0)
    begin = ((index % share) * (GROUP // share)).astype(F32)
    slots = lax.broadcasted_iota(jnp.int32, (GROUP, GROUP), 0).astype(F32).astype(BF16)
    one, zero = jnp.ones(slots.shape, BF16), jnp.zeros(slots.shape, BF16)
    count = jnp.zeros((named_tiles, 1), F32)
    rows = channels + 8

    def across(values, b):
        return jnp.concatenate([values[2 * b : 2 * b + 1, :], values[2 * b + 1 : 2 * b + 2, :]], axis=1)

    all_named = [(tiles == across(target, b)).astype(F32) for b in range(points // GROUP)]
    all_ahead = jnp.dot(jnp.concatenate(all_named, axis=0).astype(BF16), before, preferred_element_type=F32)
    for b, named in enumerate(all_named):
        part = slice(b * GROUP, (b + 1) * GROUP)
        ahead = all_ahead[b * named_tiles : (b + 1) * named_tiles, :]
        lane = jnp.sum(named * (ahead + count + begin), axis=0, keepdims=True)
        count = count + jnp.sum(named, axis=1, keepdims=True)
        onehot[:, part] = jnp.where(slots == lane.astype(BF16), one, zero)
        coords = [across(values, b) for values in (row, col, *offsets)]
        data_high, data_low = split(jnp.concatenate([cot[:, part], *coords, *coords], axis=0))
        for g in range(groups):
            mine = named[g * share : g * share + 1, :]
            for i in range(1, share):
                mine = mine + named[g * share + i : g * share + i + 1, :]
            mine = mine.astype(BF16)
            parts[g * rows : (g + 1) * rows, part] = data_high * mine
            parts[(groups + g) * rows : (groups + g + 1) * rows, part] = data_low * mine
    both = dot_nt(parts[...], onehot[...])
    packed = both[: groups * rows, :] + both[groups * rows :, :]
    upper = lax.broadcasted_iota(jnp.int32, (8, LANES), 0) < 4
    for g in range(groups):
        block = packed[g * rows : (g + 1) * rows, :]
        yield (
            block[:channels, :LANES],
            block[:channels, LANES:],
            jnp.where(upper, block[channels:, :LANES], block[channels:, LANES:]),
        )


def store_block(out, at, pieces):
    channels = pieces[0].shape[0]
    out[at : at + channels, :] = pieces[0]
    out[at + channels : at + 2 * channels, :] = pieces[1]
    out[at + 2 * channels : at + 2 * channels + 8, :] = pieces[2]


def pack_scratch(channels, points, groups):
    return [
        pltpu.VMEM((GROUP, points), BF16),
        pltpu.VMEM((2 * groups * (channels + 8), points), BF16),
    ]


def pack_all_kernel(tile_count, share, tile_rows, columns, cot, where, out, *scratch):
    tiles = lax.broadcasted_iota(jnp.int32, (tile_count, GROUP), 0).astype(F32)
    for g, pieces in enumerate(slot_blocks(cot, where, tiles, share, tile_count // share, tile_rows, columns, *scratch)):
        store_block(out.at[g], 0, pieces)


def pack_all(cot, where, tile_count, share, tile_rows, columns):
    channels, points = cot.shape
    groups = tile_count // share
    return pl.pallas_call(
        functools.partial(pack_all_kernel, tile_count, share, tile_rows, columns),
        out_shape=jax.ShapeDtypeStruct((groups, 2 * channels + 8, LANES), F32),
        scratch_shapes=pack_scratch(channels, points, groups),
        compiler_params=PARAMS,
        name="pack_points",
    )(cot, where)


NEAR = ((0, 0), (2, 0), (0, 1), (2, 1))
FAR = ((0, 2), (2, 2), (0, 3), (2, 3))


def partner_tiles(partners):
    at_row, at_col = lax.axis_index("frow"), lax.axis_index("fcol")
    n_col = lax.axis_size("fcol")
    index = lax.broadcasted_iota(jnp.int32, (8, GROUP), 0)
    tiles = jnp.full(index.shape, -1, jnp.int32)
    for g, (df, dz) in enumerate(partners):
        tiles = jnp.where(index == g, (at_row ^ df) * n_col + (at_col ^ dz), tiles)
    return tiles.astype(F32)


def pack_chip_kernel(tiles, tile_rows, columns, cot, where, pair_cot, pair_where, *refs):
    outs, scratch = refs[-4 - len(tiles) : -4], refs[-4:]
    begin = 0
    for i, points in enumerate(((cot, where), (pair_cot, pair_where))):
        blocks = slot_blocks(
            *points, partner_tiles(tiles), 1, len(tiles), tile_rows, columns, *scratch[2 * i : 2 * i + 2]
        )
        for out, pieces in zip(outs, blocks):
            store_block(out, begin, pieces)
        begin += 2 * cot.shape[0] + 8


def pack_chip(tiles, points, tile_rows, columns, after=()):
    channels, count = points[0].shape
    return pl.pallas_call(
        functools.partial(pack_chip_kernel, tiles, tile_rows, columns),
        out_shape=[jax.ShapeDtypeStruct((2 * (2 * channels + 8), LANES), F32)] * len(tiles),
        scratch_shapes=pack_scratch(channels, count, len(tiles)) * 2,
        compiler_params=PARAMS,
        name="pack_chip",
    )(*points, *after)


def scatter_kernel(count, first, later, *refs):
    blocks, refs = refs[:count], refs[count:]
    if not first:
        total, refs = refs[0], refs[1:]
    outs, scratch = refs[later : -2 * count], refs[-2 * count :]
    part_rows, channels, columns = outs[0].shape
    tile_rows = part_rows * len(outs)
    rows = 2 * channels + 8
    cells = lax.broadcasted_iota(jnp.int32, (columns, LANES), 0).astype(F32).astype(BF16)
    zero = jnp.zeros((channels, LANES), BF16)

    def spread(values, shape):
        return jnp.broadcast_to(values.astype(BF16), shape)

    sums = None
    for block, parts, weight in zip(blocks, scratch[::2], scratch[1::2]):
        at = 0
        for source in range(block.shape[0] // rows):
            for half in range(2):
                part = slice(at, at + LANES)
                at += LANES
                begin = source * rows + 2 * channels + 4 * half
                coords = block[begin : begin + 4, :]
                row, col, along_rows, along_cols = (coords[k : k + 1, :] for k in range(4))
                corner, beside = cells == spread(col, cells.shape), cells == spread(col + 1.0, cells.shape)
                for k, (near, far) in enumerate(zip(split(1.0 - along_cols), split(along_cols))):
                    chosen = jnp.where(
                        beside, spread(far, cells.shape), jnp.zeros(cells.shape, BF16)
                    )
                    weight[k * columns : (k + 1) * columns, part] = jnp.where(corner, spread(near, cells.shape), chosen)
                begin = source * rows + half * channels
                values = block[begin : begin + channels, :]
                upper, lower = split(values * (1.0 - along_rows)), split(values * along_rows)
                below = None
                line = spread(row, zero.shape)
                for r in range(tile_rows):
                    here = line == jnp.full(zero.shape, r, BF16)
                    for k in range(2):
                        product = zero if below is None else jnp.where(below, lower[k], zero)
                        product = jnp.where(here, upper[k], product)
                        begin = (k * tile_rows + r) * channels
                        parts[begin : begin + channels, part] = product
                    below = here
        both = dot_nt(parts[...], weight[...])
        both = both[:, :columns] + both[:, columns:]
        both = both[: tile_rows * channels, :] + both[tile_rows * channels :, :]
        sums = both if sums is None else sums + both
    for r in range(tile_rows):
        line = sums[r * channels : (r + 1) * channels, :]
        if not first:
            line = line + total[r]
        outs[r // part_rows][r % part_rows] = line


def scatter(blocks, total, channels, tile_rows, columns, after=(), parts=1):
    slots = [block.shape[0] // (2 * channels + 8) * GROUP for block in blocks]
    return pl.pallas_call(
        functools.partial(scatter_kernel, len(blocks), total is None, len(after)),
        out_shape=[jax.ShapeDtypeStruct((tile_rows // parts, channels, columns), F32)] * parts,
        scratch_shapes=[
            pltpu.VMEM((2 * lines, count), BF16) for count in slots for lines in (tile_rows * channels, columns)
        ],
        compiler_params=PARAMS,
        name="scatter_points",
    )(*blocks, *([] if total is None else [total]), *after)


def finish_kernel(count, total, *refs):
    parts, (canvas, to_pair, to_cross) = refs[:count], refs[-3:]
    tile_rows = canvas.shape[0]
    for r in range(tile_rows):
        line = total[r]
        if parts:
            size = parts[0].shape[0]
            line = line + parts[r // size][r % size]
        canvas[r] = line
    lower = first_of_pair()
    for k in range(HALO):
        top, bottom = canvas[k], canvas[tile_rows - HALO + k]
        to_pair[k] = jnp.where(lower, bottom, top)
        to_cross[k] = jnp.where(lower, top, bottom)


def finish(total, parts=(), after=()):
    _, channels, columns = total.shape
    rim = jax.ShapeDtypeStruct((HALO, channels, columns), F32)
    return pl.pallas_call(
        functools.partial(finish_kernel, len(parts)),
        out_shape=(jax.ShapeDtypeStruct(total.shape, F32), rim, rim),
        compiler_params=PARAMS,
        name="finish_canvas",
    )(total, *parts, *after)


def adjoint_rows(n_row, canvas, pair, cross):
    tile = [canvas[r] for r in range(canvas.shape[0])]
    rims = ([ref[k] for k in range(HALO)] for ref in (pair, cross))
    return extended_rows(tile, *rims, HALO, first_of_pair(), row_masks(n_row))


def cross_edges_kernel(canvas, cross, *refs):
    edges = refs[-1]
    lower = first_of_pair()
    tile_rows = canvas.shape[0]
    empty = jnp.zeros(edges.shape, F32)
    lines = [(k, jnp.where(lower, cross[k], empty)) for k in range(HALO)]
    lines += [(HALO + r, canvas[r]) for r in range(tile_rows)]
    lines += [(HALO + tile_rows + k, jnp.where(lower, empty, cross[k])) for k in range(HALO)]
    edges[...] = edge_columns(lines, empty)


def pair_edges_kernel(n_row, tile_rows, partial, pair, edges):
    lower, masks = first_of_pair(), row_masks(n_row)
    result = partial[...]
    empty = jnp.zeros(edges.shape, F32)
    lane = lax.broadcasted_iota(jnp.int32, edges.shape, 1)
    row = ((lane + 4) // 8) % 16
    result = jnp.where(row < HALO, masks[0], jnp.where(row < HALO + tile_rows, 1.0, masks[1])) * result
    lines = [(k, jnp.where(lower, empty, pair[k])) for k in range(HALO)]
    lines += [(HALO + tile_rows + k, jnp.where(lower, pair[k], empty)) for k in range(HALO)]
    edges[...] = result + edge_columns(lines, empty)


def adjoint_edges(n_row, canvas, pair, cross, after=()):
    tile_rows, channels, _ = canvas.shape
    edges = jax.ShapeDtypeStruct((channels, LANES), F32)
    partial = pl.pallas_call(
        cross_edges_kernel, out_shape=edges, compiler_params=PARAMS, name="cross_edges"
    )(canvas, cross, *after)
    return pl.pallas_call(
        functools.partial(pair_edges_kernel, n_row, tile_rows),
        out_shape=edges,
        compiler_params=PARAMS,
        name="pair_edges",
    )(partial, pair)


def run_stages(wide, gravity, levels, masks, tile_rows, buffers, store):
    start, middle, after, last = buffers

    def along_x(values):
        return pltpu.roll(values, LANES - 1, 1) - pltpu.roll(values, 1, 1)

    def run(stage, adjoint, put):
        width = HALO - 1 - stage
        begin, end = HALO - width, HALO + tile_rows + width
        for low in range(0, levels, PART):
            pull = (0.5 * stage_weight(stage)) * gravity[low : low + PART, :]

            def state(k, which):
                return wide[stage, k, which * levels + low : which * levels + low + PART, :]

            def line(k):
                a, b, c = (adjoint[k, w * levels + low : w * levels + low + PART, :] for w in range(3))
                v = state(k, 2)
                return a, b, c, v, v * b, v * c

            up, here = line(begin - 1), line(begin)
            for k in range(begin, end):
                down = line(k + 1)
                a, b, c, v = here[:4]
                h, u = state(k, 0), state(k, 1)
                a_x, a_y = along_x(a), down[0] - up[0]
                height = u * a_x + v * a_y + pull * (along_x(b) + (down[2] - up[2]))
                east = h * a_x + along_x(u * b) + (down[4] - up[4]) - b * state(k, 3) - c * state(k, 4)
                north = h * a_y + along_x(u * c) + (down[5] - up[5]) - b * state(k, 5) - c * state(k, 6)
                for w, (old, change) in enumerate(zip((a, b, c), (height, east, north))):
                    put(k, w, low, old, change)
                up, here = here, down

    def kept(k, value):
        if k < HALO:
            return value * masks[0]
        if k >= HALO + tile_rows:
            return value * masks[1]
        return value

    def half_into(result):
        def put(k, w, low, old, change):
            result[k, w * levels + low : w * levels + low + PART, :] = kept(k, 0.5 * old + change)

        return put

    def after_step(adjoint, k, w, low, old, change):
        return 0.5 * adjoint[k, w * levels + low : w * levels + low + PART, :] + old + change

    def to_after(k, w, low, old, change):
        after[k, w * levels + low : w * levels + low + PART, :] = kept(k, after_step(start, k, w, low, old, change))

    def to_end(k, w, low, old, change):
        store(k - HALO, w, low, after_step(after, k, w, low, old, change))

    run(0, start, half_into(middle))
    run(1, middle, to_after)
    run(2, after, half_into(last))
    run(3, last, to_end)


def tile_steps_kernel(n_row, canvas, pair, cross, wide, gravity, out, windows, *buffers):
    tile_rows, channels, _ = canvas.shape
    levels = channels // 3
    for k, line in adjoint_rows(n_row, canvas, pair, cross):
        buffers[0][k] = line
        windows[k] = edge_windows(line)

    def store(r, w, low, value):
        out[r, w * levels + low : w * levels + low + PART, :] = value

    run_stages(wide, gravity, levels, row_masks(n_row), tile_rows, buffers, store)


def tile_steps(n_row, canvas, pair, cross, wide, gravity):
    tile_rows, channels, columns = canvas.shape
    return pl.pallas_call(
        functools.partial(tile_steps_kernel, n_row),
        out_shape=(
            jax.ShapeDtypeStruct(canvas.shape, F32),
            jax.ShapeDtypeStruct((tile_rows + 2 * HALO, channels, columns), F32),
        ),
        scratch_shapes=[pltpu.VMEM((tile_rows + 2 * HALO, channels, columns), F32)] * 4,
        compiler_params=PARAMS,
        name="tile_steps",
    )(canvas, pair, cross, wide, gravity)


def edge_steps_kernel(n_row, paired, windows, one, other, wide, gravity, inner, out, *buffers):
    *buffers, result = buffers
    tile_rows, channels, _ = inner.shape
    levels = channels // 3
    left, right = from_sides(one[...], other[...], paired)
    rims = jnp.where(first_lanes(left), pltpu.roll(right, BEYOND_AT, 1), left)
    for k in range(tile_rows + 2 * HALO):
        buffers[0][k] = with_rim(windows[k], pltpu.roll(rims, (-8 * k) % LANES, 1))
    lane = lax.broadcasted_iota(jnp.int32, (PART, LANES), 1)

    def store(r, w, low, value):
        result[r, w * levels + low : w * levels + low + PART, :] = value

    run_stages(wide, gravity, levels, row_masks(n_row), tile_rows, buffers, store)
    for r in range(tile_rows):
        for begin in range(0, channels, PART):
            value = result[r, begin : begin + PART, :]
            final = pltpu.roll(value, LANES - BEYOND_AT, 1)
            line = jnp.where(lane >= LANES - HALO, final, inner[r, begin : begin + PART, :])
            out[pl.ds(begin * tile_rows + r, PART, stride=tile_rows), :] = jnp.where(lane < HALO, value, line)


def edge_steps(n_row, paired, windows, one, other, wide, gravity, inner):
    tile_rows, channels, columns = inner.shape
    return pl.pallas_call(
        functools.partial(edge_steps_kernel, n_row, paired),
        out_shape=jax.ShapeDtypeStruct((channels * tile_rows, columns), F32),
        scratch_shapes=[pltpu.VMEM(windows.shape, F32)] * 4 + [pltpu.VMEM(inner.shape, F32)],
        compiler_params=PARAMS,
        name="edge_steps",
    )(windows, one, other, wide, gravity, inner)


def shifted(values, axis, by):
    count = lax.axis_size(axis)
    return lax.ppermute(values, axis, [(i, (i + by) % count) for i in range(count)])


def exchanged(values, offset):
    n_row, n_col = lax.axis_size("frow"), lax.axis_size("fcol")
    df, dz = offset
    pairs = [(f * n_col + z, (f ^ df) * n_col + (z ^ dz)) for f in range(n_row) for z in range(n_col)]
    return lax.ppermute(values, ("frow", "fcol"), pairs)


def exchanged_across(values):
    n_row = lax.axis_size("frow")
    return lax.ppermute(values, "frow", [(f, ((f + 1) ^ 1) - 1) for f in range(1, n_row - 1)])


def from_everyone(packed, channels, tile_count):
    groups = packed.shape[0]
    rows = channels + 4
    halves = [
        jnp.concatenate(
            [
                packed[:, h * channels : (h + 1) * channels],
                packed[:, 2 * channels + 4 * h : 2 * channels + 4 * h + 4],
            ],
            axis=1,
        )
        for h in range(2)
    ]
    slots = jnp.stack(halves, axis=2).transpose(1, 0, 2, 3).reshape(rows, tile_count, -1)
    slots = lax.all_to_all(slots, ("frow", "fcol"), split_axis=1, concat_axis=1, tiled=True)
    slots = slots.reshape(rows, groups, 2, LANES).transpose(1, 2, 0, 3)
    return jnp.concatenate(
        [slots[:, 0, :channels], slots[:, 1, :channels], slots[:, 0, channels:], slots[:, 1, channels:]], axis=1
    )


def per_device(latlon_cot, dest_tile, base_cell, corner_frac, saved_states, gravity):
    n_row, n_col = lax.axis_size("frow"), lax.axis_size("fcol")
    tile_count = n_row * n_col
    levels = gravity.shape[0]
    tile_rows = saved_states.shape[4]
    columns = saved_states.shape[5]
    channels = 3 * levels
    points = base_cell.shape[0]
    lines = points // LANES
    share = GROUP * tile_count // (2 * points)
    paired = share == 1 and n_row == 4 and n_col == 4
    size = (channels, tile_rows, columns)

    cot = latlon_cot.reshape(channels, points)
    partner_cot = exchanged(cot, (1, 0)) if paired else None
    sent, to_cross, turned, cot = prepare(
        dest_tile.reshape(lines, LANES),
        base_cell.reshape(lines, LANES),
        corner_frac,
        saved_states.reshape(4, channels * tile_rows, columns),
        cot,
        (3, 2, 1, 0),
        tile_rows,
    )
    pair_at = 4 * lines
    pair = exchanged(sent, (1, 0))
    cross = exchanged_across(to_cross)
    if paired:
        chip_points = cot, sent, partner_cot, pair
        packed = pack_chip(FAR, chip_points, tile_rows, columns)
        got = [packed[0]] + [exchanged(block, (df, dz ^ 2)) for block, (df, dz) in zip(packed[1:], FAR[1:])]
        packed = pack_chip(NEAR, chip_points, tile_rows, columns, [cross, packed[0]])
        total = scatter(got[:2], None, *size, packed[:1])[0]
        sums = scatter(got[2:], total, *size, parts=2)
        far = [exchanged(part, (0, 2)) for part in sums]
        got = [packed[0]] + [exchanged(block, tile) for block, tile in zip(packed[1:], NEAR[1:])]
        one, other = all_state_edges(n_row, pair_at, paired, turned, pair, cross, sums)
        one, other = exchanged(one, (0, 1)), exchanged(other, (0, 3))
        total = scatter(got[:2], None, *size)[0]
        total = scatter(got[2:], total, *size)[0]
        fields, pull = tile_fields(n_row, pair_at, turned, pair, cross, gravity, [total])
        canvas = finish(total, far, [one, other, pull])
    else:
        packed = pack_all(cot, sent, tile_count, share, tile_rows, columns)
        got = from_everyone(packed, channels, tile_count)
        one, other = all_state_edges(n_row, pair_at, paired, turned, pair, cross)
        one, other = shifted(one, "fcol", 1), shifted(other, "fcol", -1)
        fields, pull = tile_fields(n_row, pair_at, turned, pair, cross, gravity)
        canvas = finish(scatter([got.reshape(-1, LANES)], None, *size)[0])

    near_edges = edge_fields(n_row, pair_at, paired, turned, pair, cross, one, other)
    canvas, to_pair, to_cross = canvas
    pair, cross = exchanged(to_pair, (1, 0)), exchanged_across(to_cross)
    edges = adjoint_edges(n_row, canvas, pair, cross, [near_edges])
    if paired:
        sides = exchanged(edges, (0, 1)), exchanged(edges, (0, 3))
    else:
        sides = shifted(edges, "fcol", 1), shifted(edges, "fcol", -1)
    inner, windows = tile_steps(n_row, canvas, pair, cross, fields, pull)
    result = edge_steps(n_row, paired, windows, *sides, near_edges, pull, inner)
    return result.reshape(3, levels, tile_rows, columns)


def solution(mesh):
    placed = (
        P(None, None, ("member", "frow", "fcol")),
        P(("frow", "fcol"), None),
        P(("frow", "fcol")),
        P(None, ("frow", "fcol")),
        P(None, None, None, None, ("member", "frow"), "fcol"),
        P(),
    )
    return jax.shard_map(
        per_device,
        mesh=mesh,
        in_specs=placed,
        out_specs=P(None, None, ("member", "frow"), "fcol"),
        check_vma=False,
    )
```

```python
import functools

import jax
import jax.numpy as jnp
from jax import lax
from jax.experimental import pallas as pl
from jax.experimental.pallas import tpu as pltpu
from jax.sharding import PartitionSpec as P

time_step = 0.25
coriolis_peak = 0.8

HALO = 4
GROUP = 256
LANES = 128
F32 = jnp.float32
BF16 = jnp.bfloat16
PARAMS = pltpu.CompilerParams(vmem_limit_bytes=16 * 1024 * 1024)


def split(values):
    high = values.astype(BF16)
    return high, (values - high.astype(F32)).astype(BF16)


def dot_nt(a, b):
    return lax.dot_general(a, b, (((1,), (1,)), ((), ())), preferred_element_type=F32)


def first_of_pair(axis="frow"):
    return lax.rem(lax.axis_index(axis), 2) == 0


def row_masks(n_row):
    at = lax.axis_index("frow")
    return jnp.where(at > 0, 1.0, 0.0).astype(F32), jnp.where(at < n_row - 1, 1.0, 0.0).astype(F32)


def extended_rows(tile, pair, cross, width, lower, masks):
    tile_rows = len(tile)
    lines = [(HALO - width + k, jnp.where(lower, cross[k], pair[k]) * masks[0]) for k in range(width)]
    lines += [(HALO + k, tile[k]) for k in range(tile_rows)]
    lines += [(HALO + tile_rows + k, jnp.where(lower, pair[k], cross[k]) * masks[1]) for k in range(width)]
    return lines


def edge_columns(lines, result):
    lane = lax.broadcasted_iota(jnp.int32, result.shape, 1)
    owner = ((lane + 4) // 8) % 16
    for k, line in lines:
        result = jnp.where(owner == k, pltpu.roll(line, (8 * k) % LANES, 1), result)
    return result


def first_lanes(like):
    return lax.broadcasted_iota(jnp.int32, like.shape, 1) % 8 < 4


def from_sides(one, other, paired):
    if not paired:
        return one, other
    lower = first_of_pair("fcol")
    return jnp.where(lower, other, one), jnp.where(lower, one, other)


def first_row(which):
    return sum(HALO - k for k in range(which))


def prepare_kernel(order, dest, base, frac, states, cot, sent, cross, turned, cot_out, dest_v, base_v, frac_v, states_v, sems):
    moves = ((dest, dest_v), (base, base_v), (frac, frac_v), (states, states_v), (cot, cot_out))
    copies = [pltpu.make_async_copy(source, target, sems.at[i]) for i, (source, target) in enumerate(moves)]
    for copy in copies:
        copy.start()
    for copy in copies[:3]:
        copy.wait()
    lines = dest_v.shape[0]
    sent[:lines, :] = dest_v[...].astype(F32)
    sent[lines : 2 * lines, :] = base_v[...].astype(F32)
    for k in range(2):
        for i in range(lines):
            sent[(2 + k) * lines + i : (2 + k) * lines + i + 1, :] = frac_v[k : k + 1, i * LANES : (i + 1) * LANES]
    copies[3].wait()
    _, tile_rows, channels, _ = turned.shape
    lower = first_of_pair()
    for which, source in enumerate(order):
        for r in range(tile_rows):
            turned[which, r] = states_v[source, pl.ds(r, channels, stride=tile_rows), :]
        width = HALO - which
        for k in range(width):
            top, bottom = turned[which, k], turned[which, tile_rows - width + k]
            at = (first_row(which) + k) * channels
            sent[4 * lines + at : 4 * lines + at + channels, :] = jnp.where(lower, bottom, top)
            cross[at : at + channels, :] = jnp.where(lower, top, bottom)
    copies[4].wait()


def prepare(dest, base, frac, states, cot, order, tile_rows):
    channels, points = cot.shape
    columns = states.shape[2]
    stages = len(order)
    rim = first_row(stages) * channels
    lines = points // LANES
    in_hbm = pl.BlockSpec(memory_space=pltpu.HBM)
    return pl.pallas_call(
        functools.partial(prepare_kernel, order),
        in_specs=[in_hbm] * 5,
        out_shape=(
            jax.ShapeDtypeStruct((4 * lines + rim, LANES), F32),
            jax.ShapeDtypeStruct((rim, columns), F32),
            jax.ShapeDtypeStruct((stages, tile_rows, channels, columns), F32),
            jax.ShapeDtypeStruct(cot.shape, F32),
        ),
        scratch_shapes=[
            pltpu.VMEM(dest.shape, jnp.int32),
            pltpu.VMEM(base.shape, jnp.int32),
            pltpu.VMEM(frac.shape, F32),
            pltpu.VMEM(states.shape, F32),
            pltpu.SemaphoreType.DMA((5,)),
        ],
        compiler_params=PARAMS,
        name="prepare",
    )(*(pltpu.with_memory_space_constraint(x, pltpu.HBM) for x in (dest, base, frac, states, cot)))


def state_rows(which, turned, pair, pair_at, cross, lower, masks):
    _, tile_rows, channels, _ = turned.shape
    width = HALO - which

    def rim(ref, start):
        at = [start + (first_row(which) + k) * channels for k in range(width)]
        return [ref[i : i + channels, :] for i in at]

    tile = [turned[which, r] for r in range(tile_rows)]
    return extended_rows(tile, rim(pair, pair_at), rim(cross, 0), width, lower, masks)


def edge_plan(stages, tile_rows):
    plan, lane = [], 0
    for which in range(stages):
        width = HALO - which
        for k in range(HALO - width, HALO + tile_rows + width):
            count = width - max(HALO - k, k - (HALO + tile_rows - 1), 0)
            if count > 0:
                plan.append((which, k, count, lane))
                lane += count
    return plan


def state_edges(n_row, turned, pair, pair_at, cross):
    stages, tile_rows, channels, _ = turned.shape
    lower, masks = first_of_pair(), row_masks(n_row)
    lane = lax.broadcasted_iota(jnp.int32, (channels, LANES), 1)
    first = last = jnp.zeros((channels, LANES), F32)
    lines = [dict(state_rows(which, turned, pair, pair_at, cross, lower, masks)) for which in range(stages)]
    for which, k, count, at in edge_plan(stages, tile_rows):
        here = (lane >= at) & (lane < at + count)
        first = jnp.where(here, pltpu.roll(lines[which][k], at, 1), first)
        last = jnp.where(here, pltpu.roll(lines[which][k], (at + count) % LANES, 1), last)
    return first, last


def state_edges_kernel(n_row, pair_at, paired, turned, pair, cross, *refs):
    one, other = refs[-2:]
    first, last = state_edges(n_row, turned, pair, pair_at, cross)
    if paired:
        lower = first_of_pair("fcol")
        first, last = jnp.where(lower, last, first), jnp.where(lower, first, last)
    one[...], other[...] = first, last


def all_state_edges(n_row, pair_at, paired, turned, pair, cross, after=()):
    return pl.pallas_call(
        functools.partial(state_edges_kernel, n_row, pair_at, paired),
        out_shape=[jax.ShapeDtypeStruct((turned.shape[2], LANES), F32)] * 2,
        compiler_params=PARAMS,
        name="state_edges",
    )(turned, pair, cross, *after)


FIELDS = 7


def stage_weight(which):
    return 0.5 * time_step if which % 2 == 0 else time_step


def store_fields(wide, which, lines, levels, base_row, total_rows, own=None):
    weight = stage_weight(which)
    channels = 3 * levels
    for k, line in lines:
        wide[which, k, :channels, :] = (0.5 * weight) * line
        if own is not None:
            own[which, k] = edge_windows(line)
    winds = slice(levels, channels)
    for k in range(lines[0][0] + 1, lines[-1][0]):
        values = wide[which, k, winds, :]
        change = pltpu.roll(values, LANES - 1, 1) - pltpu.roll(values, 1, 1)
        slope = wide[which, k + 1, winds, :] - wide[which, k - 1, winds, :]
        rotation = weight * (coriolis_peak * (2.0 * ((base_row + k - HALO).astype(F32) + 0.5) / total_rows - 1.0))
        begin = channels
        for value in (change[:levels], change[levels:] + rotation, slope[:levels] - rotation, slope[levels:]):
            wide[which, k, begin : begin + levels, :] = value
            begin += levels


PART = 8
BEYOND_AT = 32
TURN = LANES // 2


def ring_lanes():
    return lax.broadcasted_iota(jnp.int32, (PART, LANES), 1)


def by_half(values, ring):
    lane = ring_lanes()
    second = (lane >= TURN - LANES // 8) & (lane < LANES - LANES // 8)
    fields = []
    for begin in range(0, values.shape[0], 2 * PART):
        first, last = values[begin : begin + PART], values[begin + PART : begin + 2 * PART]
        fields.append(jnp.where(second, ring(last, TURN), ring(first, 0)))
    return jnp.concatenate(fields, axis=0)


def turned_by(values, shift):
    shift %= LANES
    return pltpu.roll(values, shift, 1) if shift else values


def edge_windows(line):
    lane = ring_lanes()

    def ring(values, turn):
        ends = (lane >= turn + BEYOND_AT // 2) & (lane < turn + BEYOND_AT)
        return jnp.where(ends, turned_by(values, BEYOND_AT + turn), turned_by(values, turn))

    return by_half(line, ring)


def with_rim(window, rim):
    lane = lax.broadcasted_iota(jnp.int32, window.shape, 1) % TURN
    beyond = (lane >= TURN - HALO) | ((lane >= BEYOND_AT) & (lane < BEYOND_AT + HALO))
    return jnp.where(beyond, rim, window)


def tile_fields_kernel(n_row, pair_at, turned, pair, cross, gravity, *refs):
    wide, pull, edge_pull, own = refs[-4:]
    stages, tile_rows, channels, _ = turned.shape
    levels = channels // 3
    level = lax.broadcasted_iota(jnp.int32, pull.shape, 0)
    pulls = jnp.zeros(pull.shape, F32)
    for i in range(levels):
        pulls = jnp.where(level == i, gravity[i], pulls)
    pull[...] = pulls
    edge_pull[...] = by_half(pulls, lambda values, _: values)
    lower, masks = first_of_pair(), row_masks(n_row)
    for which in range(stages):
        lines = state_rows(which, turned, pair, pair_at, cross, lower, masks)
        store_fields(wide, which, lines, levels, lax.axis_index("frow") * tile_rows, tile_rows * n_row, own)


def tile_fields(n_row, pair_at, turned, pair, cross, gravity, after=()):
    stages, tile_rows, channels, columns = turned.shape
    in_vmem = pl.BlockSpec(memory_space=pltpu.VMEM)
    return pl.pallas_call(
        functools.partial(tile_fields_kernel, n_row, pair_at),
        in_specs=[in_vmem] * 3 + [pl.BlockSpec(memory_space=pltpu.SMEM)] + [in_vmem] * len(after),
        out_shape=(
            jax.ShapeDtypeStruct((stages, tile_rows + 2 * HALO, channels // 3 * FIELDS, columns), F32),
            jax.ShapeDtypeStruct((channels // 3, columns), F32),
            jax.ShapeDtypeStruct((PART, columns), F32),
            jax.ShapeDtypeStruct((stages, tile_rows + 2 * HALO, 3 * PART, columns), F32),
        ),
        compiler_params=PARAMS,
        name="tile_fields",
    )(turned, pair, cross, gravity, *after)


def edge_fields_kernel(n_row, paired, own, one, other, wide):
    stages, extended, _, columns = own.shape
    tile_rows = extended - 2 * HALO
    left, right = from_sides(one[...], other[...], paired)
    lane = ring_lanes()
    sides = jnp.concatenate([left, right], axis=1)

    def rim_of(count, at):
        def ring(values, turn):
            beyond = (lane >= BEYOND_AT + turn) & (lane < BEYOND_AT + HALO + turn)
            from_left, from_right = values[:, :columns], values[:, columns:]
            return jnp.where(
                beyond, turned_by(from_right, BEYOND_AT + turn - at), turned_by(from_left, turn - at - count)
            )

        return by_half(sides, ring)

    rims = {(which, k): rim_of(count, at) for which, k, count, at in edge_plan(stages, tile_rows)}
    for which in range(stages):
        width = HALO - which
        lines = []
        for k in range(HALO - width, HALO + tile_rows + width):
            line = own[which, k]
            if (which, k) in rims:
                line = with_rim(line, rims[which, k])
            lines.append((k, line))
        store_fields(wide, which, lines, PART, lax.axis_index("frow") * tile_rows, tile_rows * n_row)


def edge_fields(n_row, paired, own, one, other):
    stages, extended, _, columns = own.shape
    return pl.pallas_call(
        functools.partial(edge_fields_kernel, n_row, paired),
        out_shape=jax.ShapeDtypeStruct((stages, extended, PART * FIELDS, columns), F32),
        compiler_params=PARAMS,
        name="edge_fields",
    )(own, one, other)


def slot_blocks(cot, where, tiles, share, groups, tile_rows, columns, onehot, parts):
    channels, points = cot.shape
    lines = points // LANES
    named_tiles = tiles.shape[0]
    corner = where[lines : 2 * lines, :]
    row = jnp.zeros_like(corner)
    for k in range(1, tile_rows - 1):
        row = row + (corner >= float(k * (columns - 1))).astype(F32)
    col = corner - row * float(columns - 1)
    target = where[:lines, :]
    offsets = [where[k * lines : (k + 1) * lines, :] for k in (2, 3)]

    before = (
        lax.broadcasted_iota(jnp.int32, (GROUP, GROUP), 0)
        < lax.broadcasted_iota(jnp.int32, (GROUP, GROUP), 1)
    ).astype(F32).astype(BF16)
    index = lax.broadcasted_iota(jnp.int32, tiles.shape, 0)
    begin = ((index % share) * (GROUP // share)).astype(F32)
    slots = lax.broadcasted_iota(jnp.int32, (GROUP, GROUP), 0).astype(F32).astype(BF16)
    one, zero = jnp.ones(slots.shape, BF16), jnp.zeros(slots.shape, BF16)
    count = jnp.zeros((named_tiles, 1), F32)
    rows = channels + 8

    def across(values, b):
        return jnp.concatenate([values[2 * b : 2 * b + 1, :], values[2 * b + 1 : 2 * b + 2, :]], axis=1)

    all_named = [(tiles == across(target, b)).astype(F32) for b in range(points // GROUP)]
    all_ahead = jnp.dot(jnp.concatenate(all_named, axis=0).astype(BF16), before, preferred_element_type=F32)
    for b, named in enumerate(all_named):
        part = slice(b * GROUP, (b + 1) * GROUP)
        ahead = all_ahead[b * named_tiles : (b + 1) * named_tiles, :]
        lane = jnp.sum(named * (ahead + count + begin), axis=0, keepdims=True)
        count = count + jnp.sum(named, axis=1, keepdims=True)
        onehot[:, part] = jnp.where(slots == lane.astype(BF16), one, zero)
        coords = [across(values, b) for values in (row, col, *offsets)]
        data_high, data_low = split(jnp.concatenate([cot[:, part], *coords, *coords], axis=0))
        for g in range(groups):
            mine = named[g * share : g * share + 1, :]
            for i in range(1, share):
                mine = mine + named[g * share + i : g * share + i + 1, :]
            mine = mine.astype(BF16)
            parts[g * rows : (g + 1) * rows, part] = data_high * mine
            parts[(groups + g) * rows : (groups + g + 1) * rows, part] = data_low * mine
    both = dot_nt(parts[...], onehot[...])
    packed = both[: groups * rows, :] + both[groups * rows :, :]
    upper = lax.broadcasted_iota(jnp.int32, (8, LANES), 0) < 4
    for g in range(groups):
        block = packed[g * rows : (g + 1) * rows, :]
        yield (
            block[:channels, :LANES],
            block[:channels, LANES:],
            jnp.where(upper, block[channels:, :LANES], block[channels:, LANES:]),
        )


def store_block(out, at, pieces):
    channels = pieces[0].shape[0]
    out[at : at + channels, :] = pieces[0]
    out[at + channels : at + 2 * channels, :] = pieces[1]
    out[at + 2 * channels : at + 2 * channels + 8, :] = pieces[2]


def pack_scratch(channels, points, groups):
    return [
        pltpu.VMEM((GROUP, points), BF16),
        pltpu.VMEM((2 * groups * (channels + 8), points), BF16),
    ]


def pack_all_kernel(tile_count, share, tile_rows, columns, cot, where, out, *scratch):
    tiles = lax.broadcasted_iota(jnp.int32, (tile_count, GROUP), 0).astype(F32)
    for g, pieces in enumerate(slot_blocks(cot, where, tiles, share, tile_count // share, tile_rows, columns, *scratch)):
        store_block(out.at[g], 0, pieces)


def pack_all(cot, where, tile_count, share, tile_rows, columns):
    channels, points = cot.shape
    groups = tile_count // share
    return pl.pallas_call(
        functools.partial(pack_all_kernel, tile_count, share, tile_rows, columns),
        out_shape=jax.ShapeDtypeStruct((groups, 2 * channels + 8, LANES), F32),
        scratch_shapes=pack_scratch(channels, points, groups),
        compiler_params=PARAMS,
        name="pack_points",
    )(cot, where)


NEAR = ((0, 0), (2, 0), (0, 1), (2, 1))
FAR = ((0, 2), (2, 2), (0, 3), (2, 3))


def partner_tiles(partners):
    at_row, at_col = lax.axis_index("frow"), lax.axis_index("fcol")
    n_col = lax.axis_size("fcol")
    index = lax.broadcasted_iota(jnp.int32, (8, GROUP), 0)
    tiles = jnp.full(index.shape, -1, jnp.int32)
    for g, (df, dz) in enumerate(partners):
        tiles = jnp.where(index == g, (at_row ^ df) * n_col + (at_col ^ dz), tiles)
    return tiles.astype(F32)


def pack_chip_kernel(tiles, tile_rows, columns, cot, where, pair_cot, pair_where, *refs):
    outs, scratch = refs[-4 - len(tiles) : -4], refs[-4:]
    begin = 0
    for i, points in enumerate(((cot, where), (pair_cot, pair_where))):
        blocks = slot_blocks(
            *points, partner_tiles(tiles), 1, len(tiles), tile_rows, columns, *scratch[2 * i : 2 * i + 2]
        )
        for out, pieces in zip(outs, blocks):
            store_block(out, begin, pieces)
        begin += 2 * cot.shape[0] + 8


def pack_chip(tiles, points, tile_rows, columns, after=()):
    channels, count = points[0].shape
    return pl.pallas_call(
        functools.partial(pack_chip_kernel, tiles, tile_rows, columns),
        out_shape=[jax.ShapeDtypeStruct((2 * (2 * channels + 8), LANES), F32)] * len(tiles),
        scratch_shapes=pack_scratch(channels, count, len(tiles)) * 2,
        compiler_params=PARAMS,
        name="pack_chip",
    )(*points, *after)


def scatter_kernel(count, first, later, *refs):
    blocks, refs = refs[:count], refs[count:]
    if not first:
        total, refs = refs[0], refs[1:]
    outs, scratch = refs[later : -2 * count], refs[-2 * count :]
    _, channels, columns = outs[0].shape
    places = [(out, r) for out in outs for r in range(out.shape[0])]
    tile_rows = len(places)
    rows = 2 * channels + 8
    cells = lax.broadcasted_iota(jnp.int32, (columns, LANES), 0).astype(F32).astype(BF16)
    zero = jnp.zeros((channels, LANES), BF16)

    def spread(values, shape):
        return jnp.broadcast_to(values.astype(BF16), shape)

    sums = None
    for block, parts, weight in zip(blocks, scratch[::2], scratch[1::2]):
        at = 0
        for source in range(block.shape[0] // rows):
            for half in range(2):
                part = slice(at, at + LANES)
                at += LANES
                begin = source * rows + 2 * channels + 4 * half
                coords = block[begin : begin + 4, :]
                row, col, along_rows, along_cols = (coords[k : k + 1, :] for k in range(4))
                corner, beside = cells == spread(col, cells.shape), cells == spread(col + 1.0, cells.shape)
                for k, (near, far) in enumerate(zip(split(1.0 - along_cols), split(along_cols))):
                    chosen = jnp.where(
                        beside, spread(far, cells.shape), jnp.zeros(cells.shape, BF16)
                    )
                    weight[k * columns : (k + 1) * columns, part] = jnp.where(corner, spread(near, cells.shape), chosen)
                begin = source * rows + half * channels
                values = block[begin : begin + channels, :]
                upper, lower = split(values * (1.0 - along_rows)), split(values * along_rows)
                below = None
                line = spread(row, zero.shape)
                for r in range(tile_rows):
                    here = line == jnp.full(zero.shape, r, BF16)
                    for k in range(2):
                        product = zero if below is None else jnp.where(below, lower[k], zero)
                        product = jnp.where(here, upper[k], product)
                        begin = (k * tile_rows + r) * channels
                        parts[begin : begin + channels, part] = product
                    below = here
        both = dot_nt(parts[...], weight[...])
        both = both[:, :columns] + both[:, columns:]
        both = both[: tile_rows * channels, :] + both[tile_rows * channels :, :]
        sums = both if sums is None else sums + both
    for r in range(tile_rows):
        line = sums[r * channels : (r + 1) * channels, :]
        if not first:
            line = line + total[r]
        out, at = places[r]
        out[at] = line


def scatter(blocks, total, channels, tile_rows, columns, after=(), parts=None):
    slots = [block.shape[0] // (2 * channels + 8) * GROUP for block in blocks]
    return pl.pallas_call(
        functools.partial(scatter_kernel, len(blocks), total is None, len(after)),
        out_shape=[jax.ShapeDtypeStruct((count, channels, columns), F32) for count in parts or (tile_rows,)],
        scratch_shapes=[
            pltpu.VMEM((2 * lines, count), BF16) for count in slots for lines in (tile_rows * channels, columns)
        ],
        compiler_params=PARAMS,
        name="scatter_points",
    )(*blocks, *([] if total is None else [total]), *after)


def finish_kernel(count, total, *refs):
    parts, (canvas, to_pair, to_cross) = refs[:count], refs[-3:]
    tile_rows = canvas.shape[0]
    places = [(part, at) for part in parts for at in range(part.shape[0])]
    for r in range(tile_rows):
        line = total[r]
        if parts:
            part, at = places[r]
            line = line + part[at]
        canvas[r] = line
    lower = first_of_pair()
    for k in range(HALO):
        top, bottom = canvas[k], canvas[tile_rows - HALO + k]
        to_pair[k] = jnp.where(lower, bottom, top)
        to_cross[k] = jnp.where(lower, top, bottom)


def finish(total, parts=(), after=()):
    _, channels, columns = total.shape
    rim = jax.ShapeDtypeStruct((HALO, channels, columns), F32)
    return pl.pallas_call(
        functools.partial(finish_kernel, len(parts)),
        out_shape=(jax.ShapeDtypeStruct(total.shape, F32), rim, rim),
        compiler_params=PARAMS,
        name="finish_canvas",
    )(total, *parts, *after)


def adjoint_rows(n_row, canvas, pair, cross):
    tile = [canvas[r] for r in range(canvas.shape[0])]
    rims = ([ref[k] for k in range(HALO)] for ref in (pair, cross))
    return extended_rows(tile, *rims, HALO, first_of_pair(), row_masks(n_row))


def cross_edges_kernel(canvas, cross, *refs):
    edges = refs[-1]
    lower = first_of_pair()
    tile_rows = canvas.shape[0]
    empty = jnp.zeros(edges.shape, F32)
    lines = [(k, jnp.where(lower, cross[k], empty)) for k in range(HALO)]
    lines += [(HALO + r, canvas[r]) for r in range(tile_rows)]
    lines += [(HALO + tile_rows + k, jnp.where(lower, empty, cross[k])) for k in range(HALO)]
    edges[...] = edge_columns(lines, empty)


def pair_edges_kernel(n_row, tile_rows, partial, pair, edges):
    lower, masks = first_of_pair(), row_masks(n_row)
    result = partial[...]
    empty = jnp.zeros(edges.shape, F32)
    lane = lax.broadcasted_iota(jnp.int32, edges.shape, 1)
    row = ((lane + 4) // 8) % 16
    result = jnp.where(row < HALO, masks[0], jnp.where(row < HALO + tile_rows, 1.0, masks[1])) * result
    lines = [(k, jnp.where(lower, empty, pair[k])) for k in range(HALO)]
    lines += [(HALO + tile_rows + k, jnp.where(lower, pair[k], empty)) for k in range(HALO)]
    edges[...] = result + edge_columns(lines, empty)


def adjoint_edges(n_row, canvas, pair, cross, after=()):
    tile_rows, channels, _ = canvas.shape
    edges = jax.ShapeDtypeStruct((channels, LANES), F32)
    partial = pl.pallas_call(
        cross_edges_kernel, out_shape=edges, compiler_params=PARAMS, name="cross_edges"
    )(canvas, cross, *after)
    return pl.pallas_call(
        functools.partial(pair_edges_kernel, n_row, tile_rows),
        out_shape=edges,
        compiler_params=PARAMS,
        name="pair_edges",
    )(partial, pair)


def run_stages(wide, gravity, levels, masks, tile_rows, buffers, store):
    start, middle, after, last = buffers

    def along_x(values):
        return pltpu.roll(values, LANES - 1, 1) - pltpu.roll(values, 1, 1)

    def run(stage, adjoint, put):
        width = HALO - 1 - stage
        begin, end = HALO - width, HALO + tile_rows + width
        for low in range(0, levels, PART):
            pull = (0.5 * stage_weight(stage)) * gravity[low : low + PART, :]

            def state(k, which):
                return wide[stage, k, which * levels + low : which * levels + low + PART, :]

            def line(k):
                a, b, c = (adjoint[k, w * levels + low : w * levels + low + PART, :] for w in range(3))
                v = state(k, 2)
                return a, b, c, v, v * b, v * c

            up, here = line(begin - 1), line(begin)
            for k in range(begin, end):
                down = line(k + 1)
                a, b, c, v = here[:4]
                h, u = state(k, 0), state(k, 1)
                a_x, a_y = along_x(a), down[0] - up[0]
                height = u * a_x + v * a_y + pull * (along_x(b) + (down[2] - up[2]))
                east = h * a_x + along_x(u * b) + (down[4] - up[4]) - b * state(k, 3) - c * state(k, 4)
                north = h * a_y + along_x(u * c) + (down[5] - up[5]) - b * state(k, 5) - c * state(k, 6)
                for w, (old, change) in enumerate(zip((a, b, c), (height, east, north))):
                    put(k, w, low, old, change)
                up, here = here, down

    def kept(k, value):
        if k < HALO:
            return value * masks[0]
        if k >= HALO + tile_rows:
            return value * masks[1]
        return value

    def half_into(result):
        def put(k, w, low, old, change):
            result[k, w * levels + low : w * levels + low + PART, :] = kept(k, 0.5 * old + change)

        return put

    def after_step(adjoint, k, w, low, old, change):
        return 0.5 * adjoint[k, w * levels + low : w * levels + low + PART, :] + old + change

    def to_after(k, w, low, old, change):
        after[k, w * levels + low : w * levels + low + PART, :] = kept(k, after_step(start, k, w, low, old, change))

    def to_end(k, w, low, old, change):
        store(k - HALO, w, low, after_step(after, k, w, low, old, change))

    run(0, start, half_into(middle))
    run(1, middle, to_after)
    run(2, after, half_into(last))
    run(3, last, to_end)


def tile_steps_kernel(n_row, canvas, pair, cross, wide, gravity, out, windows, *buffers):
    tile_rows, channels, _ = canvas.shape
    levels = channels // 3
    for k, line in adjoint_rows(n_row, canvas, pair, cross):
        buffers[0][k] = line
        windows[k] = edge_windows(line)

    def store(r, w, low, value):
        out[r, w * levels + low : w * levels + low + PART, :] = value

    run_stages(wide, gravity, levels, row_masks(n_row), tile_rows, buffers, store)


def tile_steps(n_row, canvas, pair, cross, wide, gravity):
    tile_rows, channels, columns = canvas.shape
    return pl.pallas_call(
        functools.partial(tile_steps_kernel, n_row),
        out_shape=(
            jax.ShapeDtypeStruct(canvas.shape, F32),
            jax.ShapeDtypeStruct((tile_rows + 2 * HALO, 3 * PART, columns), F32),
        ),
        scratch_shapes=[pltpu.VMEM((tile_rows + 2 * HALO, channels, columns), F32)] * 4,
        compiler_params=PARAMS,
        name="tile_steps",
    )(canvas, pair, cross, wide, gravity)


def edge_steps_kernel(n_row, paired, windows, one, other, wide, gravity, inner, out, *buffers):
    *buffers, result = buffers
    tile_rows, channels, _ = inner.shape
    levels = channels // 3
    left, right = from_sides(one[...], other[...], paired)
    rims = jnp.where(first_lanes(left), pltpu.roll(right, BEYOND_AT, 1), left)
    for k in range(tile_rows + 2 * HALO):
        rim = by_half(rims, lambda values, turn: turned_by(values, turn - 8 * k))
        buffers[0][k] = with_rim(windows[k], rim)
    lane = ring_lanes()

    def store(r, w, low, value):
        result[r, w * PART : (w + 1) * PART, :] = value

    run_stages(wide, gravity, PART, row_masks(n_row), tile_rows, buffers, store)
    for r in range(tile_rows):
        for begin in range(0, channels, PART):
            field, turn = begin // levels, begin % levels // PART * TURN
            value = result[r, field * PART : (field + 1) * PART, :]
            first = pltpu.roll(value, turn, 1) if turn else value
            final = pltpu.roll(value, LANES - BEYOND_AT - turn, 1)
            line = jnp.where(lane >= LANES - HALO, final, inner[r, begin : begin + PART, :])
            out[pl.ds(begin * tile_rows + r, PART, stride=tile_rows), :] = jnp.where(lane < HALO, first, line)


def edge_steps(n_row, paired, windows, one, other, wide, gravity, inner):
    tile_rows, channels, columns = inner.shape
    return pl.pallas_call(
        functools.partial(edge_steps_kernel, n_row, paired),
        out_shape=jax.ShapeDtypeStruct((channels * tile_rows, columns), F32),
        scratch_shapes=[pltpu.VMEM(windows.shape, F32)] * 4 + [pltpu.VMEM((tile_rows, 3 * PART, columns), F32)],
        compiler_params=PARAMS,
        name="edge_steps",
    )(windows, one, other, wide, gravity, inner)


def shifted(values, axis, by):
    count = lax.axis_size(axis)
    return lax.ppermute(values, axis, [(i, (i + by) % count) for i in range(count)])


def exchanged(values, offset):
    n_row, n_col = lax.axis_size("frow"), lax.axis_size("fcol")
    df, dz = offset
    pairs = [(f * n_col + z, (f ^ df) * n_col + (z ^ dz)) for f in range(n_row) for z in range(n_col)]
    return lax.ppermute(values, ("frow", "fcol"), pairs)


def exchanged_across(values):
    n_row = lax.axis_size("frow")
    return lax.ppermute(values, "frow", [(f, ((f + 1) ^ 1) - 1) for f in range(1, n_row - 1)])


def from_everyone(packed, channels, tile_count):
    groups = packed.shape[0]
    rows = channels + 4
    halves = [
        jnp.concatenate(
            [
                packed[:, h * channels : (h + 1) * channels],
                packed[:, 2 * channels + 4 * h : 2 * channels + 4 * h + 4],
            ],
            axis=1,
        )
        for h in range(2)
    ]
    slots = jnp.stack(halves, axis=2).transpose(1, 0, 2, 3).reshape(rows, tile_count, -1)
    slots = lax.all_to_all(slots, ("frow", "fcol"), split_axis=1, concat_axis=1, tiled=True)
    slots = slots.reshape(rows, groups, 2, LANES).transpose(1, 2, 0, 3)
    return jnp.concatenate(
        [slots[:, 0, :channels], slots[:, 1, :channels], slots[:, 0, channels:], slots[:, 1, channels:]], axis=1
    )


def per_device(latlon_cot, dest_tile, base_cell, corner_frac, saved_states, gravity):
    n_row, n_col = lax.axis_size("frow"), lax.axis_size("fcol")
    tile_count = n_row * n_col
    levels = gravity.shape[0]
    tile_rows = saved_states.shape[4]
    columns = saved_states.shape[5]
    channels = 3 * levels
    points = base_cell.shape[0]
    lines = points // LANES
    share = GROUP * tile_count // (2 * points)
    paired = share == 1 and n_row == 4 and n_col == 4
    size = (channels, tile_rows, columns)

    cot = latlon_cot.reshape(channels, points)
    partner_cot = exchanged(cot, (1, 0)) if paired else None
    sent, to_cross, turned, cot = prepare(
        dest_tile.reshape(lines, LANES),
        base_cell.reshape(lines, LANES),
        corner_frac,
        saved_states.reshape(4, channels * tile_rows, columns),
        cot,
        (3, 2, 1, 0),
        tile_rows,
    )
    pair_at = 4 * lines
    pair = exchanged(sent, (1, 0))
    cross = exchanged_across(to_cross)
    if paired:
        chip_points = cot, sent, partner_cot, pair
        packed = pack_chip(FAR, chip_points, tile_rows, columns)
        got = [packed[0]] + [exchanged(block, (df, dz ^ 2)) for block, (df, dz) in zip(packed[1:], FAR[1:])]
        packed = pack_chip(NEAR, chip_points, tile_rows, columns, [cross, packed[0]])
        total = scatter(got[:2], None, *size, packed[:1])[0]
        sums = scatter(got[2:], total, *size, parts=(5, tile_rows - 5))
        far = [exchanged(part, (0, 2)) for part in sums]
        got = [packed[0]] + [exchanged(block, tile) for block, tile in zip(packed[1:], NEAR[1:])]
        one, other = all_state_edges(n_row, pair_at, paired, turned, pair, cross, sums)
        one, other = exchanged(one, (0, 1)), exchanged(other, (0, 3))
        total = scatter(got[:2], None, *size)[0]
        total = scatter(got[2:], total, *size)[0]
        fields, pull, edge_pull, own = tile_fields(n_row, pair_at, turned, pair, cross, gravity, [total])
        canvas = finish(total, far, [one, other, pull])
    else:
        packed = pack_all(cot, sent, tile_count, share, tile_rows, columns)
        got = from_everyone(packed, channels, tile_count)
        one, other = all_state_edges(n_row, pair_at, paired, turned, pair, cross)
        one, other = shifted(one, "fcol", 1), shifted(other, "fcol", -1)
        fields, pull, edge_pull, own = tile_fields(n_row, pair_at, turned, pair, cross, gravity)
        canvas = finish(scatter([got.reshape(-1, LANES)], None, *size)[0])

    near_edges = edge_fields(n_row, paired, own, one, other)
    canvas, to_pair, to_cross = canvas
    pair, cross = exchanged(to_pair, (1, 0)), exchanged_across(to_cross)
    edges = adjoint_edges(n_row, canvas, pair, cross, [near_edges])
    if paired:
        sides = exchanged(edges, (0, 1)), exchanged(edges, (0, 3))
    else:
        sides = shifted(edges, "fcol", 1), shifted(edges, "fcol", -1)
    inner, windows = tile_steps(n_row, canvas, pair, cross, fields, pull)
    result = edge_steps(n_row, paired, windows, *sides, near_edges, edge_pull, inner)
    return result.reshape(3, levels, tile_rows, columns)


def solution(mesh):
    placed = (
        P(None, None, ("member", "frow", "fcol")),
        P(("frow", "fcol"), None),
        P(("frow", "fcol")),
        P(None, ("frow", "fcol")),
        P(None, None, None, None, ("member", "frow"), "fcol"),
        P(),
    )
    return jax.shard_map(
        per_device,
        mesh=mesh,
        in_specs=placed,
        out_specs=P(None, None, ("member", "frow"), "fcol"),
        check_vma=False,
    )
```

```python
import functools

import jax
import jax.numpy as jnp
from jax import lax
from jax.experimental import pallas as pl
from jax.experimental.pallas import tpu as pltpu
from jax.sharding import PartitionSpec as P

time_step = 0.25
coriolis_peak = 0.8

HALO = 4
GROUP = 256
LANES = 128
F32 = jnp.float32
BF16 = jnp.bfloat16
PARAMS = pltpu.CompilerParams(vmem_limit_bytes=16 * 1024 * 1024)


def split(values):
    high = values.astype(BF16)
    return high, (values - high.astype(F32)).astype(BF16)


def dot_nt(a, b):
    return lax.dot_general(a, b, (((1,), (1,)), ((), ())), preferred_element_type=F32)


def first_of_pair(axis="frow"):
    return lax.rem(lax.axis_index(axis), 2) == 0


def row_masks(n_row):
    at = lax.axis_index("frow")
    return jnp.where(at > 0, 1.0, 0.0).astype(F32), jnp.where(at < n_row - 1, 1.0, 0.0).astype(F32)


def extended_rows(tile, pair, cross, width, lower, masks):
    tile_rows = len(tile)
    lines = [(HALO - width + k, jnp.where(lower, cross[k], pair[k]) * masks[0]) for k in range(width)]
    lines += [(HALO + k, tile[k]) for k in range(tile_rows)]
    lines += [(HALO + tile_rows + k, jnp.where(lower, pair[k], cross[k]) * masks[1]) for k in range(width)]
    return lines


def edge_columns(lines, result):
    lane = lax.broadcasted_iota(jnp.int32, result.shape, 1)
    owner = ((lane + 4) // 8) % 16
    for k, line in lines:
        result = jnp.where(owner == k, pltpu.roll(line, (8 * k) % LANES, 1), result)
    return result


def first_lanes(like):
    return lax.broadcasted_iota(jnp.int32, like.shape, 1) % 8 < 4


def from_sides(one, other, paired):
    if not paired:
        return one, other
    lower = first_of_pair("fcol")
    return jnp.where(lower, other, one), jnp.where(lower, one, other)


def first_row(which):
    return sum(HALO - k for k in range(which))


def prepare_kernel(order, dest, base, frac, states, cot, sent, cross, turned, cot_out, dest_v, base_v, frac_v, states_v, sems):
    moves = ((dest, dest_v), (base, base_v), (frac, frac_v), (states, states_v), (cot, cot_out))
    copies = [pltpu.make_async_copy(source, target, sems.at[i]) for i, (source, target) in enumerate(moves)]
    for copy in copies:
        copy.start()
    for copy in copies[:3]:
        copy.wait()
    lines = dest_v.shape[0]
    sent[:lines, :] = dest_v[...].astype(F32)
    sent[lines : 2 * lines, :] = base_v[...].astype(F32)
    for k in range(2):
        for i in range(lines):
            sent[(2 + k) * lines + i : (2 + k) * lines + i + 1, :] = frac_v[k : k + 1, i * LANES : (i + 1) * LANES]
    copies[3].wait()
    _, tile_rows, channels, _ = turned.shape
    lower = first_of_pair()
    for which, source in enumerate(order):
        for r in range(tile_rows):
            turned[which, r] = states_v[source, pl.ds(r, channels, stride=tile_rows), :]
        width = HALO - which
        for k in range(width):
            top, bottom = turned[which, k], turned[which, tile_rows - width + k]
            at = (first_row(which) + k) * channels
            sent[4 * lines + at : 4 * lines + at + channels, :] = jnp.where(lower, bottom, top)
            cross[at : at + channels, :] = jnp.where(lower, top, bottom)
    copies[4].wait()


def prepare(dest, base, frac, states, cot, order, tile_rows):
    channels, points = cot.shape
    columns = states.shape[2]
    stages = len(order)
    rim = first_row(stages) * channels
    lines = points // LANES
    in_hbm = pl.BlockSpec(memory_space=pltpu.HBM)
    return pl.pallas_call(
        functools.partial(prepare_kernel, order),
        in_specs=[in_hbm] * 5,
        out_shape=(
            jax.ShapeDtypeStruct((4 * lines + rim, LANES), F32),
            jax.ShapeDtypeStruct((rim, columns), F32),
            jax.ShapeDtypeStruct((stages, tile_rows, channels, columns), F32),
            jax.ShapeDtypeStruct(cot.shape, F32),
        ),
        scratch_shapes=[
            pltpu.VMEM(dest.shape, jnp.int32),
            pltpu.VMEM(base.shape, jnp.int32),
            pltpu.VMEM(frac.shape, F32),
            pltpu.VMEM(states.shape, F32),
            pltpu.SemaphoreType.DMA((5,)),
        ],
        compiler_params=PARAMS,
        name="prepare",
    )(*(pltpu.with_memory_space_constraint(x, pltpu.HBM) for x in (dest, base, frac, states, cot)))


def state_rows(which, turned, pair, pair_at, cross, lower, masks):
    _, tile_rows, channels, _ = turned.shape
    width = HALO - which

    def rim(ref, start):
        at = [start + (first_row(which) + k) * channels for k in range(width)]
        return [ref[i : i + channels, :] for i in at]

    tile = [turned[which, r] for r in range(tile_rows)]
    return extended_rows(tile, rim(pair, pair_at), rim(cross, 0), width, lower, masks)


def edge_plan(stages, tile_rows):
    plan, lane = [], 0
    for which in range(stages):
        width = HALO - which
        for k in range(HALO - width, HALO + tile_rows + width):
            count = width - max(HALO - k, k - (HALO + tile_rows - 1), 0)
            if count > 0:
                plan.append((which, k, count, lane))
                lane += count
    return plan


def state_edges(n_row, turned, pair, pair_at, cross):
    stages, tile_rows, channels, _ = turned.shape
    lower, masks = first_of_pair(), row_masks(n_row)
    lane = lax.broadcasted_iota(jnp.int32, (channels, LANES), 1)
    first = last = jnp.zeros((channels, LANES), F32)
    lines = [dict(state_rows(which, turned, pair, pair_at, cross, lower, masks)) for which in range(stages)]
    for which, k, count, at in edge_plan(stages, tile_rows):
        here = (lane >= at) & (lane < at + count)
        first = jnp.where(here, pltpu.roll(lines[which][k], at, 1), first)
        last = jnp.where(here, pltpu.roll(lines[which][k], (at + count) % LANES, 1), last)
    return first, last


def state_edges_kernel(n_row, pair_at, paired, turned, pair, cross, *refs):
    one, other = refs[-2:]
    first, last = state_edges(n_row, turned, pair, pair_at, cross)
    one[...], other[...] = last, first
    if paired:
        lower = first_of_pair("fcol")
        one[...], other[...] = jnp.where(lower, last, first), jnp.where(lower, first, last)


def all_state_edges(n_row, pair_at, paired, turned, pair, cross, after=()):
    return pl.pallas_call(
        functools.partial(state_edges_kernel, n_row, pair_at, paired),
        out_shape=[jax.ShapeDtypeStruct((turned.shape[2], LANES), F32)] * 2,
        compiler_params=PARAMS,
        name="state_edges",
    )(turned, pair, cross, *after)


FIELDS = 7


def stage_weight(which):
    return 0.5 * time_step if which % 2 == 0 else time_step


def store_fields(wide, which, lines, levels, base_row, total_rows, own=None):
    weight = stage_weight(which)
    channels = 3 * levels
    for k, line in lines:
        wide[which, k, :channels, :] = (0.5 * weight) * line
        if own is not None:
            own[which, k] = edge_windows(line)
    winds = slice(levels, channels)
    for k in range(lines[0][0] + 1, lines[-1][0]):
        values = wide[which, k, winds, :]
        change = pltpu.roll(values, LANES - 1, 1) - pltpu.roll(values, 1, 1)
        slope = wide[which, k + 1, winds, :] - wide[which, k - 1, winds, :]
        rotation = weight * (coriolis_peak * (2.0 * ((base_row + k - HALO).astype(F32) + 0.5) / total_rows - 1.0))
        begin = channels
        for value in (change[:levels], change[levels:] + rotation, slope[:levels] - rotation, slope[levels:]):
            wide[which, k, begin : begin + levels, :] = value
            begin += levels


PART = 8
BEYOND_AT = 32
TURN = LANES // 2


def ring_lanes():
    return lax.broadcasted_iota(jnp.int32, (PART, LANES), 1)


def by_half(values, ring):
    lane = ring_lanes()
    second = (lane >= TURN - LANES // 8) & (lane < LANES - LANES // 8)
    fields = []
    for begin in range(0, values.shape[0], 2 * PART):
        first, last = values[begin : begin + PART], values[begin + PART : begin + 2 * PART]
        fields.append(jnp.where(second, ring(last, TURN), ring(first, 0)))
    return jnp.concatenate(fields, axis=0)


def turned_by(values, shift):
    shift %= LANES
    return pltpu.roll(values, shift, 1) if shift else values


def edge_windows(line):
    lane = ring_lanes()

    def ring(values, turn):
        ends = (lane >= turn + BEYOND_AT // 2) & (lane < turn + BEYOND_AT)
        return jnp.where(ends, turned_by(values, BEYOND_AT + turn), turned_by(values, turn))

    return by_half(line, ring)


def with_rim(window, rim):
    lane = lax.broadcasted_iota(jnp.int32, window.shape, 1) % TURN
    beyond = (lane >= TURN - HALO) | ((lane >= BEYOND_AT) & (lane < BEYOND_AT + HALO))
    return jnp.where(beyond, rim, window)


def tile_fields_kernel(n_row, pair_at, turned, pair, cross, gravity, *refs):
    wide, pull, edge_pull, own = refs[-4:]
    stages, tile_rows, channels, _ = turned.shape
    levels = channels // 3
    level = lax.broadcasted_iota(jnp.int32, pull.shape, 0)
    pulls = jnp.zeros(pull.shape, F32)
    for i in range(levels):
        pulls = jnp.where(level == i, gravity[i], pulls)
    pull[...] = pulls
    edge_pull[...] = by_half(pulls, lambda values, _: values)
    lower, masks = first_of_pair(), row_masks(n_row)
    for which in range(stages):
        lines = state_rows(which, turned, pair, pair_at, cross, lower, masks)
        store_fields(wide, which, lines, levels, lax.axis_index("frow") * tile_rows, tile_rows * n_row, own)


def tile_fields(n_row, pair_at, turned, pair, cross, gravity, after=()):
    stages, tile_rows, channels, columns = turned.shape
    in_vmem = pl.BlockSpec(memory_space=pltpu.VMEM)
    return pl.pallas_call(
        functools.partial(tile_fields_kernel, n_row, pair_at),
        in_specs=[in_vmem] * 3 + [pl.BlockSpec(memory_space=pltpu.SMEM)] + [in_vmem] * len(after),
        out_shape=(
            jax.ShapeDtypeStruct((stages, tile_rows + 2 * HALO, channels // 3 * FIELDS, columns), F32),
            jax.ShapeDtypeStruct((channels // 3, columns), F32),
            jax.ShapeDtypeStruct((PART, columns), F32),
            jax.ShapeDtypeStruct((stages, tile_rows + 2 * HALO, 3 * PART, columns), F32),
        ),
        compiler_params=PARAMS,
        name="tile_fields",
    )(turned, pair, cross, gravity, *after)


def edge_fields_kernel(n_row, paired, own, one, other, wide):
    stages, extended, _, columns = own.shape
    tile_rows = extended - 2 * HALO
    left, right = from_sides(one[...], other[...], paired)
    lane = ring_lanes()
    sides = jnp.concatenate([left, right], axis=1)

    def rim_of(count, at):
        def ring(values, turn):
            beyond = (lane >= BEYOND_AT + turn) & (lane < BEYOND_AT + HALO + turn)
            from_left, from_right = values[:, :columns], values[:, columns:]
            return jnp.where(
                beyond, turned_by(from_right, BEYOND_AT + turn - at), turned_by(from_left, turn - at - count)
            )

        return by_half(sides, ring)

    rims = {(which, k): rim_of(count, at) for which, k, count, at in edge_plan(stages, tile_rows)}
    for which in range(stages):
        width = HALO - which
        lines = []
        for k in range(HALO - width, HALO + tile_rows + width):
            line = own[which, k]
            if (which, k) in rims:
                line = with_rim(line, rims[which, k])
            lines.append((k, line))
        store_fields(wide, which, lines, PART, lax.axis_index("frow") * tile_rows, tile_rows * n_row)


def edge_fields(n_row, paired, own, one, other):
    stages, extended, _, columns = own.shape
    return pl.pallas_call(
        functools.partial(edge_fields_kernel, n_row, paired),
        out_shape=jax.ShapeDtypeStruct((stages, extended, PART * FIELDS, columns), F32),
        compiler_params=PARAMS,
        name="edge_fields",
    )(own, one, other)


def slot_blocks(cot, where, tiles, share, groups, tile_rows, columns, onehot, parts):
    channels, points = cot.shape
    lines = points // LANES
    named_tiles = tiles.shape[0]
    corner = where[lines : 2 * lines, :]
    row = jnp.zeros_like(corner)
    for k in range(1, tile_rows - 1):
        row = row + (corner >= float(k * (columns - 1))).astype(F32)
    col = corner - row * float(columns - 1)
    target = where[:lines, :]
    offsets = [where[k * lines : (k + 1) * lines, :] for k in (2, 3)]

    before = (
        lax.broadcasted_iota(jnp.int32, (GROUP, GROUP), 0)
        < lax.broadcasted_iota(jnp.int32, (GROUP, GROUP), 1)
    ).astype(F32).astype(BF16)
    index = lax.broadcasted_iota(jnp.int32, tiles.shape, 0)
    begin = ((index % share) * (GROUP // share)).astype(F32)
    slots = lax.broadcasted_iota(jnp.int32, (GROUP, GROUP), 0).astype(F32).astype(BF16)
    one, zero = jnp.ones(slots.shape, BF16), jnp.zeros(slots.shape, BF16)
    count = jnp.zeros((named_tiles, 1), F32)
    rows = channels + 8

    def across(values, b):
        return jnp.concatenate([values[2 * b : 2 * b + 1, :], values[2 * b + 1 : 2 * b + 2, :]], axis=1)

    all_named = [(tiles == across(target, b)).astype(F32) for b in range(points // GROUP)]
    all_ahead = jnp.dot(jnp.concatenate(all_named, axis=0).astype(BF16), before, preferred_element_type=F32)
    for b, named in enumerate(all_named):
        part = slice(b * GROUP, (b + 1) * GROUP)
        ahead = all_ahead[b * named_tiles : (b + 1) * named_tiles, :]
        lane = jnp.sum(named * (ahead + count + begin), axis=0, keepdims=True)
        count = count + jnp.sum(named, axis=1, keepdims=True)
        onehot[:, part] = jnp.where(slots == lane.astype(BF16), one, zero)
        coords = [across(values, b) for values in (row, col, *offsets)]
        data_high, data_low = split(jnp.concatenate([cot[:, part], *coords, *coords], axis=0))
        for g in range(groups):
            mine = named[g * share : g * share + 1, :]
            for i in range(1, share):
                mine = mine + named[g * share + i : g * share + i + 1, :]
            mine = mine.astype(BF16)
            parts[g * rows : (g + 1) * rows, part] = data_high * mine
            parts[(groups + g) * rows : (groups + g + 1) * rows, part] = data_low * mine
    both = dot_nt(parts[...], onehot[...])
    packed = both[: groups * rows, :] + both[groups * rows :, :]
    upper = lax.broadcasted_iota(jnp.int32, (8, LANES), 0) < 4
    for g in range(groups):
        block = packed[g * rows : (g + 1) * rows, :]
        yield (
            block[:channels, :LANES],
            block[:channels, LANES:],
            jnp.where(upper, block[channels:, :LANES], block[channels:, LANES:]),
        )


def store_block(out, at, pieces):
    channels = pieces[0].shape[0]
    out[at : at + channels, :] = pieces[0]
    out[at + channels : at + 2 * channels, :] = pieces[1]
    out[at + 2 * channels : at + 2 * channels + 8, :] = pieces[2]


def pack_scratch(channels, points, groups):
    return [
        pltpu.VMEM((GROUP, points), BF16),
        pltpu.VMEM((2 * groups * (channels + 8), points), BF16),
    ]


def pack_all_kernel(tile_count, share, tile_rows, columns, cot, where, out, *scratch):
    tiles = lax.broadcasted_iota(jnp.int32, (tile_count, GROUP), 0).astype(F32)
    for g, pieces in enumerate(slot_blocks(cot, where, tiles, share, tile_count // share, tile_rows, columns, *scratch)):
        store_block(out.at[g], 0, pieces)


def pack_all(cot, where, tile_count, share, tile_rows, columns):
    channels, points = cot.shape
    groups = tile_count // share
    return pl.pallas_call(
        functools.partial(pack_all_kernel, tile_count, share, tile_rows, columns),
        out_shape=jax.ShapeDtypeStruct((groups, 2 * channels + 8, LANES), F32),
        scratch_shapes=pack_scratch(channels, points, groups),
        compiler_params=PARAMS,
        name="pack_points",
    )(cot, where)


NEAR = ((0, 0), (2, 0), (0, 1), (2, 1))
FAR = ((0, 2), (2, 2), (0, 3), (2, 3))


def partner_tiles(partners):
    at_row, at_col = lax.axis_index("frow"), lax.axis_index("fcol")
    n_col = lax.axis_size("fcol")
    index = lax.broadcasted_iota(jnp.int32, (8, GROUP), 0)
    tiles = jnp.full(index.shape, -1, jnp.int32)
    for g, (df, dz) in enumerate(partners):
        tiles = jnp.where(index == g, (at_row ^ df) * n_col + (at_col ^ dz), tiles)
    return tiles.astype(F32)


def pack_chip_kernel(tiles, tile_rows, columns, cot, where, pair_cot, pair_where, *refs):
    outs, scratch = refs[-4 - len(tiles) : -4], refs[-4:]
    begin = 0
    for i, points in enumerate(((cot, where), (pair_cot, pair_where))):
        blocks = slot_blocks(
            *points, partner_tiles(tiles), 1, len(tiles), tile_rows, columns, *scratch[2 * i : 2 * i + 2]
        )
        for out, pieces in zip(outs, blocks):
            store_block(out, begin, pieces)
        begin += 2 * cot.shape[0] + 8


def pack_chip(tiles, points, tile_rows, columns, after=()):
    channels, count = points[0].shape
    return pl.pallas_call(
        functools.partial(pack_chip_kernel, tiles, tile_rows, columns),
        out_shape=[jax.ShapeDtypeStruct((2 * (2 * channels + 8), LANES), F32)] * len(tiles),
        scratch_shapes=pack_scratch(channels, count, len(tiles)) * 2,
        compiler_params=PARAMS,
        name="pack_chip",
    )(*points, *after)


def scatter_kernel(count, first, later, *refs):
    blocks, refs = refs[:count], refs[count:]
    if not first:
        total, refs = refs[0], refs[1:]
    outs, scratch = refs[later : -2 * count], refs[-2 * count :]
    _, channels, columns = outs[0].shape
    places = [(out, r) for out in outs for r in range(out.shape[0])]
    tile_rows = len(places)
    rows = 2 * channels + 8
    cells = lax.broadcasted_iota(jnp.int32, (columns, LANES), 0).astype(F32).astype(BF16)
    zero = jnp.zeros((channels, LANES), BF16)

    def spread(values, shape):
        return jnp.broadcast_to(values.astype(BF16), shape)

    sums = None
    for block, parts, weight in zip(blocks, scratch[::2], scratch[1::2]):
        at = 0
        for source in range(block.shape[0] // rows):
            for half in range(2):
                part = slice(at, at + LANES)
                at += LANES
                begin = source * rows + 2 * channels + 4 * half
                coords = block[begin : begin + 4, :]
                row, col, along_rows, along_cols = (coords[k : k + 1, :] for k in range(4))
                corner, beside = cells == spread(col, cells.shape), cells == spread(col + 1.0, cells.shape)
                for k, (near, far) in enumerate(zip(split(1.0 - along_cols), split(along_cols))):
                    chosen = jnp.where(
                        beside, spread(far, cells.shape), jnp.zeros(cells.shape, BF16)
                    )
                    weight[k * columns : (k + 1) * columns, part] = jnp.where(corner, spread(near, cells.shape), chosen)
                begin = source * rows + half * channels
                values = block[begin : begin + channels, :]
                upper, lower = split(values * (1.0 - along_rows)), split(values * along_rows)
                below = None
                line = spread(row, zero.shape)
                for r in range(tile_rows):
                    here = line == jnp.full(zero.shape, r, BF16)
                    for k in range(2):
                        product = zero if below is None else jnp.where(below, lower[k], zero)
                        product = jnp.where(here, upper[k], product)
                        begin = (k * tile_rows + r) * channels
                        parts[begin : begin + channels, part] = product
                    below = here
        both = dot_nt(parts[...], weight[...])
        both = both[:, :columns] + both[:, columns:]
        both = both[: tile_rows * channels, :] + both[tile_rows * channels :, :]
        sums = both if sums is None else sums + both
    for r in range(tile_rows):
        line = sums[r * channels : (r + 1) * channels, :]
        if not first:
            line = line + total[r]
        out, at = places[r]
        out[at] = line


def scatter(blocks, total, channels, tile_rows, columns, after=(), parts=None):
    slots = [block.shape[0] // (2 * channels + 8) * GROUP for block in blocks]
    return pl.pallas_call(
        functools.partial(scatter_kernel, len(blocks), total is None, len(after)),
        out_shape=[jax.ShapeDtypeStruct((count, channels, columns), F32) for count in parts or (tile_rows,)],
        scratch_shapes=[
            pltpu.VMEM((2 * lines, count), BF16) for count in slots for lines in (tile_rows * channels, columns)
        ],
        compiler_params=PARAMS,
        name="scatter_points",
    )(*blocks, *([] if total is None else [total]), *after)


def finish_kernel(count, total, *refs):
    parts, (canvas, to_pair, to_cross) = refs[:count], refs[-3:]
    tile_rows = canvas.shape[0]
    places = [(part, at) for part in parts for at in range(part.shape[0])]
    for r in range(tile_rows):
        line = total[r]
        if parts:
            part, at = places[r]
            line = line + part[at]
        canvas[r] = line
    lower = first_of_pair()
    for k in range(HALO):
        top, bottom = canvas[k], canvas[tile_rows - HALO + k]
        to_pair[k] = jnp.where(lower, bottom, top)
        to_cross[k] = jnp.where(lower, top, bottom)


def finish(total, parts=(), after=()):
    _, channels, columns = total.shape
    rim = jax.ShapeDtypeStruct((HALO, channels, columns), F32)
    return pl.pallas_call(
        functools.partial(finish_kernel, len(parts)),
        out_shape=(jax.ShapeDtypeStruct(total.shape, F32), rim, rim),
        compiler_params=PARAMS,
        name="finish_canvas",
    )(total, *parts, *after)


def adjoint_rows(n_row, canvas, pair, cross):
    tile = [canvas[r] for r in range(canvas.shape[0])]
    rims = ([ref[k] for k in range(HALO)] for ref in (pair, cross))
    return extended_rows(tile, *rims, HALO, first_of_pair(), row_masks(n_row))


def cross_edges_kernel(canvas, cross, *refs):
    edges = refs[-1]
    lower = first_of_pair()
    tile_rows = canvas.shape[0]
    empty = jnp.zeros(edges.shape, F32)
    lines = [(k, jnp.where(lower, cross[k], empty)) for k in range(HALO)]
    lines += [(HALO + r, canvas[r]) for r in range(tile_rows)]
    lines += [(HALO + tile_rows + k, jnp.where(lower, empty, cross[k])) for k in range(HALO)]
    edges[...] = edge_columns(lines, empty)


def pair_edges_kernel(n_row, tile_rows, partial, pair, edges):
    lower, masks = first_of_pair(), row_masks(n_row)
    result = partial[...]
    empty = jnp.zeros(edges.shape, F32)
    lane = lax.broadcasted_iota(jnp.int32, edges.shape, 1)
    row = ((lane + 4) // 8) % 16
    result = jnp.where(row < HALO, masks[0], jnp.where(row < HALO + tile_rows, 1.0, masks[1])) * result
    lines = [(k, jnp.where(lower, empty, pair[k])) for k in range(HALO)]
    lines += [(HALO + tile_rows + k, jnp.where(lower, pair[k], empty)) for k in range(HALO)]
    edges[...] = result + edge_columns(lines, empty)


def adjoint_edges(n_row, canvas, pair, cross, after=()):
    tile_rows, channels, _ = canvas.shape
    edges = jax.ShapeDtypeStruct((channels, LANES), F32)
    partial = pl.pallas_call(
        cross_edges_kernel, out_shape=edges, compiler_params=PARAMS, name="cross_edges"
    )(canvas, cross, *after)
    return pl.pallas_call(
        functools.partial(pair_edges_kernel, n_row, tile_rows),
        out_shape=edges,
        compiler_params=PARAMS,
        name="pair_edges",
    )(partial, pair)


def run_stages(wide, gravity, levels, masks, tile_rows, buffers, store):
    start, middle, after, last = buffers

    def along_x(values):
        return pltpu.roll(values, LANES - 1, 1) - pltpu.roll(values, 1, 1)

    def run(stage, adjoint, put):
        width = HALO - 1 - stage
        begin, end = HALO - width, HALO + tile_rows + width
        for low in range(0, levels, PART):
            pull = (0.5 * stage_weight(stage)) * gravity[low : low + PART, :]

            def state(k, which):
                return wide[stage, k, which * levels + low : which * levels + low + PART, :]

            def line(k):
                a, b, c = (adjoint[k, w * levels + low : w * levels + low + PART, :] for w in range(3))
                v = state(k, 2)
                return a, b, c, v, v * b, v * c

            up, here = line(begin - 1), line(begin)
            for k in range(begin, end):
                down = line(k + 1)
                a, b, c, v = here[:4]
                h, u = state(k, 0), state(k, 1)
                a_x, a_y = along_x(a), down[0] - up[0]
                height = u * a_x + v * a_y + pull * (along_x(b) + (down[2] - up[2]))
                east = h * a_x + along_x(u * b) + (down[4] - up[4]) - b * state(k, 3) - c * state(k, 4)
                north = h * a_y + along_x(u * c) + (down[5] - up[5]) - b * state(k, 5) - c * state(k, 6)
                for w, (old, change) in enumerate(zip((a, b, c), (height, east, north))):
                    put(k, w, low, old, change)
                up, here = here, down

    def kept(k, value):
        if k < HALO:
            return value * masks[0]
        if k >= HALO + tile_rows:
            return value * masks[1]
        return value

    def half_into(result):
        def put(k, w, low, old, change):
            result[k, w * levels + low : w * levels + low + PART, :] = kept(k, 0.5 * old + change)

        return put

    def after_step(adjoint, k, w, low, old, change):
        return 0.5 * adjoint[k, w * levels + low : w * levels + low + PART, :] + old + change

    def to_after(k, w, low, old, change):
        after[k, w * levels + low : w * levels + low + PART, :] = kept(k, after_step(start, k, w, low, old, change))

    def to_end(k, w, low, old, change):
        store(k - HALO, w, low, after_step(after, k, w, low, old, change))

    run(0, start, half_into(middle))
    run(1, middle, to_after)
    run(2, after, half_into(last))
    run(3, last, to_end)


def tile_steps_kernel(n_row, canvas, pair, cross, wide, gravity, out, windows, *buffers):
    tile_rows, channels, _ = canvas.shape
    levels = channels // 3
    for k, line in adjoint_rows(n_row, canvas, pair, cross):
        buffers[0][k] = line
        windows[k] = edge_windows(line)

    def store(r, w, low, value):
        out[r, w * levels + low : w * levels + low + PART, :] = value

    run_stages(wide, gravity, levels, row_masks(n_row), tile_rows, buffers, store)


def tile_steps(n_row, canvas, pair, cross, wide, gravity):
    tile_rows, channels, columns = canvas.shape
    return pl.pallas_call(
        functools.partial(tile_steps_kernel, n_row),
        out_shape=(
            jax.ShapeDtypeStruct(canvas.shape, F32),
            jax.ShapeDtypeStruct((tile_rows + 2 * HALO, 3 * PART, columns), F32),
        ),
        scratch_shapes=[pltpu.VMEM((tile_rows + 2 * HALO, channels, columns), F32)] * 4,
        compiler_params=PARAMS,
        name="tile_steps",
    )(canvas, pair, cross, wide, gravity)


def edge_steps_kernel(n_row, paired, windows, one, other, wide, gravity, inner, out, *buffers):
    *buffers, result = buffers
    tile_rows, channels, _ = inner.shape
    levels = channels // 3
    left, right = from_sides(one[...], other[...], paired)
    rims = jnp.where(first_lanes(left), pltpu.roll(right, BEYOND_AT, 1), left)
    for k in range(tile_rows + 2 * HALO):
        rim = by_half(rims, lambda values, turn: turned_by(values, turn - 8 * k))
        buffers[0][k] = with_rim(windows[k], rim)
    lane = ring_lanes()

    def store(r, w, low, value):
        result[r, w * PART : (w + 1) * PART, :] = value

    run_stages(wide, gravity, PART, row_masks(n_row), tile_rows, buffers, store)
    for r in range(tile_rows):
        for begin in range(0, channels, PART):
            field, turn = begin // levels, begin % levels // PART * TURN
            value = result[r, field * PART : (field + 1) * PART, :]
            first = pltpu.roll(value, turn, 1) if turn else value
            final = pltpu.roll(value, LANES - BEYOND_AT - turn, 1)
            line = jnp.where(lane >= LANES - HALO, final, inner[r, begin : begin + PART, :])
            out[pl.ds(begin * tile_rows + r, PART, stride=tile_rows), :] = jnp.where(lane < HALO, first, line)


def edge_steps(n_row, paired, windows, one, other, wide, gravity, inner):
    tile_rows, channels, columns = inner.shape
    return pl.pallas_call(
        functools.partial(edge_steps_kernel, n_row, paired),
        out_shape=jax.ShapeDtypeStruct((channels * tile_rows, columns), F32),
        scratch_shapes=[pltpu.VMEM(windows.shape, F32)] * 4 + [pltpu.VMEM((tile_rows, 3 * PART, columns), F32)],
        compiler_params=PARAMS,
        name="edge_steps",
    )(windows, one, other, wide, gravity, inner)


def shifted(values, axis, by):
    count = lax.axis_size(axis)
    return lax.ppermute(values, axis, [(i, (i + by) % count) for i in range(count)])


def exchanged(values, offset):
    n_row, n_col = lax.axis_size("frow"), lax.axis_size("fcol")
    df, dz = offset
    pairs = [(f * n_col + z, (f ^ df) * n_col + (z ^ dz)) for f in range(n_row) for z in range(n_col)]
    return lax.ppermute(values, ("frow", "fcol"), pairs)


def exchanged_across(values):
    n_row = lax.axis_size("frow")
    return lax.ppermute(values, "frow", [(f, ((f + 1) ^ 1) - 1) for f in range(1, n_row - 1)])


def from_everyone(packed, channels, tile_count):
    groups = packed.shape[0]
    rows = channels + 4
    halves = [
        jnp.concatenate(
            [
                packed[:, h * channels : (h + 1) * channels],
                packed[:, 2 * channels + 4 * h : 2 * channels + 4 * h + 4],
            ],
            axis=1,
        )
        for h in range(2)
    ]
    slots = jnp.stack(halves, axis=2).transpose(1, 0, 2, 3).reshape(rows, tile_count, -1)
    slots = lax.all_to_all(slots, ("frow", "fcol"), split_axis=1, concat_axis=1, tiled=True)
    slots = slots.reshape(rows, groups, 2, LANES).transpose(1, 2, 0, 3)
    return jnp.concatenate(
        [slots[:, 0, :channels], slots[:, 1, :channels], slots[:, 0, channels:], slots[:, 1, channels:]], axis=1
    )


def per_device(latlon_cot, dest_tile, base_cell, corner_frac, saved_states, gravity):
    n_row, n_col = lax.axis_size("frow"), lax.axis_size("fcol")
    tile_count = n_row * n_col
    levels = gravity.shape[0]
    tile_rows = saved_states.shape[4]
    columns = saved_states.shape[5]
    channels = 3 * levels
    points = base_cell.shape[0]
    lines = points // LANES
    share = GROUP * tile_count // (2 * points)
    paired = share == 1 and n_row == 4 and n_col == 4
    size = (channels, tile_rows, columns)

    cot = latlon_cot.reshape(channels, points)
    partner_cot = exchanged(cot, (1, 0)) if paired else None
    sent, to_cross, turned, cot = prepare(
        dest_tile.reshape(lines, LANES),
        base_cell.reshape(lines, LANES),
        corner_frac,
        saved_states.reshape(4, channels * tile_rows, columns),
        cot,
        (3, 2, 1, 0),
        tile_rows,
    )
    pair_at = 4 * lines
    pair = exchanged(sent, (1, 0))
    cross = exchanged_across(to_cross)
    if paired:
        chip_points = cot, sent, partner_cot, pair
        packed = pack_chip(FAR, chip_points, tile_rows, columns)
        got = [packed[0]] + [exchanged(block, (df, dz ^ 2)) for block, (df, dz) in zip(packed[1:], FAR[1:])]
        packed = pack_chip(NEAR, chip_points, tile_rows, columns, [cross, packed[0]])
        total = scatter(got[:2], None, *size, packed[:1])[0]
        sums = scatter(got[2:], total, *size, parts=(5, tile_rows - 5))
        far = [exchanged(part, (0, 2)) for part in sums]
        got = [packed[0]] + [exchanged(block, tile) for block, tile in zip(packed[1:], NEAR[1:])]
        one, other = all_state_edges(n_row, pair_at, paired, turned, pair, cross, sums)
        one, other = exchanged(one, (0, 1)), exchanged(other, (0, 3))
        total = scatter(got[:2], None, *size)[0]
        total = scatter(got[2:], total, *size)[0]
        fields, pull, edge_pull, own = tile_fields(n_row, pair_at, turned, pair, cross, gravity, [total])
        canvas = finish(total, far, [one, other, pull])
    else:
        packed = pack_all(cot, sent, tile_count, share, tile_rows, columns)
        got = from_everyone(packed, channels, tile_count)
        one, other = all_state_edges(n_row, pair_at, paired, turned, pair, cross)
        one, other = shifted(one, "fcol", 1), shifted(other, "fcol", -1)
        fields, pull, edge_pull, own = tile_fields(n_row, pair_at, turned, pair, cross, gravity)
        canvas = finish(scatter([got.reshape(-1, LANES)], None, *size)[0])

    near_edges = edge_fields(n_row, paired, own, one, other)
    canvas, to_pair, to_cross = canvas
    pair, cross = exchanged(to_pair, (1, 0)), exchanged_across(to_cross)
    edges = adjoint_edges(n_row, canvas, pair, cross, [near_edges])
    if paired:
        sides = exchanged(edges, (0, 1)), exchanged(edges, (0, 3))
    else:
        sides = shifted(edges, "fcol", 1), shifted(edges, "fcol", -1)
    inner, windows = tile_steps(n_row, canvas, pair, cross, fields, pull)
    result = edge_steps(n_row, paired, windows, *sides, near_edges, edge_pull, inner)
    return result.reshape(3, levels, tile_rows, columns)


def solution(mesh):
    placed = (
        P(None, None, ("member", "frow", "fcol")),
        P(("frow", "fcol"), None),
        P(("frow", "fcol")),
        P(None, ("frow", "fcol")),
        P(None, None, None, None, ("member", "frow"), "fcol"),
        P(),
    )
    return jax.shard_map(
        per_device,
        mesh=mesh,
        in_specs=placed,
        out_specs=P(None, None, ("member", "frow"), "fcol"),
        check_vma=False,
    )
```

```python
import functools

import jax
import jax.numpy as jnp
from jax import lax
from jax.experimental import pallas as pl
from jax.experimental.pallas import tpu as pltpu
from jax.sharding import PartitionSpec as P

time_step = 0.25
coriolis_peak = 0.8

HALO = 4
GROUP = 256
LANES = 128
F32 = jnp.float32
BF16 = jnp.bfloat16
PARAMS = pltpu.CompilerParams(vmem_limit_bytes=16 * 1024 * 1024)


def split(values):
    high = values.astype(BF16)
    return high, (values - high.astype(F32)).astype(BF16)


def dot_nt(a, b):
    return lax.dot_general(a, b, (((1,), (1,)), ((), ())), preferred_element_type=F32)


def first_of_pair(axis="frow"):
    return lax.rem(lax.axis_index(axis), 2) == 0


def row_masks(n_row):
    at = lax.axis_index("frow")
    return jnp.where(at > 0, 1.0, 0.0).astype(F32), jnp.where(at < n_row - 1, 1.0, 0.0).astype(F32)


def extended_rows(tile, pair, cross, width, lower, masks):
    tile_rows = len(tile)
    lines = [(HALO - width + k, jnp.where(lower, cross[k], pair[k]) * masks[0]) for k in range(width)]
    lines += [(HALO + k, tile[k]) for k in range(tile_rows)]
    lines += [(HALO + tile_rows + k, jnp.where(lower, pair[k], cross[k]) * masks[1]) for k in range(width)]
    return lines


def edge_columns(lines, result):
    lane = lax.broadcasted_iota(jnp.int32, result.shape, 1)
    owner = ((lane + 4) // 8) % 16
    for k, line in lines:
        result = jnp.where(owner == k, pltpu.roll(line, (8 * k) % LANES, 1), result)
    return result


def first_lanes(like):
    return lax.broadcasted_iota(jnp.int32, like.shape, 1) % 8 < 4


def from_sides(one, other, paired):
    if not paired:
        return one, other
    lower = first_of_pair("fcol")
    return jnp.where(lower, other, one), jnp.where(lower, one, other)


def first_row(which):
    return sum(HALO - k for k in range(which))


def prepare_kernel(order, dest, base, frac, states, cot, sent, cross, turned, cot_out, dest_v, base_v, frac_v, states_v, sems):
    moves = ((dest, dest_v), (base, base_v), (frac, frac_v), (states, states_v), (cot, cot_out))
    copies = [pltpu.make_async_copy(source, target, sems.at[i]) for i, (source, target) in enumerate(moves)]
    for copy in copies:
        copy.start()
    for copy in copies[:3]:
        copy.wait()
    lines = dest_v.shape[0]
    sent[:lines, :] = dest_v[...].astype(F32)
    sent[lines : 2 * lines, :] = base_v[...].astype(F32)
    for k in range(2):
        for i in range(lines):
            sent[(2 + k) * lines + i : (2 + k) * lines + i + 1, :] = frac_v[k : k + 1, i * LANES : (i + 1) * LANES]
    copies[3].wait()
    _, tile_rows, channels, _ = turned.shape
    lower = first_of_pair()
    for which, source in enumerate(order):
        for r in range(tile_rows):
            turned[which, r] = states_v[source, pl.ds(r, channels, stride=tile_rows), :]
        width = HALO - which
        for k in range(width):
            top, bottom = turned[which, k], turned[which, tile_rows - width + k]
            at = (first_row(which) + k) * channels
            sent[4 * lines + at : 4 * lines + at + channels, :] = jnp.where(lower, bottom, top)
            cross[at : at + channels, :] = jnp.where(lower, top, bottom)
    copies[4].wait()


def prepare(dest, base, frac, states, cot, order, tile_rows):
    channels, points = cot.shape
    columns = states.shape[2]
    stages = len(order)
    rim = first_row(stages) * channels
    lines = points // LANES
    in_hbm = pl.BlockSpec(memory_space=pltpu.HBM)
    return pl.pallas_call(
        functools.partial(prepare_kernel, order),
        in_specs=[in_hbm] * 5,
        out_shape=(
            jax.ShapeDtypeStruct((4 * lines + rim, LANES), F32),
            jax.ShapeDtypeStruct((rim, columns), F32),
            jax.ShapeDtypeStruct((stages, tile_rows, channels, columns), F32),
            jax.ShapeDtypeStruct(cot.shape, F32),
        ),
        scratch_shapes=[
            pltpu.VMEM(dest.shape, jnp.int32),
            pltpu.VMEM(base.shape, jnp.int32),
            pltpu.VMEM(frac.shape, F32),
            pltpu.VMEM(states.shape, F32),
            pltpu.SemaphoreType.DMA((5,)),
        ],
        compiler_params=PARAMS,
        name="prepare",
    )(*(pltpu.with_memory_space_constraint(x, pltpu.HBM) for x in (dest, base, frac, states, cot)))


def state_rows(which, turned, pair, pair_at, cross, lower, masks):
    _, tile_rows, channels, _ = turned.shape
    width = HALO - which

    def rim(ref, start):
        at = [start + (first_row(which) + k) * channels for k in range(width)]
        return [ref[i : i + channels, :] for i in at]

    tile = [turned[which, r] for r in range(tile_rows)]
    return extended_rows(tile, rim(pair, pair_at), rim(cross, 0), width, lower, masks)


def edge_plan(stages, tile_rows):
    plan, lane = [], 0
    for which in range(stages):
        width = HALO - which
        for k in range(HALO - width, HALO + tile_rows + width):
            count = width - max(HALO - k, k - (HALO + tile_rows - 1), 0)
            if count > 0:
                plan.append((which, k, count, lane))
                lane += count
    return plan


def state_edges(n_row, turned, pair, pair_at, cross):
    stages, tile_rows, channels, _ = turned.shape
    lower, masks = first_of_pair(), row_masks(n_row)
    lane = lax.broadcasted_iota(jnp.int32, (channels, LANES), 1)
    first = last = jnp.zeros((channels, LANES), F32)
    lines = [dict(state_rows(which, turned, pair, pair_at, cross, lower, masks)) for which in range(stages)]
    for which, k, count, at in edge_plan(stages, tile_rows):
        here = (lane >= at) & (lane < at + count)
        first = jnp.where(here, pltpu.roll(lines[which][k], at, 1), first)
        last = jnp.where(here, pltpu.roll(lines[which][k], (at + count) % LANES, 1), last)
    return first, last


def state_edges_kernel(n_row, pair_at, paired, turned, pair, cross, *refs):
    one, other = refs[-2:]
    first, last = state_edges(n_row, turned, pair, pair_at, cross)
    one[...], other[...] = last, first
    if paired:
        lower = first_of_pair("fcol")
        one[...], other[...] = jnp.where(lower, last, first), jnp.where(lower, first, last)


def all_state_edges(n_row, pair_at, paired, turned, pair, cross, after=()):
    return pl.pallas_call(
        functools.partial(state_edges_kernel, n_row, pair_at, paired),
        out_shape=[jax.ShapeDtypeStruct((turned.shape[2], LANES), F32)] * 2,
        compiler_params=PARAMS,
        name="state_edges",
    )(turned, pair, cross, *after)


FIELDS = 7


def stage_weight(which):
    return 0.5 * time_step if which % 2 == 0 else time_step


def store_fields(wide, which, lines, levels, base_row, total_rows, own=None):
    weight = stage_weight(which)
    channels = 3 * levels
    for k, line in lines:
        wide[which, k, :channels, :] = (0.5 * weight) * line
        if own is not None:
            own[which, k] = edge_windows(line)
    winds = slice(levels, channels)
    for k in range(lines[0][0] + 1, lines[-1][0]):
        values = wide[which, k, winds, :]
        change = pltpu.roll(values, LANES - 1, 1) - pltpu.roll(values, 1, 1)
        slope = wide[which, k + 1, winds, :] - wide[which, k - 1, winds, :]
        rotation = weight * (coriolis_peak * (2.0 * ((base_row + k - HALO).astype(F32) + 0.5) / total_rows - 1.0))
        begin = channels
        for value in (change[:levels], change[levels:] + rotation, slope[:levels] - rotation, slope[levels:]):
            wide[which, k, begin : begin + levels, :] = value
            begin += levels


PART = 8
BEYOND_AT = 32
TURN = LANES // 2


def ring_lanes():
    return lax.broadcasted_iota(jnp.int32, (PART, LANES), 1)


def by_half(values, ring):
    lane = ring_lanes()
    second = (lane >= TURN - LANES // 8) & (lane < LANES - LANES // 8)
    fields = []
    for begin in range(0, values.shape[0], 2 * PART):
        first, last = values[begin : begin + PART], values[begin + PART : begin + 2 * PART]
        fields.append(jnp.where(second, ring(last, TURN), ring(first, 0)))
    return jnp.concatenate(fields, axis=0)


def turned_by(values, shift):
    shift %= LANES
    return pltpu.roll(values, shift, 1) if shift else values


def edge_windows(line):
    lane = ring_lanes()

    def ring(values, turn):
        ends = (lane >= turn + BEYOND_AT // 2) & (lane < turn + BEYOND_AT)
        return jnp.where(ends, turned_by(values, BEYOND_AT + turn), turned_by(values, turn))

    return by_half(line, ring)


def with_rim(window, rim):
    lane = lax.broadcasted_iota(jnp.int32, window.shape, 1) % TURN
    beyond = (lane >= TURN - HALO) | ((lane >= BEYOND_AT) & (lane < BEYOND_AT + HALO))
    return jnp.where(beyond, rim, window)


def tile_fields_kernel(n_row, pair_at, turned, pair, cross, gravity, *refs):
    wide, pull, edge_pull, own = refs[-4:]
    stages, tile_rows, channels, _ = turned.shape
    levels = channels // 3
    level = lax.broadcasted_iota(jnp.int32, pull.shape, 0)
    pulls = jnp.zeros(pull.shape, F32)
    for i in range(levels):
        pulls = jnp.where(level == i, gravity[i], pulls)
    pull[...] = pulls
    edge_pull[...] = by_half(pulls, lambda values, _: values)
    lower, masks = first_of_pair(), row_masks(n_row)
    for which in range(stages):
        lines = state_rows(which, turned, pair, pair_at, cross, lower, masks)
        store_fields(wide, which, lines, levels, lax.axis_index("frow") * tile_rows, tile_rows * n_row, own)


def tile_fields(n_row, pair_at, turned, pair, cross, gravity, after=()):
    stages, tile_rows, channels, columns = turned.shape
    in_vmem = pl.BlockSpec(memory_space=pltpu.VMEM)
    return pl.pallas_call(
        functools.partial(tile_fields_kernel, n_row, pair_at),
        in_specs=[in_vmem] * 3 + [pl.BlockSpec(memory_space=pltpu.SMEM)] + [in_vmem] * len(after),
        out_shape=(
            jax.ShapeDtypeStruct((stages, tile_rows + 2 * HALO, channels // 3 * FIELDS, columns), F32),
            jax.ShapeDtypeStruct((channels // 3, columns), F32),
            jax.ShapeDtypeStruct((PART, columns), F32),
            jax.ShapeDtypeStruct((stages, tile_rows + 2 * HALO, 3 * PART, columns), F32),
        ),
        compiler_params=PARAMS,
        name="tile_fields",
    )(turned, pair, cross, gravity, *after)


def edge_fields_kernel(n_row, paired, own, one, other, wide):
    stages, extended, _, columns = own.shape
    tile_rows = extended - 2 * HALO
    left, right = from_sides(one[...], other[...], paired)
    lane = ring_lanes()
    sides = jnp.concatenate([left, right], axis=1)

    def rim_of(count, at):
        def ring(values, turn):
            beyond = (lane >= BEYOND_AT + turn) & (lane < BEYOND_AT + HALO + turn)
            from_left, from_right = values[:, :columns], values[:, columns:]
            return jnp.where(
                beyond, turned_by(from_right, BEYOND_AT + turn - at), turned_by(from_left, turn - at - count)
            )

        return by_half(sides, ring)

    rims = {(which, k): rim_of(count, at) for which, k, count, at in edge_plan(stages, tile_rows)}
    for which in range(stages):
        width = HALO - which
        lines = []
        for k in range(HALO - width, HALO + tile_rows + width):
            line = own[which, k]
            if (which, k) in rims:
                line = with_rim(line, rims[which, k])
            lines.append((k, line))
        store_fields(wide, which, lines, PART, lax.axis_index("frow") * tile_rows, tile_rows * n_row)


def edge_fields(n_row, paired, own, one, other):
    stages, extended, _, columns = own.shape
    return pl.pallas_call(
        functools.partial(edge_fields_kernel, n_row, paired),
        out_shape=jax.ShapeDtypeStruct((stages, extended, PART * FIELDS, columns), F32),
        compiler_params=PARAMS,
        name="edge_fields",
    )(own, one, other)


def slot_blocks(cot, where, tiles, share, groups, tile_rows, columns, onehot, parts):
    channels, points = cot.shape
    lines = points // LANES
    named_tiles = tiles.shape[0]
    corner = where[lines : 2 * lines, :]
    row = jnp.zeros_like(corner)
    for k in range(1, tile_rows - 1):
        row = row + (corner >= float(k * (columns - 1))).astype(F32)
    col = corner - row * float(columns - 1)
    target = where[:lines, :]
    offsets = [where[k * lines : (k + 1) * lines, :] for k in (2, 3)]

    before = (
        lax.broadcasted_iota(jnp.int32, (GROUP, GROUP), 0)
        < lax.broadcasted_iota(jnp.int32, (GROUP, GROUP), 1)
    ).astype(F32).astype(BF16)
    index = lax.broadcasted_iota(jnp.int32, tiles.shape, 0)
    begin = ((index % share) * (GROUP // share)).astype(F32)
    slots = lax.broadcasted_iota(jnp.int32, (GROUP, GROUP), 0).astype(F32).astype(BF16)
    one, zero = jnp.ones(slots.shape, BF16), jnp.zeros(slots.shape, BF16)
    count = jnp.zeros((named_tiles, 1), F32)
    rows = channels + 8

    def across(values, b):
        return jnp.concatenate([values[2 * b : 2 * b + 1, :], values[2 * b + 1 : 2 * b + 2, :]], axis=1)

    all_named = [(tiles == across(target, b)).astype(F32) for b in range(points // GROUP)]
    all_ahead = jnp.dot(jnp.concatenate(all_named, axis=0).astype(BF16), before, preferred_element_type=F32)
    for b, named in enumerate(all_named):
        part = slice(b * GROUP, (b + 1) * GROUP)
        ahead = all_ahead[b * named_tiles : (b + 1) * named_tiles, :]
        lane = jnp.sum(named * (ahead + count + begin), axis=0, keepdims=True)
        count = count + jnp.sum(named, axis=1, keepdims=True)
        onehot[:, part] = jnp.where(slots == lane.astype(BF16), one, zero)
        coords = [across(values, b) for values in (row, col, *offsets)]
        data_high, data_low = split(jnp.concatenate([cot[:, part], *coords, *coords], axis=0))
        for g in range(groups):
            mine = named[g * share : g * share + 1, :]
            for i in range(1, share):
                mine = mine + named[g * share + i : g * share + i + 1, :]
            mine = mine.astype(BF16)
            parts[g * rows : (g + 1) * rows, part] = data_high * mine
            parts[(groups + g) * rows : (groups + g + 1) * rows, part] = data_low * mine
    both = dot_nt(parts[...], onehot[...])
    packed = both[: groups * rows, :] + both[groups * rows :, :]
    upper = lax.broadcasted_iota(jnp.int32, (8, LANES), 0) < 4
    for g in range(groups):
        block = packed[g * rows : (g + 1) * rows, :]
        yield (
            block[:channels, :LANES],
            block[:channels, LANES:],
            jnp.where(upper, block[channels:, :LANES], block[channels:, LANES:]),
        )


def store_block(out, at, pieces):
    channels = pieces[0].shape[0]
    out[at : at + channels, :] = pieces[0]
    out[at + channels : at + 2 * channels, :] = pieces[1]
    out[at + 2 * channels : at + 2 * channels + 8, :] = pieces[2]


def pack_scratch(channels, points, groups):
    return [
        pltpu.VMEM((GROUP, points), BF16),
        pltpu.VMEM((2 * groups * (channels + 8), points), BF16),
    ]


def pack_all_kernel(tile_count, share, tile_rows, columns, cot, where, out, *scratch):
    tiles = lax.broadcasted_iota(jnp.int32, (tile_count, GROUP), 0).astype(F32)
    for g, pieces in enumerate(slot_blocks(cot, where, tiles, share, tile_count // share, tile_rows, columns, *scratch)):
        store_block(out.at[g], 0, pieces)


def pack_all(cot, where, tile_count, share, tile_rows, columns):
    channels, points = cot.shape
    groups = tile_count // share
    return pl.pallas_call(
        functools.partial(pack_all_kernel, tile_count, share, tile_rows, columns),
        out_shape=jax.ShapeDtypeStruct((groups, 2 * channels + 8, LANES), F32),
        scratch_shapes=pack_scratch(channels, points, groups),
        compiler_params=PARAMS,
        name="pack_points",
    )(cot, where)


NEAR = ((0, 0), (2, 0), (0, 1), (2, 1))
FAR = ((0, 2), (2, 2), (0, 3), (2, 3))


def partner_tiles(partners):
    at_row, at_col = lax.axis_index("frow"), lax.axis_index("fcol")
    n_col = lax.axis_size("fcol")
    index = lax.broadcasted_iota(jnp.int32, (8, GROUP), 0)
    tiles = jnp.full(index.shape, -1, jnp.int32)
    for g, (df, dz) in enumerate(partners):
        tiles = jnp.where(index == g, (at_row ^ df) * n_col + (at_col ^ dz), tiles)
    return tiles.astype(F32)


def pack_chip_kernel(tiles, tile_rows, columns, cot, where, pair_cot, pair_where, *refs):
    outs, scratch = refs[-4 - len(tiles) : -4], refs[-4:]
    begin = 0
    for i, points in enumerate(((cot, where), (pair_cot, pair_where))):
        blocks = slot_blocks(
            *points, partner_tiles(tiles), 1, len(tiles), tile_rows, columns, *scratch[2 * i : 2 * i + 2]
        )
        for out, pieces in zip(outs, blocks):
            store_block(out, begin, pieces)
        begin += 2 * cot.shape[0] + 8


def pack_chip(tiles, points, tile_rows, columns, after=()):
    channels, count = points[0].shape
    return pl.pallas_call(
        functools.partial(pack_chip_kernel, tiles, tile_rows, columns),
        out_shape=[jax.ShapeDtypeStruct((2 * (2 * channels + 8), LANES), F32)] * len(tiles),
        scratch_shapes=pack_scratch(channels, count, len(tiles)) * 2,
        compiler_params=PARAMS,
        name="pack_chip",
    )(*points, *after)


def scatter_kernel(count, first, later, *refs):
    blocks, refs = refs[:count], refs[count:]
    if not first:
        total, refs = refs[0], refs[1:]
    outs, scratch = refs[later : -2 * count], refs[-2 * count :]
    _, channels, columns = outs[0].shape
    places = [(out, r) for out in outs for r in range(out.shape[0])]
    tile_rows = len(places)
    rows = 2 * channels + 8
    cells = lax.broadcasted_iota(jnp.int32, (columns, LANES), 0).astype(F32).astype(BF16)
    zero = jnp.zeros((channels, LANES), BF16)

    def spread(values, shape):
        return jnp.broadcast_to(values.astype(BF16), shape)

    sums = None
    for block, parts, weight in zip(blocks, scratch[::2], scratch[1::2]):
        at = 0
        for source in range(block.shape[0] // rows):
            for half in range(2):
                part = slice(at, at + LANES)
                at += LANES
                begin = source * rows + 2 * channels + 4 * half
                coords = block[begin : begin + 4, :]
                row, col, along_rows, along_cols = (coords[k : k + 1, :] for k in range(4))
                corner, beside = cells == spread(col, cells.shape), cells == spread(col + 1.0, cells.shape)
                for k, (near, far) in enumerate(zip(split(1.0 - along_cols), split(along_cols))):
                    chosen = jnp.where(
                        beside, spread(far, cells.shape), jnp.zeros(cells.shape, BF16)
                    )
                    weight[k * columns : (k + 1) * columns, part] = jnp.where(corner, spread(near, cells.shape), chosen)
                begin = source * rows + half * channels
                values = block[begin : begin + channels, :]
                upper, lower = split(values * (1.0 - along_rows)), split(values * along_rows)
                below = None
                line = spread(row, zero.shape)
                for r in range(tile_rows):
                    here = line == jnp.full(zero.shape, r, BF16)
                    for k in range(2):
                        product = zero if below is None else jnp.where(below, lower[k], zero)
                        product = jnp.where(here, upper[k], product)
                        begin = (k * tile_rows + r) * channels
                        parts[begin : begin + channels, part] = product
                    below = here
        both = dot_nt(parts[...], weight[...])
        both = both[:, :columns] + both[:, columns:]
        both = both[: tile_rows * channels, :] + both[tile_rows * channels :, :]
        sums = both if sums is None else sums + both
    for r in range(tile_rows):
        line = sums[r * channels : (r + 1) * channels, :]
        if not first:
            line = line + total[r]
        out, at = places[r]
        out[at] = line


def scatter(blocks, total, channels, tile_rows, columns, after=(), parts=None):
    slots = [block.shape[0] // (2 * channels + 8) * GROUP for block in blocks]
    return pl.pallas_call(
        functools.partial(scatter_kernel, len(blocks), total is None, len(after)),
        out_shape=[jax.ShapeDtypeStruct((count, channels, columns), F32) for count in parts or (tile_rows,)],
        scratch_shapes=[
            pltpu.VMEM((2 * lines, count), BF16) for count in slots for lines in (tile_rows * channels, columns)
        ],
        compiler_params=PARAMS,
        name="scatter_points",
    )(*blocks, *([] if total is None else [total]), *after)


def finish_kernel(count, total, *refs):
    parts, (canvas, to_pair, to_cross) = refs[:count], refs[-3:]
    tile_rows = canvas.shape[0]
    places = [(part, at) for part in parts for at in range(part.shape[0])]
    for r in range(tile_rows):
        line = total[r]
        if parts:
            part, at = places[r]
            line = line + part[at]
        canvas[r] = line
    lower = first_of_pair()
    for k in range(HALO):
        top, bottom = canvas[k], canvas[tile_rows - HALO + k]
        to_pair[k] = jnp.where(lower, bottom, top)
        to_cross[k] = jnp.where(lower, top, bottom)


def finish(total, parts=(), after=()):
    _, channels, columns = total.shape
    rim = jax.ShapeDtypeStruct((HALO, channels, columns), F32)
    return pl.pallas_call(
        functools.partial(finish_kernel, len(parts)),
        out_shape=(jax.ShapeDtypeStruct(total.shape, F32), rim, rim),
        compiler_params=PARAMS,
        name="finish_canvas",
    )(total, *parts, *after)


def adjoint_rows(n_row, canvas, pair, cross):
    tile = [canvas[r] for r in range(canvas.shape[0])]
    rims = ([ref[k] for k in range(HALO)] for ref in (pair, cross))
    return extended_rows(tile, *rims, HALO, first_of_pair(), row_masks(n_row))


def cross_edges_kernel(canvas, cross, *refs):
    edges = refs[-1]
    lower = first_of_pair()
    tile_rows = canvas.shape[0]
    empty = jnp.zeros(edges.shape, F32)
    lines = [(k, jnp.where(lower, cross[k], empty)) for k in range(HALO)]
    lines += [(HALO + r, canvas[r]) for r in range(tile_rows)]
    lines += [(HALO + tile_rows + k, jnp.where(lower, empty, cross[k])) for k in range(HALO)]
    edges[...] = edge_columns(lines, empty)


def pair_edges_kernel(n_row, tile_rows, partial, pair, edges):
    lower, masks = first_of_pair(), row_masks(n_row)
    result = partial[...]
    empty = jnp.zeros(edges.shape, F32)
    lane = lax.broadcasted_iota(jnp.int32, edges.shape, 1)
    row = ((lane + 4) // 8) % 16
    result = jnp.where(row < HALO, masks[0], jnp.where(row < HALO + tile_rows, 1.0, masks[1])) * result
    lines = [(k, jnp.where(lower, empty, pair[k])) for k in range(HALO)]
    lines += [(HALO + tile_rows + k, jnp.where(lower, pair[k], empty)) for k in range(HALO)]
    edges[...] = result + edge_columns(lines, empty)


def adjoint_edges(n_row, canvas, pair, cross, after=()):
    tile_rows, channels, _ = canvas.shape
    edges = jax.ShapeDtypeStruct((channels, LANES), F32)
    partial = pl.pallas_call(
        cross_edges_kernel, out_shape=edges, compiler_params=PARAMS, name="cross_edges"
    )(canvas, cross, *after)
    return pl.pallas_call(
        functools.partial(pair_edges_kernel, n_row, tile_rows),
        out_shape=edges,
        compiler_params=PARAMS,
        name="pair_edges",
    )(partial, pair)


def run_stages(wide, gravity, levels, masks, tile_rows, buffers, store):
    start, middle, after, last = buffers

    def along_x(values):
        return pltpu.roll(values, LANES - 1, 1) - pltpu.roll(values, 1, 1)

    def run(stage, adjoint, put):
        width = HALO - 1 - stage
        begin, end = HALO - width, HALO + tile_rows + width
        for low in range(0, levels, PART):
            pull = (0.5 * stage_weight(stage)) * gravity[low : low + PART, :]

            def state(k, which):
                return wide[stage, k, which * levels + low : which * levels + low + PART, :]

            def line(k):
                a, b, c = (adjoint[k, w * levels + low : w * levels + low + PART, :] for w in range(3))
                v = state(k, 2)
                return a, b, c, v, v * b, v * c

            up, here = line(begin - 1), line(begin)
            for k in range(begin, end):
                down = line(k + 1)
                a, b, c, v = here[:4]
                h, u = state(k, 0), state(k, 1)
                a_x, a_y = along_x(a), down[0] - up[0]
                height = u * a_x + v * a_y + pull * (along_x(b) + (down[2] - up[2]))
                east = h * a_x + along_x(u * b) + (down[4] - up[4]) - b * state(k, 3) - c * state(k, 4)
                north = h * a_y + along_x(u * c) + (down[5] - up[5]) - b * state(k, 5) - c * state(k, 6)
                for w, (old, change) in enumerate(zip((a, b, c), (height, east, north))):
                    put(k, w, low, old, change)
                up, here = here, down

    def kept(k, value):
        if k < HALO:
            return value * masks[0]
        if k >= HALO + tile_rows:
            return value * masks[1]
        return value

    def half_into(result):
        def put(k, w, low, old, change):
            result[k, w * levels + low : w * levels + low + PART, :] = kept(k, 0.5 * old + change)

        return put

    def after_step(adjoint, k, w, low, old, change):
        return 0.5 * adjoint[k, w * levels + low : w * levels + low + PART, :] + old + change

    def to_after(k, w, low, old, change):
        after[k, w * levels + low : w * levels + low + PART, :] = kept(k, after_step(start, k, w, low, old, change))

    def to_end(k, w, low, old, change):
        store(k - HALO, w, low, after_step(after, k, w, low, old, change))

    run(0, start, half_into(middle))
    run(1, middle, to_after)
    run(2, after, half_into(last))
    run(3, last, to_end)


def tile_steps_kernel(n_row, canvas, pair, cross, wide, gravity, out, windows, *buffers):
    tile_rows, channels, _ = canvas.shape
    levels = channels // 3
    for k, line in adjoint_rows(n_row, canvas, pair, cross):
        buffers[0][k] = line
        windows[k] = edge_windows(line)

    def store(r, w, low, value):
        out[r, w * levels + low : w * levels + low + PART, :] = value

    run_stages(wide, gravity, levels, row_masks(n_row), tile_rows, buffers, store)


def tile_steps(n_row, canvas, pair, cross, wide, gravity):
    tile_rows, channels, columns = canvas.shape
    return pl.pallas_call(
        functools.partial(tile_steps_kernel, n_row),
        out_shape=(
            jax.ShapeDtypeStruct(canvas.shape, F32),
            jax.ShapeDtypeStruct((tile_rows + 2 * HALO, 3 * PART, columns), F32),
        ),
        scratch_shapes=[pltpu.VMEM((tile_rows + 2 * HALO, channels, columns), F32)] * 4,
        compiler_params=PARAMS,
        name="tile_steps",
    )(canvas, pair, cross, wide, gravity)


def edge_steps_kernel(n_row, paired, windows, one, other, wide, gravity, inner, out, *buffers):
    *buffers, result = buffers
    tile_rows, channels, _ = inner.shape
    levels = channels // 3
    left, right = from_sides(one[...], other[...], paired)
    rims = jnp.where(first_lanes(left), pltpu.roll(right, BEYOND_AT, 1), left)
    for k in range(tile_rows + 2 * HALO):
        rim = by_half(rims, lambda values, turn: turned_by(values, turn - 8 * k))
        buffers[0][k] = with_rim(windows[k], rim)
    lane = ring_lanes()

    def store(r, w, low, value):
        result[r, w * PART : (w + 1) * PART, :] = value

    run_stages(wide, gravity, PART, row_masks(n_row), tile_rows, buffers, store)
    for r in range(tile_rows):
        for begin in range(0, channels, PART):
            field, turn = begin // levels, begin % levels // PART * TURN
            value = result[r, field * PART : (field + 1) * PART, :]
            first = pltpu.roll(value, turn, 1) if turn else value
            final = pltpu.roll(value, LANES - BEYOND_AT - turn, 1)
            line = jnp.where(lane >= LANES - HALO, final, inner[r, begin : begin + PART, :])
            out[pl.ds(begin * tile_rows + r, PART, stride=tile_rows), :] = jnp.where(lane < HALO, first, line)


def edge_steps(n_row, paired, windows, one, other, wide, gravity, inner):
    tile_rows, channels, columns = inner.shape
    return pl.pallas_call(
        functools.partial(edge_steps_kernel, n_row, paired),
        out_shape=jax.ShapeDtypeStruct((channels * tile_rows, columns), F32),
        scratch_shapes=[pltpu.VMEM(windows.shape, F32)] * 4 + [pltpu.VMEM((tile_rows, 3 * PART, columns), F32)],
        compiler_params=PARAMS,
        name="edge_steps",
    )(windows, one, other, wide, gravity, inner)


def shifted(values, axis, by):
    count = lax.axis_size(axis)
    return lax.ppermute(values, axis, [(i, (i + by) % count) for i in range(count)])


def exchanged(values, offset):
    n_row, n_col = lax.axis_size("frow"), lax.axis_size("fcol")
    df, dz = offset
    pairs = [(f * n_col + z, (f ^ df) * n_col + (z ^ dz)) for f in range(n_row) for z in range(n_col)]
    return lax.ppermute(values, ("frow", "fcol"), pairs)


def exchanged_across(values):
    n_row = lax.axis_size("frow")
    return lax.ppermute(values, "frow", [(f, ((f + 1) ^ 1) - 1) for f in range(1, n_row - 1)])


def from_everyone(packed, channels, tile_count):
    groups = packed.shape[0]
    rows = channels + 4
    halves = [
        jnp.concatenate(
            [
                packed[:, h * channels : (h + 1) * channels],
                packed[:, 2 * channels + 4 * h : 2 * channels + 4 * h + 4],
            ],
            axis=1,
        )
        for h in range(2)
    ]
    slots = jnp.stack(halves, axis=2).transpose(1, 0, 2, 3).reshape(rows, tile_count, -1)
    slots = lax.all_to_all(slots, ("frow", "fcol"), split_axis=1, concat_axis=1, tiled=True)
    slots = slots.reshape(rows, groups, 2, LANES).transpose(1, 2, 0, 3)
    return jnp.concatenate(
        [slots[:, 0, :channels], slots[:, 1, :channels], slots[:, 0, channels:], slots[:, 1, channels:]], axis=1
    )


def per_device(latlon_cot, dest_tile, base_cell, corner_frac, saved_states, gravity):
    n_row, n_col = lax.axis_size("frow"), lax.axis_size("fcol")
    tile_count = n_row * n_col
    levels = gravity.shape[0]
    tile_rows = saved_states.shape[4]
    columns = saved_states.shape[5]
    channels = 3 * levels
    points = base_cell.shape[0]
    lines = points // LANES
    share = GROUP * tile_count // (2 * points)
    paired = share == 1 and n_row == 4 and n_col == 4
    size = (channels, tile_rows, columns)

    cot = latlon_cot.reshape(channels, points)
    partner_cot = exchanged(cot, (1, 0)) if paired else None
    sent, to_cross, turned, cot = prepare(
        dest_tile.reshape(lines, LANES),
        base_cell.reshape(lines, LANES),
        corner_frac,
        saved_states.reshape(4, channels * tile_rows, columns),
        cot,
        (3, 2, 1, 0),
        tile_rows,
    )
    pair_at = 4 * lines
    pair = exchanged(sent, (1, 0))
    cross = exchanged_across(to_cross)
    if paired:
        chip_points = cot, sent, partner_cot, pair
        packed = pack_chip(FAR, chip_points, tile_rows, columns)
        got = [packed[0]] + [exchanged(block, (df, dz ^ 2)) for block, (df, dz) in zip(packed[1:], FAR[1:])]
        packed = pack_chip(NEAR, chip_points, tile_rows, columns, [cross, packed[0]])
        total = scatter(got[:3], None, *size, packed[:1])[0]
        sums = scatter(got[3:], total, *size, parts=(5, tile_rows - 5))
        far = [exchanged(part, (0, 2)) for part in sums]
        got = [packed[0]] + [exchanged(block, tile) for block, tile in zip(packed[1:], NEAR[1:])]
        one, other = all_state_edges(n_row, pair_at, paired, turned, pair, cross, sums)
        one, other = exchanged(one, (0, 1)), exchanged(other, (0, 3))
        total = scatter(got[:3], None, *size)[0]
        total = scatter(got[3:], total, *size)[0]
        fields, pull, edge_pull, own = tile_fields(n_row, pair_at, turned, pair, cross, gravity, [total])
        canvas = finish(total, far, [one, other, pull])
    else:
        packed = pack_all(cot, sent, tile_count, share, tile_rows, columns)
        got = from_everyone(packed, channels, tile_count)
        one, other = all_state_edges(n_row, pair_at, paired, turned, pair, cross)
        one, other = shifted(one, "fcol", 1), shifted(other, "fcol", -1)
        fields, pull, edge_pull, own = tile_fields(n_row, pair_at, turned, pair, cross, gravity)
        canvas = finish(scatter([got.reshape(-1, LANES)], None, *size)[0])

    near_edges = edge_fields(n_row, paired, own, one, other)
    canvas, to_pair, to_cross = canvas
    pair, cross = exchanged(to_pair, (1, 0)), exchanged_across(to_cross)
    edges = adjoint_edges(n_row, canvas, pair, cross, [near_edges])
    if paired:
        sides = exchanged(edges, (0, 1)), exchanged(edges, (0, 3))
    else:
        sides = shifted(edges, "fcol", 1), shifted(edges, "fcol", -1)
    inner, windows = tile_steps(n_row, canvas, pair, cross, fields, pull)
    result = edge_steps(n_row, paired, windows, *sides, near_edges, edge_pull, inner)
    return result.reshape(3, levels, tile_rows, columns)


def solution(mesh):
    placed = (
        P(None, None, ("member", "frow", "fcol")),
        P(("frow", "fcol"), None),
        P(("frow", "fcol")),
        P(None, ("frow", "fcol")),
        P(None, None, None, None, ("member", "frow"), "fcol"),
        P(),
    )
    return jax.shard_map(
        per_device,
        mesh=mesh,
        in_specs=placed,
        out_specs=P(None, None, ("member", "frow"), "fcol"),
        check_vma=False,
    )
```

```python
import functools

import jax
import jax.numpy as jnp
from jax import lax
from jax.experimental import pallas as pl
from jax.experimental.pallas import tpu as pltpu
from jax.sharding import PartitionSpec as P

time_step = 0.25
coriolis_peak = 0.8

HALO = 4
GROUP = 256
LANES = 128
F32 = jnp.float32
BF16 = jnp.bfloat16
PARAMS = pltpu.CompilerParams(vmem_limit_bytes=16 * 1024 * 1024)


def split(values):
    high = values.astype(BF16)
    return high, (values - high.astype(F32)).astype(BF16)


def dot_nt(a, b):
    return lax.dot_general(a, b, (((1,), (1,)), ((), ())), preferred_element_type=F32)


def first_of_pair(axis="frow"):
    return lax.rem(lax.axis_index(axis), 2) == 0


def row_masks(n_row):
    at = lax.axis_index("frow")
    return jnp.where(at > 0, 1.0, 0.0).astype(F32), jnp.where(at < n_row - 1, 1.0, 0.0).astype(F32)


def extended_rows(tile, pair, cross, width, lower, masks):
    tile_rows = len(tile)
    lines = [(HALO - width + k, jnp.where(lower, cross[k], pair[k]) * masks[0]) for k in range(width)]
    lines += [(HALO + k, tile[k]) for k in range(tile_rows)]
    lines += [(HALO + tile_rows + k, jnp.where(lower, pair[k], cross[k]) * masks[1]) for k in range(width)]
    return lines


def edge_columns(lines, result):
    lane = lax.broadcasted_iota(jnp.int32, result.shape, 1)
    owner = ((lane + 4) // 8) % 16
    for k, line in lines:
        result = jnp.where(owner == k, pltpu.roll(line, (8 * k) % LANES, 1), result)
    return result


def first_lanes(like):
    return lax.broadcasted_iota(jnp.int32, like.shape, 1) % 8 < 4


def from_sides(one, other, paired):
    if not paired:
        return one, other
    lower = first_of_pair("fcol")
    return jnp.where(lower, other, one), jnp.where(lower, one, other)


def first_row(which):
    return sum(HALO - k for k in range(which))


def prepare_kernel(order, dest, base, frac, states, cot, sent, cross, turned, cot_out, dest_v, base_v, frac_v, states_v, sems):
    moves = ((dest, dest_v), (base, base_v), (frac, frac_v), (states, states_v), (cot, cot_out))
    copies = [pltpu.make_async_copy(source, target, sems.at[i]) for i, (source, target) in enumerate(moves)]
    for copy in copies:
        copy.start()
    for copy in copies[:3]:
        copy.wait()
    lines = dest_v.shape[0]
    sent[:lines, :] = dest_v[...].astype(F32)
    sent[lines : 2 * lines, :] = base_v[...].astype(F32)
    for k in range(2):
        for i in range(lines):
            sent[(2 + k) * lines + i : (2 + k) * lines + i + 1, :] = frac_v[k : k + 1, i * LANES : (i + 1) * LANES]
    copies[3].wait()
    _, tile_rows, channels, _ = turned.shape
    lower = first_of_pair()
    for which, source in enumerate(order):
        for r in range(tile_rows):
            turned[which, r] = states_v[source, pl.ds(r, channels, stride=tile_rows), :]
        width = HALO - which
        for k in range(width):
            top, bottom = turned[which, k], turned[which, tile_rows - width + k]
            at = (first_row(which) + k) * channels
            sent[4 * lines + at : 4 * lines + at + channels, :] = jnp.where(lower, bottom, top)
            cross[at : at + channels, :] = jnp.where(lower, top, bottom)
    copies[4].wait()


def prepare(dest, base, frac, states, cot, order, tile_rows):
    channels, points = cot.shape
    columns = states.shape[2]
    stages = len(order)
    rim = first_row(stages) * channels
    lines = points // LANES
    in_hbm = pl.BlockSpec(memory_space=pltpu.HBM)
    return pl.pallas_call(
        functools.partial(prepare_kernel, order),
        in_specs=[in_hbm] * 5,
        out_shape=(
            jax.ShapeDtypeStruct((4 * lines + rim, LANES), F32),
            jax.ShapeDtypeStruct((rim, columns), F32),
            jax.ShapeDtypeStruct((stages, tile_rows, channels, columns), F32),
            jax.ShapeDtypeStruct(cot.shape, F32),
        ),
        scratch_shapes=[
            pltpu.VMEM(dest.shape, jnp.int32),
            pltpu.VMEM(base.shape, jnp.int32),
            pltpu.VMEM(frac.shape, F32),
            pltpu.VMEM(states.shape, F32),
            pltpu.SemaphoreType.DMA((5,)),
        ],
        compiler_params=PARAMS,
        name="prepare",
    )(*(pltpu.with_memory_space_constraint(x, pltpu.HBM) for x in (dest, base, frac, states, cot)))


def state_rows(which, turned, pair, pair_at, cross, lower, masks):
    _, tile_rows, channels, _ = turned.shape
    width = HALO - which

    def rim(ref, start):
        at = [start + (first_row(which) + k) * channels for k in range(width)]
        return [ref[i : i + channels, :] for i in at]

    tile = [turned[which, r] for r in range(tile_rows)]
    return extended_rows(tile, rim(pair, pair_at), rim(cross, 0), width, lower, masks)


def edge_plan(stages, tile_rows):
    plan, lane = [], 0
    for which in range(stages):
        width = HALO - which
        for k in range(HALO - width, HALO + tile_rows + width):
            count = width - max(HALO - k, k - (HALO + tile_rows - 1), 0)
            if count > 0:
                plan.append((which, k, count, lane))
                lane += count
    return plan


def state_edges(n_row, turned, pair, pair_at, cross):
    stages, tile_rows, channels, _ = turned.shape
    lower, masks = first_of_pair(), row_masks(n_row)
    lane = lax.broadcasted_iota(jnp.int32, (channels, LANES), 1)
    first = last = jnp.zeros((channels, LANES), F32)
    lines = [dict(state_rows(which, turned, pair, pair_at, cross, lower, masks)) for which in range(stages)]
    for which, k, count, at in edge_plan(stages, tile_rows):
        here = (lane >= at) & (lane < at + count)
        first = jnp.where(here, pltpu.roll(lines[which][k], at, 1), first)
        last = jnp.where(here, pltpu.roll(lines[which][k], (at + count) % LANES, 1), last)
    return first, last


def state_edges_kernel(n_row, pair_at, paired, turned, pair, cross, *refs):
    one, other = refs[-2:]
    first, last = state_edges(n_row, turned, pair, pair_at, cross)
    one[...], other[...] = last, first
    if paired:
        lower = first_of_pair("fcol")
        one[...], other[...] = jnp.where(lower, last, first), jnp.where(lower, first, last)


def all_state_edges(n_row, pair_at, paired, turned, pair, cross, after=()):
    return pl.pallas_call(
        functools.partial(state_edges_kernel, n_row, pair_at, paired),
        out_shape=[jax.ShapeDtypeStruct((turned.shape[2], LANES), F32)] * 2,
        compiler_params=PARAMS,
        name="state_edges",
    )(turned, pair, cross, *after)


FIELDS = 7


def stage_weight(which):
    return 0.5 * time_step if which % 2 == 0 else time_step


def store_fields(wide, which, lines, levels, base_row, total_rows, own=None):
    weight = stage_weight(which)
    channels = 3 * levels
    for k, line in lines:
        wide[which, k, :channels, :] = (0.5 * weight) * line
        if own is not None:
            own[which, k] = edge_windows(line)
    winds = slice(levels, channels)
    for k in range(lines[0][0] + 1, lines[-1][0]):
        values = wide[which, k, winds, :]
        change = pltpu.roll(values, LANES - 1, 1) - pltpu.roll(values, 1, 1)
        slope = wide[which, k + 1, winds, :] - wide[which, k - 1, winds, :]
        rotation = weight * (coriolis_peak * (2.0 * ((base_row + k - HALO).astype(F32) + 0.5) / total_rows - 1.0))
        begin = channels
        for value in (change[:levels], change[levels:] + rotation, slope[:levels] - rotation, slope[levels:]):
            wide[which, k, begin : begin + levels, :] = value
            begin += levels


PART = 8
BEYOND_AT = 32
TURN = LANES // 2


def ring_lanes():
    return lax.broadcasted_iota(jnp.int32, (PART, LANES), 1)


def by_half(values, ring):
    lane = ring_lanes()
    second = (lane >= TURN - LANES // 8) & (lane < LANES - LANES // 8)
    fields = []
    for begin in range(0, values.shape[0], 2 * PART):
        first, last = values[begin : begin + PART], values[begin + PART : begin + 2 * PART]
        fields.append(jnp.where(second, ring(last, TURN), ring(first, 0)))
    return jnp.concatenate(fields, axis=0)


def turned_by(values, shift):
    shift %= LANES
    return pltpu.roll(values, shift, 1) if shift else values


def edge_windows(line):
    lane = ring_lanes()

    def ring(values, turn):
        ends = (lane >= turn + BEYOND_AT // 2) & (lane < turn + BEYOND_AT)
        return jnp.where(ends, turned_by(values, BEYOND_AT + turn), turned_by(values, turn))

    return by_half(line, ring)


def with_rim(window, rim):
    lane = lax.broadcasted_iota(jnp.int32, window.shape, 1) % TURN
    beyond = (lane >= TURN - HALO) | ((lane >= BEYOND_AT) & (lane < BEYOND_AT + HALO))
    return jnp.where(beyond, rim, window)


def tile_fields_kernel(n_row, pair_at, turned, pair, cross, gravity, *refs):
    wide, pull, edge_pull, own = refs[-4:]
    stages, tile_rows, channels, _ = turned.shape
    levels = channels // 3
    level = lax.broadcasted_iota(jnp.int32, pull.shape, 0)
    pulls = jnp.zeros(pull.shape, F32)
    for i in range(levels):
        pulls = jnp.where(level == i, gravity[i], pulls)
    pull[...] = pulls
    edge_pull[...] = by_half(pulls, lambda values, _: values)
    lower, masks = first_of_pair(), row_masks(n_row)
    for which in range(stages):
        lines = state_rows(which, turned, pair, pair_at, cross, lower, masks)
        store_fields(wide, which, lines, levels, lax.axis_index("frow") * tile_rows, tile_rows * n_row, own)


def tile_fields(n_row, pair_at, turned, pair, cross, gravity, after=()):
    stages, tile_rows, channels, columns = turned.shape
    in_vmem = pl.BlockSpec(memory_space=pltpu.VMEM)
    return pl.pallas_call(
        functools.partial(tile_fields_kernel, n_row, pair_at),
        in_specs=[in_vmem] * 3 + [pl.BlockSpec(memory_space=pltpu.SMEM)] + [in_vmem] * len(after),
        out_shape=(
            jax.ShapeDtypeStruct((stages, tile_rows + 2 * HALO, channels // 3 * FIELDS, columns), F32),
            jax.ShapeDtypeStruct((channels // 3, columns), F32),
            jax.ShapeDtypeStruct((PART, columns), F32),
            jax.ShapeDtypeStruct((stages, tile_rows + 2 * HALO, 3 * PART, columns), F32),
        ),
        compiler_params=PARAMS,
        name="tile_fields",
    )(turned, pair, cross, gravity, *after)


def edge_fields_kernel(n_row, paired, own, one, other, wide):
    stages, extended, _, columns = own.shape
    tile_rows = extended - 2 * HALO
    left, right = from_sides(one[...], other[...], paired)
    lane = ring_lanes()
    sides = jnp.concatenate([left, right], axis=1)

    def rim_of(count, at):
        def ring(values, turn):
            beyond = (lane >= BEYOND_AT + turn) & (lane < BEYOND_AT + HALO + turn)
            from_left, from_right = values[:, :columns], values[:, columns:]
            return jnp.where(
                beyond, turned_by(from_right, BEYOND_AT + turn - at), turned_by(from_left, turn - at - count)
            )

        return by_half(sides, ring)

    rims = {(which, k): rim_of(count, at) for which, k, count, at in edge_plan(stages, tile_rows)}
    for which in range(stages):
        width = HALO - which
        lines = []
        for k in range(HALO - width, HALO + tile_rows + width):
            line = own[which, k]
            if (which, k) in rims:
                line = with_rim(line, rims[which, k])
            lines.append((k, line))
        store_fields(wide, which, lines, PART, lax.axis_index("frow") * tile_rows, tile_rows * n_row)


def edge_fields(n_row, paired, own, one, other):
    stages, extended, _, columns = own.shape
    return pl.pallas_call(
        functools.partial(edge_fields_kernel, n_row, paired),
        out_shape=jax.ShapeDtypeStruct((stages, extended, PART * FIELDS, columns), F32),
        compiler_params=PARAMS,
        name="edge_fields",
    )(own, one, other)


def slot_blocks(cot, where, tiles, share, groups, tile_rows, columns, onehot, parts):
    channels, points = cot.shape
    lines = points // LANES
    named_tiles = tiles.shape[0]
    corner = where[lines : 2 * lines, :]
    row = jnp.zeros_like(corner)
    for k in range(1, tile_rows - 1):
        row = row + (corner >= float(k * (columns - 1))).astype(F32)
    col = corner - row * float(columns - 1)
    target = where[:lines, :]
    offsets = [where[k * lines : (k + 1) * lines, :] for k in (2, 3)]

    before = (
        lax.broadcasted_iota(jnp.int32, (GROUP, GROUP), 0)
        < lax.broadcasted_iota(jnp.int32, (GROUP, GROUP), 1)
    ).astype(F32).astype(BF16)
    index = lax.broadcasted_iota(jnp.int32, tiles.shape, 0)
    begin = ((index % share) * (GROUP // share)).astype(F32)
    slots = lax.broadcasted_iota(jnp.int32, (GROUP, GROUP), 0).astype(F32).astype(BF16)
    one, zero = jnp.ones(slots.shape, BF16), jnp.zeros(slots.shape, BF16)
    count = jnp.zeros((named_tiles, 1), F32)
    rows = channels + 8

    def across(values, b):
        return jnp.concatenate([values[2 * b : 2 * b + 1, :], values[2 * b + 1 : 2 * b + 2, :]], axis=1)

    all_named = [(tiles == across(target, b)).astype(F32) for b in range(points // GROUP)]
    all_ahead = jnp.dot(jnp.concatenate(all_named, axis=0).astype(BF16), before, preferred_element_type=F32)
    for b, named in enumerate(all_named):
        part = slice(b * GROUP, (b + 1) * GROUP)
        ahead = all_ahead[b * named_tiles : (b + 1) * named_tiles, :]
        lane = jnp.sum(named * (ahead + count + begin), axis=0, keepdims=True)
        count = count + jnp.sum(named, axis=1, keepdims=True)
        onehot[:, part] = jnp.where(slots == lane.astype(BF16), one, zero)
        coords = [across(values, b) for values in (row, col, *offsets)]
        data_high, data_low = split(jnp.concatenate([cot[:, part], *coords, *coords], axis=0))
        for g in range(groups):
            mine = named[g * share : g * share + 1, :]
            for i in range(1, share):
                mine = mine + named[g * share + i : g * share + i + 1, :]
            mine = mine.astype(BF16)
            parts[g * rows : (g + 1) * rows, part] = data_high * mine
            parts[(groups + g) * rows : (groups + g + 1) * rows, part] = data_low * mine
    both = dot_nt(parts[...], onehot[...])
    packed = both[: groups * rows, :] + both[groups * rows :, :]
    upper = lax.broadcasted_iota(jnp.int32, (8, LANES), 0) < 4
    for g in range(groups):
        block = packed[g * rows : (g + 1) * rows, :]
        yield (
            block[:channels, :LANES],
            block[:channels, LANES:],
            jnp.where(upper, block[channels:, :LANES], block[channels:, LANES:]),
        )


def store_block(out, at, pieces):
    channels = pieces[0].shape[0]
    out[at : at + channels, :] = pieces[0]
    out[at + channels : at + 2 * channels, :] = pieces[1]
    out[at + 2 * channels : at + 2 * channels + 8, :] = pieces[2]


def pack_scratch(channels, points, groups):
    return [
        pltpu.VMEM((GROUP, points), BF16),
        pltpu.VMEM((2 * groups * (channels + 8), points), BF16),
    ]


def pack_all_kernel(tile_count, share, tile_rows, columns, cot, where, out, *scratch):
    tiles = lax.broadcasted_iota(jnp.int32, (tile_count, GROUP), 0).astype(F32)
    for g, pieces in enumerate(slot_blocks(cot, where, tiles, share, tile_count // share, tile_rows, columns, *scratch)):
        store_block(out.at[g], 0, pieces)


def pack_all(cot, where, tile_count, share, tile_rows, columns):
    channels, points = cot.shape
    groups = tile_count // share
    return pl.pallas_call(
        functools.partial(pack_all_kernel, tile_count, share, tile_rows, columns),
        out_shape=jax.ShapeDtypeStruct((groups, 2 * channels + 8, LANES), F32),
        scratch_shapes=pack_scratch(channels, points, groups),
        compiler_params=PARAMS,
        name="pack_points",
    )(cot, where)


NEAR = ((0, 0), (2, 0), (0, 1), (2, 1))
FAR = ((0, 2), (2, 2), (0, 3), (2, 3))


def partner_tiles(partners):
    at_row, at_col = lax.axis_index("frow"), lax.axis_index("fcol")
    n_col = lax.axis_size("fcol")
    index = lax.broadcasted_iota(jnp.int32, (8, GROUP), 0)
    tiles = jnp.full(index.shape, -1, jnp.int32)
    for g, (df, dz) in enumerate(partners):
        tiles = jnp.where(index == g, (at_row ^ df) * n_col + (at_col ^ dz), tiles)
    return tiles.astype(F32)


def pack_chip_kernel(tiles, tile_rows, columns, cot, where, pair_cot, pair_where, *refs):
    outs, scratch = refs[-4 - len(tiles) : -4], refs[-4:]
    begin = 0
    for i, points in enumerate(((cot, where), (pair_cot, pair_where))):
        blocks = slot_blocks(
            *points, partner_tiles(tiles), 1, len(tiles), tile_rows, columns, *scratch[2 * i : 2 * i + 2]
        )
        for out, pieces in zip(outs, blocks):
            store_block(out, begin, pieces)
        begin += 2 * cot.shape[0] + 8


def pack_chip(tiles, points, tile_rows, columns, after=()):
    channels, count = points[0].shape
    return pl.pallas_call(
        functools.partial(pack_chip_kernel, tiles, tile_rows, columns),
        out_shape=[jax.ShapeDtypeStruct((2 * (2 * channels + 8), LANES), F32)] * len(tiles),
        scratch_shapes=pack_scratch(channels, count, len(tiles)) * 2,
        compiler_params=PARAMS,
        name="pack_chip",
    )(*points, *after)


def scatter_kernel(count, first, later, *refs):
    blocks, refs = refs[:count], refs[count:]
    if not first:
        total, refs = refs[0], refs[1:]
    outs, scratch = refs[later : -2 * count], refs[-2 * count :]
    _, channels, columns = outs[0].shape
    places = [(out, r) for out in outs for r in range(out.shape[0])]
    tile_rows = len(places)
    rows = 2 * channels + 8
    cells = lax.broadcasted_iota(jnp.int32, (columns, LANES), 0).astype(F32).astype(BF16)
    zero = jnp.zeros((channels, LANES), BF16)

    def spread(values, shape):
        return jnp.broadcast_to(values.astype(BF16), shape)

    sums = None
    for block, parts, weight in zip(blocks, scratch[::2], scratch[1::2]):
        at = 0
        for source in range(block.shape[0] // rows):
            for half in range(2):
                part = slice(at, at + LANES)
                at += LANES
                begin = source * rows + 2 * channels + 4 * half
                coords = block[begin : begin + 4, :]
                row, col, along_rows, along_cols = (coords[k : k + 1, :] for k in range(4))
                corner, beside = cells == spread(col, cells.shape), cells == spread(col + 1.0, cells.shape)
                for k, (near, far) in enumerate(zip(split(1.0 - along_cols), split(along_cols))):
                    chosen = jnp.where(
                        beside, spread(far, cells.shape), jnp.zeros(cells.shape, BF16)
                    )
                    weight[k * columns : (k + 1) * columns, part] = jnp.where(corner, spread(near, cells.shape), chosen)
                begin = source * rows + half * channels
                values = block[begin : begin + channels, :]
                upper, lower = split(values * (1.0 - along_rows)), split(values * along_rows)
                below = None
                line = spread(row, zero.shape)
                for r in range(tile_rows):
                    here = line == jnp.full(zero.shape, r, BF16)
                    for k in range(2):
                        product = zero if below is None else jnp.where(below, lower[k], zero)
                        product = jnp.where(here, upper[k], product)
                        begin = (k * tile_rows + r) * channels
                        parts[begin : begin + channels, part] = product
                    below = here
        both = dot_nt(parts[...], weight[...])
        both = both[:, :columns] + both[:, columns:]
        both = both[: tile_rows * channels, :] + both[tile_rows * channels :, :]
        sums = both if sums is None else sums + both
    for r in range(tile_rows):
        line = sums[r * channels : (r + 1) * channels, :]
        if not first:
            line = line + total[r]
        out, at = places[r]
        out[at] = line


def scatter(blocks, total, channels, tile_rows, columns, after=(), parts=None):
    slots = [block.shape[0] // (2 * channels + 8) * GROUP for block in blocks]
    return pl.pallas_call(
        functools.partial(scatter_kernel, len(blocks), total is None, len(after)),
        out_shape=[jax.ShapeDtypeStruct((count, channels, columns), F32) for count in parts or (tile_rows,)],
        scratch_shapes=[
            pltpu.VMEM((2 * lines, count), BF16) for count in slots for lines in (tile_rows * channels, columns)
        ],
        compiler_params=PARAMS,
        name="scatter_points",
    )(*blocks, *([] if total is None else [total]), *after)


def finish_kernel(count, total, *refs):
    parts, (canvas, to_pair, to_cross) = refs[:count], refs[-3:]
    tile_rows = canvas.shape[0]
    places = [(part, at) for part in parts for at in range(part.shape[0])]
    for r in range(tile_rows):
        line = total[r]
        if parts:
            part, at = places[r]
            line = line + part[at]
        canvas[r] = line
    lower = first_of_pair()
    for k in range(HALO):
        top, bottom = canvas[k], canvas[tile_rows - HALO + k]
        to_pair[k] = jnp.where(lower, bottom, top)
        to_cross[k] = jnp.where(lower, top, bottom)


def finish(total, parts=(), after=()):
    _, channels, columns = total.shape
    rim = jax.ShapeDtypeStruct((HALO, channels, columns), F32)
    return pl.pallas_call(
        functools.partial(finish_kernel, len(parts)),
        out_shape=(jax.ShapeDtypeStruct(total.shape, F32), rim, rim),
        compiler_params=PARAMS,
        name="finish_canvas",
    )(total, *parts, *after)


def adjoint_rows(n_row, canvas, pair, cross):
    tile = [canvas[r] for r in range(canvas.shape[0])]
    rims = ([ref[k] for k in range(HALO)] for ref in (pair, cross))
    return extended_rows(tile, *rims, HALO, first_of_pair(), row_masks(n_row))


def cross_edges_kernel(canvas, cross, *refs):
    edges = refs[-1]
    lower = first_of_pair()
    tile_rows = canvas.shape[0]
    empty = jnp.zeros(edges.shape, F32)
    lines = [(k, jnp.where(lower, cross[k], empty)) for k in range(HALO)]
    lines += [(HALO + r, canvas[r]) for r in range(tile_rows)]
    lines += [(HALO + tile_rows + k, jnp.where(lower, empty, cross[k])) for k in range(HALO)]
    edges[...] = edge_columns(lines, empty)


def pair_edges_kernel(n_row, tile_rows, partial, pair, edges):
    lower, masks = first_of_pair(), row_masks(n_row)
    result = partial[...]
    empty = jnp.zeros(edges.shape, F32)
    lane = lax.broadcasted_iota(jnp.int32, edges.shape, 1)
    row = ((lane + 4) // 8) % 16
    result = jnp.where(row < HALO, masks[0], jnp.where(row < HALO + tile_rows, 1.0, masks[1])) * result
    lines = [(k, jnp.where(lower, empty, pair[k])) for k in range(HALO)]
    lines += [(HALO + tile_rows + k, jnp.where(lower, pair[k], empty)) for k in range(HALO)]
    edges[...] = result + edge_columns(lines, empty)


def adjoint_edges(n_row, canvas, pair, cross, after=()):
    tile_rows, channels, _ = canvas.shape
    edges = jax.ShapeDtypeStruct((channels, LANES), F32)
    partial = pl.pallas_call(
        cross_edges_kernel, out_shape=edges, compiler_params=PARAMS, name="cross_edges"
    )(canvas, cross, *after)
    return pl.pallas_call(
        functools.partial(pair_edges_kernel, n_row, tile_rows),
        out_shape=edges,
        compiler_params=PARAMS,
        name="pair_edges",
    )(partial, pair)


def run_stages(wide, gravity, levels, masks, tile_rows, buffers, store):
    start, middle, after, last = buffers

    def along_x(values):
        return pltpu.roll(values, LANES - 1, 1) - pltpu.roll(values, 1, 1)

    def run(stage, adjoint, put):
        width = HALO - 1 - stage
        begin, end = HALO - width, HALO + tile_rows + width
        for low in range(0, levels, PART):
            pull = (0.5 * stage_weight(stage)) * gravity[low : low + PART, :]

            def state(k, which):
                return wide[stage, k, which * levels + low : which * levels + low + PART, :]

            def line(k):
                a, b, c = (adjoint[k, w * levels + low : w * levels + low + PART, :] for w in range(3))
                v = state(k, 2)
                return a, b, c, v, v * b, v * c

            up, here = line(begin - 1), line(begin)
            for k in range(begin, end):
                down = line(k + 1)
                a, b, c, v = here[:4]
                h, u = state(k, 0), state(k, 1)
                a_x, a_y = along_x(a), down[0] - up[0]
                height = u * a_x + v * a_y + pull * (along_x(b) + (down[2] - up[2]))
                east = h * a_x + along_x(u * b) + (down[4] - up[4]) - b * state(k, 3) - c * state(k, 4)
                north = h * a_y + along_x(u * c) + (down[5] - up[5]) - b * state(k, 5) - c * state(k, 6)
                for w, (old, change) in enumerate(zip((a, b, c), (height, east, north))):
                    put(k, w, low, old, change)
                up, here = here, down

    def kept(k, value):
        if k < HALO:
            return value * masks[0]
        if k >= HALO + tile_rows:
            return value * masks[1]
        return value

    def half_into(result):
        def put(k, w, low, old, change):
            result[k, w * levels + low : w * levels + low + PART, :] = kept(k, 0.5 * old + change)

        return put

    def after_step(adjoint, k, w, low, old, change):
        return 0.5 * adjoint[k, w * levels + low : w * levels + low + PART, :] + old + change

    def to_after(k, w, low, old, change):
        after[k, w * levels + low : w * levels + low + PART, :] = kept(k, after_step(start, k, w, low, old, change))

    def to_end(k, w, low, old, change):
        store(k - HALO, w, low, after_step(after, k, w, low, old, change))

    run(0, start, half_into(middle))
    run(1, middle, to_after)
    run(2, after, half_into(last))
    run(3, last, to_end)


def tile_steps_kernel(n_row, canvas, pair, cross, wide, gravity, out, windows, *buffers):
    tile_rows, channels, _ = canvas.shape
    levels = channels // 3
    for k, line in adjoint_rows(n_row, canvas, pair, cross):
        buffers[0][k] = line
        windows[k] = edge_windows(line)

    def store(r, w, low, value):
        out[r, w * levels + low : w * levels + low + PART, :] = value

    run_stages(wide, gravity, levels, row_masks(n_row), tile_rows, buffers, store)


def tile_steps(n_row, canvas, pair, cross, wide, gravity):
    tile_rows, channels, columns = canvas.shape
    return pl.pallas_call(
        functools.partial(tile_steps_kernel, n_row),
        out_shape=(
            jax.ShapeDtypeStruct(canvas.shape, F32),
            jax.ShapeDtypeStruct((tile_rows + 2 * HALO, 3 * PART, columns), F32),
        ),
        scratch_shapes=[pltpu.VMEM((tile_rows + 2 * HALO, channels, columns), F32)] * 4,
        compiler_params=PARAMS,
        name="tile_steps",
    )(canvas, pair, cross, wide, gravity)


def edge_steps_kernel(n_row, paired, windows, one, other, wide, gravity, inner, out, *buffers):
    *buffers, result, merged, sems = buffers
    tile_rows, channels, _ = inner.shape
    levels = channels // 3
    left, right = from_sides(one[...], other[...], paired)
    rims = jnp.where(first_lanes(left), pltpu.roll(right, BEYOND_AT, 1), left)
    for k in range(tile_rows + 2 * HALO):
        rim = by_half(rims, lambda values, turn: turned_by(values, turn - 8 * k))
        buffers[0][k] = with_rim(windows[k], rim)
    lane = ring_lanes()

    def store(r, w, low, value):
        result[r, w * PART : (w + 1) * PART, :] = value

    run_stages(wide, gravity, PART, row_masks(n_row), tile_rows, buffers, store)
    copies = []
    for w in range(3):
        for begin in range(w * levels, (w + 1) * levels, PART):
            turn = begin % levels // PART * TURN
            for r in range(tile_rows):
                value = result[r, w * PART : (w + 1) * PART, :]
                final = turned_by(value, LANES - BEYOND_AT - turn)
                line = jnp.where(lane >= LANES - HALO, final, inner[r, begin : begin + PART, :])
                line = jnp.where(lane < HALO, turned_by(value, turn), line)
                merged[pl.ds(begin * tile_rows + r, PART, stride=tile_rows), :] = line
        field = pl.ds(w * levels * tile_rows, levels * tile_rows)
        copies.append(pltpu.make_async_copy(merged.at[field, :], out.at[field, :], sems.at[w]))
        copies[-1].start()
    for copy in copies:
        copy.wait()


def edge_steps(n_row, paired, windows, one, other, wide, gravity, inner):
    tile_rows, channels, columns = inner.shape
    return pl.pallas_call(
        functools.partial(edge_steps_kernel, n_row, paired),
        out_shape=jax.ShapeDtypeStruct((channels * tile_rows, columns), F32),
        out_specs=pl.BlockSpec(memory_space=pltpu.HBM),
        scratch_shapes=[pltpu.VMEM(windows.shape, F32)] * 4
        + [
            pltpu.VMEM((tile_rows, 3 * PART, columns), F32),
            pltpu.VMEM((channels * tile_rows, columns), F32),
            pltpu.SemaphoreType.DMA((3,)),
        ],
        compiler_params=PARAMS,
        name="edge_steps",
    )(windows, one, other, wide, gravity, inner)


def shifted(values, axis, by):
    count = lax.axis_size(axis)
    return lax.ppermute(values, axis, [(i, (i + by) % count) for i in range(count)])


def exchanged(values, offset):
    n_row, n_col = lax.axis_size("frow"), lax.axis_size("fcol")
    df, dz = offset
    pairs = [(f * n_col + z, (f ^ df) * n_col + (z ^ dz)) for f in range(n_row) for z in range(n_col)]
    return lax.ppermute(values, ("frow", "fcol"), pairs)


def exchanged_across(values):
    n_row = lax.axis_size("frow")
    return lax.ppermute(values, "frow", [(f, ((f + 1) ^ 1) - 1) for f in range(1, n_row - 1)])


def from_everyone(packed, channels, tile_count):
    groups = packed.shape[0]
    rows = channels + 4
    halves = [
        jnp.concatenate(
            [
                packed[:, h * channels : (h + 1) * channels],
                packed[:, 2 * channels + 4 * h : 2 * channels + 4 * h + 4],
            ],
            axis=1,
        )
        for h in range(2)
    ]
    slots = jnp.stack(halves, axis=2).transpose(1, 0, 2, 3).reshape(rows, tile_count, -1)
    slots = lax.all_to_all(slots, ("frow", "fcol"), split_axis=1, concat_axis=1, tiled=True)
    slots = slots.reshape(rows, groups, 2, LANES).transpose(1, 2, 0, 3)
    return jnp.concatenate(
        [slots[:, 0, :channels], slots[:, 1, :channels], slots[:, 0, channels:], slots[:, 1, channels:]], axis=1
    )


def per_device(latlon_cot, dest_tile, base_cell, corner_frac, saved_states, gravity):
    n_row, n_col = lax.axis_size("frow"), lax.axis_size("fcol")
    tile_count = n_row * n_col
    levels = gravity.shape[0]
    tile_rows = saved_states.shape[4]
    columns = saved_states.shape[5]
    channels = 3 * levels
    points = base_cell.shape[0]
    lines = points // LANES
    share = GROUP * tile_count // (2 * points)
    paired = share == 1 and n_row == 4 and n_col == 4
    size = (channels, tile_rows, columns)

    cot = latlon_cot.reshape(channels, points)
    partner_cot = exchanged(cot, (1, 0)) if paired else None
    sent, to_cross, turned, cot = prepare(
        dest_tile.reshape(lines, LANES),
        base_cell.reshape(lines, LANES),
        corner_frac,
        saved_states.reshape(4, channels * tile_rows, columns),
        cot,
        (3, 2, 1, 0),
        tile_rows,
    )
    pair_at = 4 * lines
    pair = exchanged(sent, (1, 0))
    cross = exchanged_across(to_cross)
    if paired:
        chip_points = cot, sent, partner_cot, pair
        packed = pack_chip(FAR, chip_points, tile_rows, columns)
        got = [packed[0]] + [exchanged(block, (df, dz ^ 2)) for block, (df, dz) in zip(packed[1:], FAR[1:])]
        packed = pack_chip(NEAR, chip_points, tile_rows, columns, [cross, packed[0]])
        total = scatter(got[:3], None, *size, packed[:1])[0]
        sums = scatter(got[3:], total, *size, parts=(5, tile_rows - 5))
        far = [exchanged(part, (0, 2)) for part in sums]
        got = [packed[0]] + [exchanged(block, tile) for block, tile in zip(packed[1:], NEAR[1:])]
        one, other = all_state_edges(n_row, pair_at, paired, turned, pair, cross, sums)
        one, other = exchanged(one, (0, 1)), exchanged(other, (0, 3))
        total = scatter(got[:3], None, *size)[0]
        total = scatter(got[3:], total, *size)[0]
        fields, pull, edge_pull, own = tile_fields(n_row, pair_at, turned, pair, cross, gravity, [total])
        canvas = finish(total, far, [one, other, pull])
    else:
        packed = pack_all(cot, sent, tile_count, share, tile_rows, columns)
        got = from_everyone(packed, channels, tile_count)
        one, other = all_state_edges(n_row, pair_at, paired, turned, pair, cross)
        one, other = shifted(one, "fcol", 1), shifted(other, "fcol", -1)
        fields, pull, edge_pull, own = tile_fields(n_row, pair_at, turned, pair, cross, gravity)
        canvas = finish(scatter([got.reshape(-1, LANES)], None, *size)[0])

    near_edges = edge_fields(n_row, paired, own, one, other)
    canvas, to_pair, to_cross = canvas
    pair, cross = exchanged(to_pair, (1, 0)), exchanged_across(to_cross)
    edges = adjoint_edges(n_row, canvas, pair, cross, [near_edges])
    if paired:
        sides = exchanged(edges, (0, 1)), exchanged(edges, (0, 3))
    else:
        sides = shifted(edges, "fcol", 1), shifted(edges, "fcol", -1)
    inner, windows = tile_steps(n_row, canvas, pair, cross, fields, pull)
    result = edge_steps(n_row, paired, windows, *sides, near_edges, edge_pull, inner)
    return result.reshape(3, levels, tile_rows, columns)


def solution(mesh):
    placed = (
        P(None, None, ("member", "frow", "fcol")),
        P(("frow", "fcol"), None),
        P(("frow", "fcol")),
        P(None, ("frow", "fcol")),
        P(None, None, None, None, ("member", "frow"), "fcol"),
        P(),
    )
    return jax.shard_map(
        per_device,
        mesh=mesh,
        in_specs=placed,
        out_specs=P(None, None, ("member", "frow"), "fcol"),
        check_vma=False,
    )
```

```python
import functools

import jax
import jax.numpy as jnp
from jax import lax
from jax.experimental import pallas as pl
from jax.experimental.pallas import tpu as pltpu
from jax.sharding import PartitionSpec as P

time_step = 0.25
coriolis_peak = 0.8

HALO = 4
GROUP = 256
LANES = 128
F32 = jnp.float32
BF16 = jnp.bfloat16
PARAMS = pltpu.CompilerParams(vmem_limit_bytes=16 * 1024 * 1024)


def split(values):
    high = values.astype(BF16)
    return high, (values - high.astype(F32)).astype(BF16)


def dot_nt(a, b):
    return lax.dot_general(a, b, (((1,), (1,)), ((), ())), preferred_element_type=F32)


def first_of_pair(axis="frow"):
    return lax.rem(lax.axis_index(axis), 2) == 0


def row_masks(n_row):
    at = lax.axis_index("frow")
    return jnp.where(at > 0, 1.0, 0.0).astype(F32), jnp.where(at < n_row - 1, 1.0, 0.0).astype(F32)


def extended_rows(tile, pair, cross, width, lower, masks):
    tile_rows = len(tile)
    lines = [(HALO - width + k, jnp.where(lower, cross[k], pair[k]) * masks[0]) for k in range(width)]
    lines += [(HALO + k, tile[k]) for k in range(tile_rows)]
    lines += [(HALO + tile_rows + k, jnp.where(lower, pair[k], cross[k]) * masks[1]) for k in range(width)]
    return lines


def edge_columns(lines, result):
    lane = lax.broadcasted_iota(jnp.int32, result.shape, 1)
    owner = ((lane + 4) // 8) % 16
    for k, line in lines:
        result = jnp.where(owner == k, pltpu.roll(line, (8 * k) % LANES, 1), result)
    return result


def first_lanes(like):
    return lax.broadcasted_iota(jnp.int32, like.shape, 1) % 8 < 4


def from_sides(one, other, paired):
    if not paired:
        return one, other
    lower = first_of_pair("fcol")
    return jnp.where(lower, other, one), jnp.where(lower, one, other)


def first_row(which):
    return sum(HALO - k for k in range(which))


def prepare_kernel(order, dest, base, frac, states, cot, sent, cross, turned, cot_out, dest_v, base_v, frac_v, states_v, sems):
    moves = ((dest, dest_v), (base, base_v), (frac, frac_v), (states, states_v), (cot, cot_out))
    copies = [pltpu.make_async_copy(source, target, sems.at[i]) for i, (source, target) in enumerate(moves)]
    for copy in copies:
        copy.start()
    for copy in copies[:3]:
        copy.wait()
    lines = dest_v.shape[0]
    sent[:lines, :] = dest_v[...].astype(F32)
    sent[lines : 2 * lines, :] = base_v[...].astype(F32)
    for k in range(2):
        for i in range(lines):
            sent[(2 + k) * lines + i : (2 + k) * lines + i + 1, :] = frac_v[k : k + 1, i * LANES : (i + 1) * LANES]
    copies[3].wait()
    _, tile_rows, channels, _ = turned.shape
    lower = first_of_pair()
    for which, source in enumerate(order):
        for r in range(tile_rows):
            turned[which, r] = states_v[source, pl.ds(r, channels, stride=tile_rows), :]
        width = HALO - which
        for k in range(width):
            top, bottom = turned[which, k], turned[which, tile_rows - width + k]
            at = (first_row(which) + k) * channels
            sent[4 * lines + at : 4 * lines + at + channels, :] = jnp.where(lower, bottom, top)
            cross[at : at + channels, :] = jnp.where(lower, top, bottom)
    copies[4].wait()


def prepare(dest, base, frac, states, cot, order, tile_rows):
    channels, points = cot.shape
    columns = states.shape[2]
    stages = len(order)
    rim = first_row(stages) * channels
    lines = points // LANES
    in_hbm = pl.BlockSpec(memory_space=pltpu.HBM)
    return pl.pallas_call(
        functools.partial(prepare_kernel, order),
        in_specs=[in_hbm] * 5,
        out_shape=(
            jax.ShapeDtypeStruct((4 * lines + rim, LANES), F32),
            jax.ShapeDtypeStruct((rim, columns), F32),
            jax.ShapeDtypeStruct((stages, tile_rows, channels, columns), F32),
            jax.ShapeDtypeStruct(cot.shape, F32),
        ),
        scratch_shapes=[
            pltpu.VMEM(dest.shape, jnp.int32),
            pltpu.VMEM(base.shape, jnp.int32),
            pltpu.VMEM(frac.shape, F32),
            pltpu.VMEM(states.shape, F32),
            pltpu.SemaphoreType.DMA((5,)),
        ],
        compiler_params=PARAMS,
        name="prepare",
    )(*(pltpu.with_memory_space_constraint(x, pltpu.HBM) for x in (dest, base, frac, states, cot)))


def state_rows(which, turned, pair, pair_at, cross, lower, masks):
    _, tile_rows, channels, _ = turned.shape
    width = HALO - which

    def rim(ref, start):
        at = [start + (first_row(which) + k) * channels for k in range(width)]
        return [ref[i : i + channels, :] for i in at]

    tile = [turned[which, r] for r in range(tile_rows)]
    return extended_rows(tile, rim(pair, pair_at), rim(cross, 0), width, lower, masks)


def edge_plan(stages, tile_rows):
    plan, lane = [], 0
    for which in range(stages):
        width = HALO - which
        for k in range(HALO - width, HALO + tile_rows + width):
            count = width - max(HALO - k, k - (HALO + tile_rows - 1), 0)
            if count > 0:
                plan.append((which, k, count, lane))
                lane += count
    return plan


def state_edges(n_row, turned, pair, pair_at, cross):
    stages, tile_rows, channels, _ = turned.shape
    lower, masks = first_of_pair(), row_masks(n_row)
    lane = lax.broadcasted_iota(jnp.int32, (channels, LANES), 1)
    first = last = jnp.zeros((channels, LANES), F32)
    lines = [dict(state_rows(which, turned, pair, pair_at, cross, lower, masks)) for which in range(stages)]
    for which, k, count, at in edge_plan(stages, tile_rows):
        here = (lane >= at) & (lane < at + count)
        first = jnp.where(here, pltpu.roll(lines[which][k], at, 1), first)
        last = jnp.where(here, pltpu.roll(lines[which][k], (at + count) % LANES, 1), last)
    return first, last


def state_edges_kernel(n_row, pair_at, paired, turned, pair, cross, *refs):
    one, other = refs[-2:]
    first, last = state_edges(n_row, turned, pair, pair_at, cross)
    one[...], other[...] = last, first
    if paired:
        lower = first_of_pair("fcol")
        one[...], other[...] = jnp.where(lower, last, first), jnp.where(lower, first, last)


def all_state_edges(n_row, pair_at, paired, turned, pair, cross, after=()):
    return pl.pallas_call(
        functools.partial(state_edges_kernel, n_row, pair_at, paired),
        out_shape=[jax.ShapeDtypeStruct((turned.shape[2], LANES), F32)] * 2,
        compiler_params=PARAMS,
        name="state_edges",
    )(turned, pair, cross, *after)


FIELDS = 7


def stage_weight(which):
    return 0.5 * time_step if which % 2 == 0 else time_step


def store_fields(wide, which, lines, levels, base_row, total_rows, own=None):
    weight = stage_weight(which)
    channels = 3 * levels
    for k, line in lines:
        wide[which, k, :channels, :] = (0.5 * weight) * line
        if own is not None:
            own[which, k] = edge_windows(line)
    winds = slice(levels, channels)
    for k in range(lines[0][0] + 1, lines[-1][0]):
        values = wide[which, k, winds, :]
        change = pltpu.roll(values, LANES - 1, 1) - pltpu.roll(values, 1, 1)
        slope = wide[which, k + 1, winds, :] - wide[which, k - 1, winds, :]
        rotation = weight * (coriolis_peak * (2.0 * ((base_row + k - HALO).astype(F32) + 0.5) / total_rows - 1.0))
        begin = channels
        for value in (change[:levels], change[levels:] + rotation, slope[:levels] - rotation, slope[levels:]):
            wide[which, k, begin : begin + levels, :] = value
            begin += levels


PART = 8
BEYOND_AT = 32
TURN = LANES // 2


def ring_lanes():
    return lax.broadcasted_iota(jnp.int32, (PART, LANES), 1)


def by_half(values, ring):
    lane = ring_lanes()
    second = (lane >= TURN - LANES // 8) & (lane < LANES - LANES // 8)
    fields = []
    for begin in range(0, values.shape[0], 2 * PART):
        first, last = values[begin : begin + PART], values[begin + PART : begin + 2 * PART]
        fields.append(jnp.where(second, ring(last, TURN), ring(first, 0)))
    return jnp.concatenate(fields, axis=0)


def turned_by(values, shift):
    shift %= LANES
    return pltpu.roll(values, shift, 1) if shift else values


def edge_windows(line):
    lane = ring_lanes()

    def ring(values, turn):
        ends = (lane >= turn + BEYOND_AT // 2) & (lane < turn + BEYOND_AT)
        return jnp.where(ends, turned_by(values, BEYOND_AT + turn), turned_by(values, turn))

    return by_half(line, ring)


def with_rim(window, rim):
    lane = lax.broadcasted_iota(jnp.int32, window.shape, 1) % TURN
    beyond = (lane >= TURN - HALO) | ((lane >= BEYOND_AT) & (lane < BEYOND_AT + HALO))
    return jnp.where(beyond, rim, window)


def tile_fields_kernel(n_row, pair_at, turned, pair, cross, gravity, *refs):
    wide, pull, edge_pull, own = refs[-4:]
    stages, tile_rows, channels, _ = turned.shape
    levels = channels // 3
    level = lax.broadcasted_iota(jnp.int32, pull.shape, 0)
    pulls = jnp.zeros(pull.shape, F32)
    for i in range(levels):
        pulls = jnp.where(level == i, gravity[i], pulls)
    pull[...] = pulls
    edge_pull[...] = by_half(pulls, lambda values, _: values)
    lower, masks = first_of_pair(), row_masks(n_row)
    for which in range(stages):
        lines = state_rows(which, turned, pair, pair_at, cross, lower, masks)
        store_fields(wide, which, lines, levels, lax.axis_index("frow") * tile_rows, tile_rows * n_row, own)


def tile_fields(n_row, pair_at, turned, pair, cross, gravity, after=()):
    stages, tile_rows, channels, columns = turned.shape
    in_vmem = pl.BlockSpec(memory_space=pltpu.VMEM)
    return pl.pallas_call(
        functools.partial(tile_fields_kernel, n_row, pair_at),
        in_specs=[in_vmem] * 3 + [pl.BlockSpec(memory_space=pltpu.SMEM)] + [in_vmem] * len(after),
        out_shape=(
            jax.ShapeDtypeStruct((stages, tile_rows + 2 * HALO, channels // 3 * FIELDS, columns), F32),
            jax.ShapeDtypeStruct((channels // 3, columns), F32),
            jax.ShapeDtypeStruct((PART, columns), F32),
            jax.ShapeDtypeStruct((stages, tile_rows + 2 * HALO, 3 * PART, columns), F32),
        ),
        compiler_params=PARAMS,
        name="tile_fields",
    )(turned, pair, cross, gravity, *after)


def edge_fields_kernel(n_row, paired, own, one, other, wide):
    stages, extended, _, columns = own.shape
    tile_rows = extended - 2 * HALO
    left, right = from_sides(one[...], other[...], paired)
    lane = ring_lanes()
    sides = jnp.concatenate([left, right], axis=1)

    def rim_of(count, at):
        def ring(values, turn):
            beyond = (lane >= BEYOND_AT + turn) & (lane < BEYOND_AT + HALO + turn)
            from_left, from_right = values[:, :columns], values[:, columns:]
            return jnp.where(
                beyond, turned_by(from_right, BEYOND_AT + turn - at), turned_by(from_left, turn - at - count)
            )

        return by_half(sides, ring)

    rims = {(which, k): rim_of(count, at) for which, k, count, at in edge_plan(stages, tile_rows)}
    for which in range(stages):
        width = HALO - which
        lines = []
        for k in range(HALO - width, HALO + tile_rows + width):
            line = own[which, k]
            if (which, k) in rims:
                line = with_rim(line, rims[which, k])
            lines.append((k, line))
        store_fields(wide, which, lines, PART, lax.axis_index("frow") * tile_rows, tile_rows * n_row)


def edge_fields(n_row, paired, own, one, other):
    stages, extended, _, columns = own.shape
    return pl.pallas_call(
        functools.partial(edge_fields_kernel, n_row, paired),
        out_shape=jax.ShapeDtypeStruct((stages, extended, PART * FIELDS, columns), F32),
        compiler_params=PARAMS,
        name="edge_fields",
    )(own, one, other)


def slot_blocks(cot, where, tiles, share, groups, tile_rows, columns, onehot, parts):
    channels, points = cot.shape
    lines = points // LANES
    named_tiles = tiles.shape[0]
    corner = where[lines : 2 * lines, :]
    row = jnp.zeros_like(corner)
    for k in range(1, tile_rows - 1):
        row = row + (corner >= float(k * (columns - 1))).astype(F32)
    col = corner - row * float(columns - 1)
    target = where[:lines, :]
    offsets = [where[k * lines : (k + 1) * lines, :] for k in (2, 3)]

    before = (
        lax.broadcasted_iota(jnp.int32, (GROUP, GROUP), 0)
        < lax.broadcasted_iota(jnp.int32, (GROUP, GROUP), 1)
    ).astype(F32).astype(BF16)
    index = lax.broadcasted_iota(jnp.int32, tiles.shape, 0)
    begin = ((index % share) * (GROUP // share)).astype(F32)
    slots = lax.broadcasted_iota(jnp.int32, (GROUP, GROUP), 0).astype(F32).astype(BF16)
    one, zero = jnp.ones(slots.shape, BF16), jnp.zeros(slots.shape, BF16)
    count = jnp.zeros((named_tiles, 1), F32)
    rows = channels + 8

    def across(values, b):
        return jnp.concatenate([values[2 * b : 2 * b + 1, :], values[2 * b + 1 : 2 * b + 2, :]], axis=1)

    all_named = [(tiles == across(target, b)).astype(F32) for b in range(points // GROUP)]
    all_ahead = jnp.dot(jnp.concatenate(all_named, axis=0).astype(BF16), before, preferred_element_type=F32)
    for b, named in enumerate(all_named):
        part = slice(b * GROUP, (b + 1) * GROUP)
        ahead = all_ahead[b * named_tiles : (b + 1) * named_tiles, :]
        lane = jnp.sum(named * (ahead + count + begin), axis=0, keepdims=True)
        count = count + jnp.sum(named, axis=1, keepdims=True)
        onehot[:, part] = jnp.where(slots == lane.astype(BF16), one, zero)
        coords = [across(values, b) for values in (row, col, *offsets)]
        data_high, data_low = split(jnp.concatenate([cot[:, part], *coords, *coords], axis=0))
        for g in range(groups):
            mine = named[g * share : g * share + 1, :]
            for i in range(1, share):
                mine = mine + named[g * share + i : g * share + i + 1, :]
            mine = mine.astype(BF16)
            parts[g * rows : (g + 1) * rows, part] = data_high * mine
            parts[(groups + g) * rows : (groups + g + 1) * rows, part] = data_low * mine
    both = dot_nt(parts[...], onehot[...])
    packed = both[: groups * rows, :] + both[groups * rows :, :]
    upper = lax.broadcasted_iota(jnp.int32, (8, LANES), 0) < 4
    for g in range(groups):
        block = packed[g * rows : (g + 1) * rows, :]
        yield (
            block[:channels, :LANES],
            block[:channels, LANES:],
            jnp.where(upper, block[channels:, :LANES], block[channels:, LANES:]),
        )


def store_block(out, at, pieces):
    channels = pieces[0].shape[0]
    out[at : at + channels, :] = pieces[0]
    out[at + channels : at + 2 * channels, :] = pieces[1]
    out[at + 2 * channels : at + 2 * channels + 8, :] = pieces[2]


def pack_scratch(channels, points, groups):
    return [
        pltpu.VMEM((GROUP, points), BF16),
        pltpu.VMEM((2 * groups * (channels + 8), points), BF16),
    ]


def pack_all_kernel(tile_count, share, tile_rows, columns, cot, where, out, *scratch):
    tiles = lax.broadcasted_iota(jnp.int32, (tile_count, GROUP), 0).astype(F32)
    for g, pieces in enumerate(slot_blocks(cot, where, tiles, share, tile_count // share, tile_rows, columns, *scratch)):
        store_block(out.at[g], 0, pieces)


def pack_all(cot, where, tile_count, share, tile_rows, columns):
    channels, points = cot.shape
    groups = tile_count // share
    return pl.pallas_call(
        functools.partial(pack_all_kernel, tile_count, share, tile_rows, columns),
        out_shape=jax.ShapeDtypeStruct((groups, 2 * channels + 8, LANES), F32),
        scratch_shapes=pack_scratch(channels, points, groups),
        compiler_params=PARAMS,
        name="pack_points",
    )(cot, where)


NEAR = ((0, 0), (2, 1), (2, 0), (0, 1))
FAR = ((0, 2), (2, 2), (0, 3), (2, 3))


def partner_tiles(partners):
    at_row, at_col = lax.axis_index("frow"), lax.axis_index("fcol")
    n_col = lax.axis_size("fcol")
    index = lax.broadcasted_iota(jnp.int32, (8, GROUP), 0)
    tiles = jnp.full(index.shape, -1, jnp.int32)
    for g, (df, dz) in enumerate(partners):
        tiles = jnp.where(index == g, (at_row ^ df) * n_col + (at_col ^ dz), tiles)
    return tiles.astype(F32)


def pack_chip_kernel(tiles, tile_rows, columns, cot, where, pair_cot, pair_where, *refs):
    outs, scratch = refs[-4 - len(tiles) : -4], refs[-4:]
    begin = 0
    for i, points in enumerate(((cot, where), (pair_cot, pair_where))):
        blocks = slot_blocks(
            *points, partner_tiles(tiles), 1, len(tiles), tile_rows, columns, *scratch[2 * i : 2 * i + 2]
        )
        for out, pieces in zip(outs, blocks):
            store_block(out, begin, pieces)
        begin += 2 * cot.shape[0] + 8


def pack_chip(tiles, points, tile_rows, columns, after=()):
    channels, count = points[0].shape
    return pl.pallas_call(
        functools.partial(pack_chip_kernel, tiles, tile_rows, columns),
        out_shape=[jax.ShapeDtypeStruct((2 * (2 * channels + 8), LANES), F32)] * len(tiles),
        scratch_shapes=pack_scratch(channels, count, len(tiles)) * 2,
        compiler_params=PARAMS,
        name="pack_chip",
    )(*points, *after)


def scatter_kernel(count, first, later, *refs):
    blocks, refs = refs[:count], refs[count:]
    if not first:
        total, refs = refs[0], refs[1:]
    outs, scratch = refs[later : -2 * count], refs[-2 * count :]
    _, channels, columns = outs[0].shape
    places = [(out, r) for out in outs for r in range(out.shape[0])]
    tile_rows = len(places)
    rows = 2 * channels + 8
    cells = lax.broadcasted_iota(jnp.int32, (columns, LANES), 0).astype(F32).astype(BF16)
    zero = jnp.zeros((channels, LANES), BF16)

    def spread(values, shape):
        return jnp.broadcast_to(values.astype(BF16), shape)

    sums = None
    for block, parts, weight in zip(blocks, scratch[::2], scratch[1::2]):
        at = 0
        for source in range(block.shape[0] // rows):
            for half in range(2):
                part = slice(at, at + LANES)
                at += LANES
                begin = source * rows + 2 * channels + 4 * half
                coords = block[begin : begin + 4, :]
                row, col, along_rows, along_cols = (coords[k : k + 1, :] for k in range(4))
                corner, beside = cells == spread(col, cells.shape), cells == spread(col + 1.0, cells.shape)
                for k, (near, far) in enumerate(zip(split(1.0 - along_cols), split(along_cols))):
                    chosen = jnp.where(
                        beside, spread(far, cells.shape), jnp.zeros(cells.shape, BF16)
                    )
                    weight[k * columns : (k + 1) * columns, part] = jnp.where(corner, spread(near, cells.shape), chosen)
                begin = source * rows + half * channels
                values = block[begin : begin + channels, :]
                upper, lower = split(values * (1.0 - along_rows)), split(values * along_rows)
                below = None
                line = spread(row, zero.shape)
                for r in range(tile_rows):
                    here = line == jnp.full(zero.shape, r, BF16)
                    for k in range(2):
                        product = zero if below is None else jnp.where(below, lower[k], zero)
                        product = jnp.where(here, upper[k], product)
                        begin = (k * tile_rows + r) * channels
                        parts[begin : begin + channels, part] = product
                    below = here
        both = dot_nt(parts[...], weight[...])
        both = both[:, :columns] + both[:, columns:]
        both = both[: tile_rows * channels, :] + both[tile_rows * channels :, :]
        sums = both if sums is None else sums + both
    for r in range(tile_rows):
        line = sums[r * channels : (r + 1) * channels, :]
        if not first:
            line = line + total[r]
        out, at = places[r]
        out[at] = line


def scatter(blocks, total, channels, tile_rows, columns, after=(), parts=None):
    slots = [block.shape[0] // (2 * channels + 8) * GROUP for block in blocks]
    return pl.pallas_call(
        functools.partial(scatter_kernel, len(blocks), total is None, len(after)),
        out_shape=[jax.ShapeDtypeStruct((count, channels, columns), F32) for count in parts or (tile_rows,)],
        scratch_shapes=[
            pltpu.VMEM((2 * lines, count), BF16) for count in slots for lines in (tile_rows * channels, columns)
        ],
        compiler_params=PARAMS,
        name="scatter_points",
    )(*blocks, *([] if total is None else [total]), *after)


def finish_kernel(count, total, *refs):
    parts, (canvas, to_pair, to_cross) = refs[:count], refs[-3:]
    tile_rows = canvas.shape[0]
    places = [(part, at) for part in parts for at in range(part.shape[0])]
    for r in range(tile_rows):
        line = total[r]
        if parts:
            part, at = places[r]
            line = line + part[at]
        canvas[r] = line
    lower = first_of_pair()
    for k in range(HALO):
        top, bottom = canvas[k], canvas[tile_rows - HALO + k]
        to_pair[k] = jnp.where(lower, bottom, top)
        to_cross[k] = jnp.where(lower, top, bottom)


def finish(total, parts=(), after=()):
    _, channels, columns = total.shape
    rim = jax.ShapeDtypeStruct((HALO, channels, columns), F32)
    return pl.pallas_call(
        functools.partial(finish_kernel, len(parts)),
        out_shape=(jax.ShapeDtypeStruct(total.shape, F32), rim, rim),
        compiler_params=PARAMS,
        name="finish_canvas",
    )(total, *parts, *after)


def adjoint_rows(n_row, canvas, pair, cross):
    tile = [canvas[r] for r in range(canvas.shape[0])]
    rims = ([ref[k] for k in range(HALO)] for ref in (pair, cross))
    return extended_rows(tile, *rims, HALO, first_of_pair(), row_masks(n_row))


def cross_edges_kernel(canvas, cross, *refs):
    edges = refs[-1]
    lower = first_of_pair()
    tile_rows = canvas.shape[0]
    empty = jnp.zeros(edges.shape, F32)
    lines = [(k, jnp.where(lower, cross[k], empty)) for k in range(HALO)]
    lines += [(HALO + r, canvas[r]) for r in range(tile_rows)]
    lines += [(HALO + tile_rows + k, jnp.where(lower, empty, cross[k])) for k in range(HALO)]
    edges[...] = edge_columns(lines, empty)


def pair_edges_kernel(n_row, tile_rows, partial, pair, edges):
    lower, masks = first_of_pair(), row_masks(n_row)
    result = partial[...]
    empty = jnp.zeros(edges.shape, F32)
    lane = lax.broadcasted_iota(jnp.int32, edges.shape, 1)
    row = ((lane + 4) // 8) % 16
    result = jnp.where(row < HALO, masks[0], jnp.where(row < HALO + tile_rows, 1.0, masks[1])) * result
    lines = [(k, jnp.where(lower, empty, pair[k])) for k in range(HALO)]
    lines += [(HALO + tile_rows + k, jnp.where(lower, pair[k], empty)) for k in range(HALO)]
    edges[...] = result + edge_columns(lines, empty)


def adjoint_edges(n_row, canvas, pair, cross, after=()):
    tile_rows, channels, _ = canvas.shape
    edges = jax.ShapeDtypeStruct((channels, LANES), F32)
    partial = pl.pallas_call(
        cross_edges_kernel, out_shape=edges, compiler_params=PARAMS, name="cross_edges"
    )(canvas, cross, *after)
    return pl.pallas_call(
        functools.partial(pair_edges_kernel, n_row, tile_rows),
        out_shape=edges,
        compiler_params=PARAMS,
        name="pair_edges",
    )(partial, pair)


def run_stages(wide, gravity, levels, masks, tile_rows, buffers, store):
    start, middle, after, last = buffers

    def along_x(values):
        return pltpu.roll(values, LANES - 1, 1) - pltpu.roll(values, 1, 1)

    def run(stage, adjoint, put):
        width = HALO - 1 - stage
        begin, end = HALO - width, HALO + tile_rows + width
        for low in range(0, levels, PART):
            pull = (0.5 * stage_weight(stage)) * gravity[low : low + PART, :]

            def state(k, which):
                return wide[stage, k, which * levels + low : which * levels + low + PART, :]

            def line(k):
                a, b, c = (adjoint[k, w * levels + low : w * levels + low + PART, :] for w in range(3))
                v = state(k, 2)
                return a, b, c, v, v * b, v * c

            up, here = line(begin - 1), line(begin)
            for k in range(begin, end):
                down = line(k + 1)
                a, b, c, v = here[:4]
                h, u = state(k, 0), state(k, 1)
                a_x, a_y = along_x(a), down[0] - up[0]
                height = u * a_x + v * a_y + pull * (along_x(b) + (down[2] - up[2]))
                east = h * a_x + along_x(u * b) + (down[4] - up[4]) - b * state(k, 3) - c * state(k, 4)
                north = h * a_y + along_x(u * c) + (down[5] - up[5]) - b * state(k, 5) - c * state(k, 6)
                for w, (old, change) in enumerate(zip((a, b, c), (height, east, north))):
                    put(k, w, low, old, change)
                up, here = here, down

    def kept(k, value):
        if k < HALO:
            return value * masks[0]
        if k >= HALO + tile_rows:
            return value * masks[1]
        return value

    def half_into(result):
        def put(k, w, low, old, change):
            result[k, w * levels + low : w * levels + low + PART, :] = kept(k, 0.5 * old + change)

        return put

    def after_step(adjoint, k, w, low, old, change):
        return 0.5 * adjoint[k, w * levels + low : w * levels + low + PART, :] + old + change

    def to_after(k, w, low, old, change):
        after[k, w * levels + low : w * levels + low + PART, :] = kept(k, after_step(start, k, w, low, old, change))

    def to_end(k, w, low, old, change):
        store(k - HALO, w, low, after_step(after, k, w, low, old, change))

    run(0, start, half_into(middle))
    run(1, middle, to_after)
    run(2, after, half_into(last))
    run(3, last, to_end)


def tile_steps_kernel(n_row, canvas, pair, cross, wide, gravity, out, windows, *buffers):
    tile_rows, channels, _ = canvas.shape
    levels = channels // 3
    for k, line in adjoint_rows(n_row, canvas, pair, cross):
        buffers[0][k] = line
        windows[k] = edge_windows(line)

    def store(r, w, low, value):
        out[r, w * levels + low : w * levels + low + PART, :] = value

    run_stages(wide, gravity, levels, row_masks(n_row), tile_rows, buffers, store)


def tile_steps(n_row, canvas, pair, cross, wide, gravity):
    tile_rows, channels, columns = canvas.shape
    return pl.pallas_call(
        functools.partial(tile_steps_kernel, n_row),
        out_shape=(
            jax.ShapeDtypeStruct(canvas.shape, F32),
            jax.ShapeDtypeStruct((tile_rows + 2 * HALO, 3 * PART, columns), F32),
        ),
        scratch_shapes=[pltpu.VMEM((tile_rows + 2 * HALO, channels, columns), F32)] * 4,
        compiler_params=PARAMS,
        name="tile_steps",
    )(canvas, pair, cross, wide, gravity)


def edge_steps_kernel(n_row, paired, windows, one, other, wide, gravity, inner, out, *buffers):
    *buffers, result = buffers
    tile_rows, channels, _ = inner.shape
    levels = channels // 3
    left, right = from_sides(one[...], other[...], paired)
    rims = jnp.where(first_lanes(left), pltpu.roll(right, BEYOND_AT, 1), left)
    for k in range(tile_rows + 2 * HALO):
        rim = by_half(rims, lambda values, turn: turned_by(values, turn - 8 * k))
        buffers[0][k] = with_rim(windows[k], rim)
    lane = ring_lanes()

    def store(r, w, low, value):
        result[r, w * PART : (w + 1) * PART, :] = value

    run_stages(wide, gravity, PART, row_masks(n_row), tile_rows, buffers, store)
    for r in range(tile_rows):
        for begin in range(0, channels, PART):
            field, turn = begin // levels, begin % levels // PART * TURN
            value = result[r, field * PART : (field + 1) * PART, :]
            first = pltpu.roll(value, turn, 1) if turn else value
            final = pltpu.roll(value, LANES - BEYOND_AT - turn, 1)
            line = jnp.where(lane >= LANES - HALO, final, inner[r, begin : begin + PART, :])
            out[pl.ds(begin * tile_rows + r, PART, stride=tile_rows), :] = jnp.where(lane < HALO, first, line)


def edge_steps(n_row, paired, windows, one, other, wide, gravity, inner):
    tile_rows, channels, columns = inner.shape
    return pl.pallas_call(
        functools.partial(edge_steps_kernel, n_row, paired),
        out_shape=jax.ShapeDtypeStruct((channels * tile_rows, columns), F32),
        scratch_shapes=[pltpu.VMEM(windows.shape, F32)] * 4 + [pltpu.VMEM((tile_rows, 3 * PART, columns), F32)],
        compiler_params=PARAMS,
        name="edge_steps",
    )(windows, one, other, wide, gravity, inner)


def shifted(values, axis, by):
    count = lax.axis_size(axis)
    return lax.ppermute(values, axis, [(i, (i + by) % count) for i in range(count)])


def exchanged(values, offset):
    n_row, n_col = lax.axis_size("frow"), lax.axis_size("fcol")
    df, dz = offset
    pairs = [(f * n_col + z, (f ^ df) * n_col + (z ^ dz)) for f in range(n_row) for z in range(n_col)]
    return lax.ppermute(values, ("frow", "fcol"), pairs)


def exchanged_across(values):
    n_row = lax.axis_size("frow")
    return lax.ppermute(values, "frow", [(f, ((f + 1) ^ 1) - 1) for f in range(1, n_row - 1)])


def from_everyone(packed, channels, tile_count):
    groups = packed.shape[0]
    rows = channels + 4
    halves = [
        jnp.concatenate(
            [
                packed[:, h * channels : (h + 1) * channels],
                packed[:, 2 * channels + 4 * h : 2 * channels + 4 * h + 4],
            ],
            axis=1,
        )
        for h in range(2)
    ]
    slots = jnp.stack(halves, axis=2).transpose(1, 0, 2, 3).reshape(rows, tile_count, -1)
    slots = lax.all_to_all(slots, ("frow", "fcol"), split_axis=1, concat_axis=1, tiled=True)
    slots = slots.reshape(rows, groups, 2, LANES).transpose(1, 2, 0, 3)
    return jnp.concatenate(
        [slots[:, 0, :channels], slots[:, 1, :channels], slots[:, 0, channels:], slots[:, 1, channels:]], axis=1
    )


def per_device(latlon_cot, dest_tile, base_cell, corner_frac, saved_states, gravity):
    n_row, n_col = lax.axis_size("frow"), lax.axis_size("fcol")
    tile_count = n_row * n_col
    levels = gravity.shape[0]
    tile_rows = saved_states.shape[4]
    columns = saved_states.shape[5]
    channels = 3 * levels
    points = base_cell.shape[0]
    lines = points // LANES
    share = GROUP * tile_count // (2 * points)
    paired = share == 1 and n_row == 4 and n_col == 4
    size = (channels, tile_rows, columns)

    cot = latlon_cot.reshape(channels, points)
    partner_cot = exchanged(cot, (1, 0)) if paired else None
    sent, to_cross, turned, cot = prepare(
        dest_tile.reshape(lines, LANES),
        base_cell.reshape(lines, LANES),
        corner_frac,
        saved_states.reshape(4, channels * tile_rows, columns),
        cot,
        (3, 2, 1, 0),
        tile_rows,
    )
    pair_at = 4 * lines
    pair = exchanged(sent, (1, 0))
    cross = exchanged_across(to_cross)
    if paired:
        chip_points = cot, sent, partner_cot, pair
        packed = pack_chip(FAR, chip_points, tile_rows, columns)
        got = [packed[0]] + [exchanged(block, (df, dz ^ 2)) for block, (df, dz) in zip(packed[1:], FAR[1:])]
        packed = pack_chip(NEAR, chip_points, tile_rows, columns, [cross, packed[0]])
        total = scatter(got[:3], None, *size, packed[:1])[0]
        sums = scatter(got[3:], total, *size, parts=(5, tile_rows - 5))
        far = [exchanged(part, (0, 2)) for part in sums]
        got = [packed[0]] + [exchanged(block, tile) for block, tile in zip(packed[1:], NEAR[1:])]
        one, other = all_state_edges(n_row, pair_at, paired, turned, pair, cross, sums)
        one, other = exchanged(one, (0, 1)), exchanged(other, (0, 3))
        total = scatter(got[:3], None, *size)[0]
        total = scatter(got[3:], total, *size)[0]
        fields, pull, edge_pull, own = tile_fields(n_row, pair_at, turned, pair, cross, gravity, [total])
        canvas = finish(total, far, [one, other, pull])
    else:
        packed = pack_all(cot, sent, tile_count, share, tile_rows, columns)
        got = from_everyone(packed, channels, tile_count)
        one, other = all_state_edges(n_row, pair_at, paired, turned, pair, cross)
        one, other = shifted(one, "fcol", 1), shifted(other, "fcol", -1)
        fields, pull, edge_pull, own = tile_fields(n_row, pair_at, turned, pair, cross, gravity)
        canvas = finish(scatter([got.reshape(-1, LANES)], None, *size)[0])

    near_edges = edge_fields(n_row, paired, own, one, other)
    canvas, to_pair, to_cross = canvas
    pair, cross = exchanged(to_pair, (1, 0)), exchanged_across(to_cross)
    edges = adjoint_edges(n_row, canvas, pair, cross, [near_edges])
    if paired:
        sides = exchanged(edges, (0, 1)), exchanged(edges, (0, 3))
    else:
        sides = shifted(edges, "fcol", 1), shifted(edges, "fcol", -1)
    inner, windows = tile_steps(n_row, canvas, pair, cross, fields, pull)
    result = edge_steps(n_row, paired, windows, *sides, near_edges, edge_pull, inner)
    return result.reshape(3, levels, tile_rows, columns)


def solution(mesh):
    placed = (
        P(None, None, ("member", "frow", "fcol")),
        P(("frow", "fcol"), None),
        P(("frow", "fcol")),
        P(None, ("frow", "fcol")),
        P(None, None, None, None, ("member", "frow"), "fcol"),
        P(),
    )
    return jax.shard_map(
        per_device,
        mesh=mesh,
        in_specs=placed,
        out_specs=P(None, None, ("member", "frow"), "fcol"),
        check_vma=False,
    )
```
